32 devices in a mesh: dp: 16 (over z, x, core), mp: 2 (over y).
Axes of the slice: x: 2, y: 2, z: 4, core: 2. Of those that a mesh axis runs over, the one named last changes fastest.
Arguments:
- tokens: bfloat16 [16384, 768], P(('dp', 'mp')), may hold values from -6 to 6
- cotangent: bfloat16 [16384, 768], P(('dp', 'mp')), may hold values from -6 to 6
- seq_counts: int32 [32, 4], P(('dp', 'mp')), may hold values from 0 to 4, as said below
- pattern: int32 [512, 512], replicated, may hold values from 0 to 1, as said below
- project_in: float32 [768, 2304], P('dp'), may hold values from -0.21875 to 0.21875
- project_in_first: float32 [768, 2304], P('dp'), may hold values from -80 to 80
- project_in_second: float32 [768, 2304], P('dp'), may hold values from 16.384 to 65.536
- project_out: float32 [768, 768], P('dp'), may hold values from -1.75 to 1.75
- project_out_first: float32 [768, 768], P('dp'), may hold values from -8 to 8
- project_out_second: float32 [768, 768], P('dp'), may hold values from 0.16384 to 0.65536
- feed_forward: float32 [2, 768, 3072], P(None, 'dp', 'mp'), may hold values from -0.21875 to 0.21875
- feed_forward_first: float32 [2, 768, 3072], P(None, 'dp', 'mp'), may hold values from -32 to 32
- feed_forward_second: float32 [2, 768, 3072], P(None, 'dp', 'mp'), may hold values from 2.4576 to 9.8304
- gate_logits: float32 [12, 1023], replicated, may hold values from -3 to 3
- gate_logits_first: float32 [12, 1023], replicated, may hold values from -10 to 10
- gate_logits_second: float32 [12, 1023], replicated, may hold values from 0.256 to 1.024
- norm_vectors: float32 [5, 768], replicated
- norm_vectors_first: float32 [5, 768], replicated, may hold values from -80 to 80
- norm_vectors_second: float32 [5, 768], replicated, may hold values from 16.384 to 65.536
- hidden_bias: float32 [3072], replicated, may hold values from -1.75 to 1.75
- hidden_bias_first: float32 [3072], replicated, may hold values from -24 to 24
- hidden_bias_second: float32 [3072], replicated, may hold values from 1.6384 to 6.5536
Outputs:
- layer_out: bfloat16 [16384, 768], P(('dp', 'mp'))
- input_grad: float32 [16384, 768], P(('dp', 'mp'))
- new_project_in: float32 [768, 2304], P('dp')
- first_project_in: float32 [768, 2304], P('dp')
- second_project_in: float32 [768, 2304], P('dp')
- new_project_out: float32 [768, 768], P('dp')
- first_project_out: float32 [768, 768], P('dp')
- second_project_out: float32 [768, 768], P('dp')
- new_feed_forward: float32 [2, 768, 3072], P(None, 'dp', 'mp')
- first_feed_forward: float32 [2, 768, 3072], P(None, 'dp', 'mp')
- second_feed_forward: float32 [2, 768, 3072], P(None, 'dp', 'mp')
- new_gate_logits: float32 [12, 1023], replicated
- first_gate_logits: float32 [12, 1023], replicated
- second_gate_logits: float32 [12, 1023], replicated
- new_norm_vectors: float32 [5, 768], replicated
- first_norm_vectors: float32 [5, 768], replicated
- second_norm_vectors: float32 [5, 768], replicated
- new_hidden_bias: float32 [3072], replicated
- first_hidden_bias: float32 [3072], replicated
- second_hidden_bias: float32 [3072], replicated
The draws below stay inside these ranges and needn't reach their ends.
Inputs may be any that keep to these rules, and one draw needn't show every extreme that they name: `seq_counts`: row w gives the counts c1, c2, c3, c4 of sequences of 128, 256, 384, 512 tokens in window w, with c1 + 2 c2 + 3 c3 + 4 c4 = 4. `pattern`: every diagonal entry is 1.
All inputs are finite; a program needn't handle non-finite values.
Results may differ from the reference program's by a relative error of at most 0.015.
Values may be sent and summed in bfloat16 or wider, within the bound.
A program may use at most 256 MiB of HBM per device.

```python
import math
import jax
import jax.numpy as jnp
from jax import lax

D = 768
H = 12
HEAD = 64
FF = 3072
TILE = 128
WIN = 512
STEP = 10
TOKENS = 16384
WINDOWS = 32


def draw_seq_counts(key, part):
    key = jax.random.fold_in(key, 11)
    kinds = jax.random.randint(key, (WINDOWS,), 0, 5)
    chosen = jax.random.randint(jax.random.fold_in(key, 1), (), 0, WINDOWS)
    kinds = jnp.where(jnp.arange(WINDOWS) == chosen, 4, kinds)
    table = jnp.array([[0, 0, 0, 1], [1, 0, 1, 0], [0, 2, 0, 0], [2, 1, 0, 0], [4, 0, 0, 0]], jnp.int32)
    return table[kinds].astype(jnp.int32)


def draw_pattern(key, part):
    key = jax.random.fold_in(key, 12)
    picks = jax.random.randint(key, (WIN, WIN), 0, 4)
    place = jnp.arange(WIN)
    diagonal = place[:, None] == place[None, :]
    return jnp.where(diagonal | (picks == 0), 1, 0).astype(jnp.int32)


def draw_norm_vectors(key, part):
    key = jax.random.fold_in(key, 13)
    gains = jax.random.uniform(key, (5, D), jnp.float32, 0.6, 1.4)
    shifts = 0.3 * jax.random.normal(jax.random.fold_in(key, 1), (5, D), jnp.float32)
    which = jnp.arange(5)[:, None]
    return jnp.where((which == 0) | (which == 2), gains, shifts).astype(jnp.float32)


def level_of(own_key, dims, shards, least, largest):
    level = 1.0
    for dim, parts in shards:
        steps = jax.random.uniform(jax.random.fold_in(jax.random.fold_in(own_key, 6), dim), (parts,), jnp.float32, least / len(shards), largest / len(shards))
        level = level * jnp.repeat(jnp.exp(steps), dims[dim] // parts).reshape((-1,) + (1,) * (len(dims) - 1 - dim))
    return level


def normal_values(rng, extent, scale, most, cuts=(), kind=jnp.bfloat16):
    level = level_of(rng, extent, cuts, -0.22, 0.18) if cuts else 1.0
    values = jax.random.normal(rng, extent, jnp.float32) * scale * level
    return jnp.minimum(jnp.maximum(values, -most), most).astype(kind)


def setup_inputs(seed: int = 0) -> dict:
    key_list = jax.random.split(jax.random.key(seed), 23)
    return {
        "tokens": normal_values(key_list[0], (TOKENS, D), 1.0, 6.0, ((0, 32),)),
        "cotangent": normal_values(key_list[1], (TOKENS, D), 1.0, 6.0, ((0, 32),)),
        "seq_counts": draw_seq_counts(jax.random.fold_in(key_list[22], 71), 0),
        "pattern": draw_pattern(jax.random.fold_in(key_list[22], 71), 0),
        "project_in": normal_values(key_list[4], (D, 3 * D), D ** -0.5, 0.21875, ((0, 16),), jnp.float32),
        "project_in_first": normal_values(key_list[5], (D, 3 * D), (0.1 * TOKENS ** 0.5), 80.0, ((0, 16),), jnp.float32),
        "project_in_second": jnp.clip(jnp.exp(math.log(65.536) - 1.3862944 * jax.random.uniform(key_list[6], (D, 3 * D), jnp.float32) ** level_of(key_list[6], (D, 3 * D), ((0, 16),), -0.2, 0.2)), 16.384, 65.536),
        "project_out": normal_values(key_list[7], (D, D), (max(8 * D // WIN, 1)) ** -0.5, 1.75, ((0, 16),), jnp.float32),
        "project_out_first": normal_values(key_list[8], (D, D), (0.01 * TOKENS ** 0.5), 8.0, ((0, 16),), jnp.float32),
        "project_out_second": jnp.clip(jnp.exp(math.log(0.65536) - 1.3862944 * jax.random.uniform(key_list[9], (D, D), jnp.float32) ** level_of(key_list[9], (D, D), ((0, 16),), -0.2, 0.2)), 0.16384, 0.65536),
        "feed_forward": normal_values(key_list[10], (2, D, FF), D ** -0.5, 0.21875, ((1, 16), (2, 2)), jnp.float32),
        "feed_forward_first": normal_values(key_list[11], (2, D, FF), (0.04 * TOKENS ** 0.5), 32.0, ((1, 16), (2, 2)), jnp.float32),
        "feed_forward_second": jnp.clip(jnp.exp(math.log(9.8304) - 1.3862944 * jax.random.uniform(key_list[12], (2, D, FF), jnp.float32) ** level_of(key_list[12], (2, D, FF), ((1, 16), (2, 2)), -0.2, 0.2)), 2.4576, 9.8304),
        "gate_logits": jnp.clip(jax.random.uniform(key_list[13], (H, 2 * WIN - 1), jnp.float32, -3.0, 3.0), -3.0, 3.0),
        "gate_logits_first": normal_values(key_list[14], (H, 2 * WIN - 1), (0.28 * WINDOWS ** 0.5), 10.0, (), jnp.float32),
        "gate_logits_second": jnp.clip(jnp.exp(jax.random.uniform(key_list[15], (H, 2 * WIN - 1), jnp.float32, math.log(0.256), math.log(1.024))), 0.256, 1.024),
        "norm_vectors": draw_norm_vectors(jax.random.fold_in(key_list[22], 71), 0),
        "norm_vectors_first": normal_values(key_list[17], (5, D), (0.1 * TOKENS ** 0.5), 80.0, (), jnp.float32),
        "norm_vectors_second": jnp.clip(jnp.exp(jax.random.uniform(key_list[18], (5, D), jnp.float32, math.log(16.384), math.log(65.536))), 16.384, 65.536),
        "hidden_bias": normal_values(key_list[19], (FF,), 0.3, 1.75, (), jnp.float32),
        "hidden_bias_first": normal_values(key_list[20], (FF,), (0.03 * TOKENS ** 0.5), 24.0, (), jnp.float32),
        "hidden_bias_second": jnp.clip(jnp.exp(jax.random.uniform(key_list[21], (FF,), jnp.float32, math.log(1.6384), math.log(6.5536))), 1.6384, 6.5536),
    }


@jax.custom_vjp
def low(v):
    return lax.optimization_barrier(v.astype(jnp.bfloat16)).astype(jnp.float32)

@jax.custom_vjp
def low_back(v):
    return v

def low_keep(v):
    return (low(v), None)

def low_pass(kept, grad):
    return (grad,)

def back_keep(v):
    return (v, None)

def back_low(kept, grad):
    return (low(grad),)
low.defvjp(low_keep, low_pass)
low_back.defvjp(back_keep, back_low)
HIGH = lax.Precision.HIGHEST
NORM_EPS = 1e-12
BETA_ONE = 0.9
BETA_TWO = 0.999
ADAM_EPS = 1e-08
DECAY = 0.01
MASKED = -1e+30
RATES = (0.03, 0.25, 0.03, 1.0, 0.2, 0.2)

def layer_norm(value, gain, shift):
    center = value - lax.optimization_barrier(jnp.mean(value, axis=-1, keepdims=True))
    spread = lax.optimization_barrier(jnp.mean(center * center, axis=-1, keepdims=True))
    return center * lax.rsqrt(spread + NORM_EPS) * gain + shift

def segment_layout(counts):
    place = jnp.arange(WIN, dtype=jnp.int32)
    tile = place // TILE
    after_four = 4 * counts[3]
    after_three = after_four + 3 * counts[2]
    after_two = after_three + 2 * counts[1]
    begin = jnp.where(tile < after_four, tile // 4 * 4, jnp.where(tile < after_three, after_four + (tile - after_four) // 3 * 3, jnp.where(tile < after_two, after_three + (tile - after_three) // 2 * 2, tile)))
    begin = (begin * TILE).astype(jnp.int32)
    return (begin, (place - begin).astype(jnp.int32))

def window_bias(counts, pattern, gate_table):
    begin, position = segment_layout(counts)
    same = begin[:, None] == begin[None, :]
    allowed = same & (pattern[position[:, None], position[None, :]] == 1)
    place = jnp.arange(WIN, dtype=jnp.int32)
    offset = (place[:, None] - place[None, :] + (WIN - 1)).astype(jnp.int32)
    table = gate_table[:, offset]
    return jnp.where(allowed[None], table, MASKED)

def window_attend(block, bias):
    query = block[:, :D].reshape(WIN, H, HEAD)
    keys = block[:, D:2 * D].reshape(WIN, H, HEAD)
    values = block[:, 2 * D:].reshape(WIN, H, HEAD)
    scale = HEAD ** (-0.5)
    raw = low_back(jnp.einsum('qhd,khd->hqk', query, keys, precision=HIGH) * scale)
    scores = raw + bias
    top = lax.optimization_barrier(jnp.max(scores, axis=-1, keepdims=True))
    expo = jnp.exp(scores - top)
    attend = expo / lax.optimization_barrier(jnp.sum(expo, axis=-1, keepdims=True))
    context = jnp.einsum('hqk,khd->qhd', low(attend), values, precision=HIGH)
    return context.reshape(WIN, D)

def layer_forward(params, tokens, counts, pattern):
    project_in, project_out, feed_forward, gate_logits, norm_vectors, hidden_bias = params
    mixed = low_back(low(jnp.dot(tokens, low(project_in), precision=HIGH)))
    gate_table = jax.nn.log_sigmoid(gate_logits)
    windows = tokens.shape[0] // WIN
    grouped = mixed.reshape(windows, WIN, 3 * D)

    def one_window(item):
        block, count_row = item
        return window_attend(block, window_bias(count_row, pattern, gate_table))
    context = lax.map(jax.checkpoint(one_window), (grouped, counts)).reshape(-1, D)
    context = low_back(low(context))
    branch = low_back(jnp.dot(context, low(project_out), precision=HIGH))
    summed = tokens + branch
    normed = low_back(low(layer_norm(summed, norm_vectors[0], norm_vectors[1])))
    before = low_back(jnp.dot(normed, low(feed_forward[0]), precision=HIGH) + hidden_bias)
    active = low(jax.nn.gelu(before, approximate=False))
    result = low_back(jnp.dot(active, low(feed_forward[1]).T, precision=HIGH))
    total = normed + result + norm_vectors[4]
    return layer_norm(total, norm_vectors[2], norm_vectors[3])

def adam_step(weight, first, second, grad, rate):
    first = BETA_ONE * first + (1.0 - BETA_ONE) * grad
    second = BETA_TWO * second + (1.0 - BETA_TWO) * grad * grad
    update = first / (1.0 - BETA_ONE ** STEP) / (jnp.sqrt(second / (1.0 - BETA_TWO ** STEP)) + ADAM_EPS)
    return (weight - rate * (update + DECAY * weight), first, second)

def reference(tokens, cotangent, seq_counts, pattern, project_in, project_in_first, project_in_second, project_out, project_out_first, project_out_second, feed_forward, feed_forward_first, feed_forward_second, gate_logits, gate_logits_first, gate_logits_second, norm_vectors, norm_vectors_first, norm_vectors_second, hidden_bias, hidden_bias_first, hidden_bias_second):
    params = (project_in, project_out, feed_forward, gate_logits, norm_vectors, hidden_bias)
    rows = 8 * WIN
    groups = TOKENS // rows
    token_groups = tokens.astype(jnp.float32).reshape(groups, rows, D)
    back_groups = cotangent.astype(jnp.float32).reshape(groups, rows, D)
    count_groups = seq_counts.reshape(groups, 8, 4)

    def one_group(carry, item):
        block, back, counts = item

        def forward(weights, inputs):
            return layer_forward(weights, inputs, counts, pattern)
        outcome, pullback = jax.vjp(forward, params, block)
        grads, block_grad = pullback(back)
        carry = jax.tree.map(jnp.add, carry, grads)
        return (carry, (outcome.astype(jnp.bfloat16), block_grad))
    zeros = jax.tree.map(jnp.zeros_like, params)
    sums, (outcomes, block_grads) = lax.scan(one_group, zeros, (token_groups, back_groups, count_groups))
    firsts = (project_in_first, project_out_first, feed_forward_first, gate_logits_first, norm_vectors_first, hidden_bias_first)
    seconds = (project_in_second, project_out_second, feed_forward_second, gate_logits_second, norm_vectors_second, hidden_bias_second)
    updated = []
    for index in range(6):
        updated.extend(adam_step(params[index], firsts[index], seconds[index], sums[index], RATES[index]))
    return (outcomes.reshape(TOKENS, D), block_grads.reshape(TOKENS, D), updated[0], updated[1], updated[2], updated[3], updated[4], updated[5], updated[6], updated[7], updated[8], updated[9], updated[10], updated[11], updated[12], updated[13], updated[14], updated[15], updated[16], updated[17])
```

```python
import functools
import math

import jax
import jax.numpy as jnp
from jax import lax
from jax.experimental import pallas as pl
from jax.experimental.pallas import tpu as pltpu
from jax.sharding import PartitionSpec as P

D = 768
H = 12
HEAD = 64
FF = 3072
TILE = 128
WIN = 512
STEP = 10
HALF = 2
HD = D // HALF
HF = FF // HALF
CH = 512
NCH = HF // CH
PAIRS = HD // 128

NORM_EPS = 1e-12
BETA_ONE = 0.9
BETA_TWO = 0.999
ADAM_EPS = 1e-08
DECAY = 0.01
MASKED = -1e30
RATES = (0.03, 0.25, 0.03, 1.0, 0.2, 0.2)

F32 = jnp.float32
BF = jnp.bfloat16
NN = ((1,), (0,))
NT = ((1,), (1,))
R_VEC, R_HID, R_ALL = 24, 34, 40


def dot(a, b, dims=NN):
    return lax.dot_general(a, b, (dims, ((), ())), preferred_element_type=F32)


def adam_step(weight, first, second, grad, rate):
    first = BETA_ONE * first + (1.0 - BETA_ONE) * grad
    second = BETA_TWO * second + (1.0 - BETA_TWO) * grad * grad
    update = first / (1.0 - BETA_ONE**STEP) / (jnp.sqrt(second / (1.0 - BETA_TWO**STEP)) + ADAM_EPS)
    return (weight - rate * (update + DECAY * weight), first, second)


def cols(ref, part, start, size):
    block = ref[part, :, :, :, :, pl.ds(start, size)]
    return block.reshape(D, size)


def put_cols(ref, part, start, value):
    shape = ref.shape[1:5] + (value.shape[1],)
    ref[part, :, :, :, :, pl.ds(start, value.shape[1])] = value.reshape(shape)


def build_mask(counts, pattern, mask):
    two, three, four = counts[0, 1], counts[0, 2], counts[0, 3]
    after_four = 4 * four
    after_three = after_four + 3 * three
    after_two = after_three + 2 * two
    begins, places = [], []
    for tile in range(WIN // TILE):
        in_three = after_four + jnp.where(tile - after_four >= 3, 3, 0)
        in_two = after_three + jnp.where(tile - after_three >= 2, 2, 0)
        begin = jnp.where(
            tile < after_four,
            0,
            jnp.where(tile < after_three, in_three, jnp.where(tile < after_two, in_two, tile)),
        )
        begins.append(begin)
        places.append(pl.multiple_of((tile - begin) * TILE, TILE))
    for i in range(WIN // TILE):
        for j in range(WIN // TILE):
            block = pattern[pl.ds(places[i], TILE), pl.ds(places[j], TILE)].astype(F32)
            block = jnp.where(block > 0.5, 0.0, MASKED)
            block = jnp.where(begins[i] == begins[j], block, MASKED)
            mask[pl.ds(j * TILE, TILE), pl.ds(i * TILE, TILE)] = block.T


def build_bias(gate, table, bias):
    x = gate[...]
    x = jnp.minimum(x, 0.0) - jnp.log(1.0 + jnp.exp(-jnp.abs(x)))
    table[:, pl.ds(0, x.shape[1])] = x

    def one(h, _):
        row = table[pl.ds(h, 1), :]
        for d in range(7):
            part = jnp.broadcast_to(row[:, d * TILE : d * TILE + 2 * TILE], (TILE, 2 * TILE))
            bias[h, d] = pltpu.roll(part, TILE + 1, 1, stride=1, stride_axis=0)[:, :TILE]
        return 0

    lax.fori_loop(0, H, one, 0)


def project_mixed(part, tok, wi, mixed_t, mixed_n):
    for kind in range(3):
        value = dot(tok[...], cols(wi, part, kind * HD, HD)).astype(BF)
        if kind == 0:
            value = value * jnp.asarray(HEAD**-0.5, BF)
        else:
            mixed_n[part, :, pl.ds((kind - 1) * HD, HD)] = value
        mixed_t[part, pl.ds(kind * HD, HD), :] = value.T


def pad_head(value, e):
    zero = jnp.zeros_like(value)
    return jnp.concatenate([value, zero] if e == 0 else [zero, value], axis=0)


def attend_pair(part, g, mixed_t, mixed_n, bias, mask, scores, attend, context_t):
    keys = mixed_n[part, :, pl.ds(pl.multiple_of(g * 128, 128), 128)]
    for e in range(2):
        row = pl.multiple_of(g * 128 + e * HEAD, HEAD)
        h = part * (H // HALF) + g * 2 + e
        query = pad_head(mixed_t[part, pl.ds(row, HEAD), :], e)
        scores[...] = dot(keys, query)
        for i in range(WIN // TILE):
            here = pl.ds(i * TILE, TILE)
            table = jnp.concatenate([bias[h, i - j + 3] for j in range(WIN // TILE)], axis=0)
            s = scores[:, here] + (table + mask[:, here])
            top = jnp.max(s, axis=0, keepdims=True)
            s = jnp.exp(s - top)
            total = jnp.sum(s, axis=0, keepdims=True)
            attend[h, :, here] = (s * (1.0 / total)).astype(BF)
        values = mixed_t[part, pl.ds(pl.multiple_of(2 * HD + row, HEAD), HEAD), :]
        out = dot(values, attend[h])
        context_t[pl.ds(pl.multiple_of(part * HD + row, HEAD), HEAD), :] = out.astype(BF)


def norm_of(value):
    mean = jnp.mean(value, axis=-1, keepdims=True)
    center = value - mean
    spread = jnp.mean(center * center, axis=-1, keepdims=True)
    scale = lax.rsqrt(spread + NORM_EPS)
    return center * scale, scale


def norm_back(grad, hat, scale, gain):
    g = grad * gain
    first = jnp.mean(g, axis=-1, keepdims=True)
    second = jnp.mean(g * hat, axis=-1, keepdims=True)
    return (
        scale * (g - first - hat * second),
        jnp.sum(grad * hat, axis=0, keepdims=True),
        jnp.sum(grad, axis=0, keepdims=True),
    )


ROWS = 256


def out_project(tok, context_t, wo, vectors, hat, scale, normed, normed_t):
    for r in range(0, WIN, ROWS):
        here = pl.ds(r, ROWS)
        context = context_t[:, here].T
        branch = jnp.concatenate(
            [dot(context, cols(wo, part, 0, HD)) for part in range(HALF)], axis=1
        )
        h, s = norm_of(tok[here, :].astype(F32) + branch)
        hat[here, :] = h
        scale[here, :] = jnp.broadcast_to(s, (ROWS, 128))
        low = (h * vectors[0:1, :] + vectors[1:2, :]).astype(BF)
        normed[here, :] = low
        normed_t[:, here] = low.T


def hidden_step(part, c, normed, w1, hidden, active, slope):
    j = part * NCH + c
    before = dot(normed[...], cols(w1, part, pl.multiple_of(c * CH, CH), CH)) + hidden[pl.ds(j, 1), :]
    half = 0.5 + 0.5 * lax.erf(before * math.sqrt(0.5))
    active[j] = (before * half).astype(BF)
    bell = jnp.exp(-0.5 * before * before) * (1.0 / math.sqrt(2 * math.pi))
    slope[j] = (half + before * bell).astype(BF)


def result_step(part, c, active, w2, acc):
    acc[...] += dot(active[part * NCH + c], cols(w2, part, pl.multiple_of(c * CH, CH), CH), NT)


def second_norm(acc, normed, cot, vectors, low_out, grad, grad_t, small):
    sums = [0.0, 0.0, 0.0]
    for r in range(0, WIN, ROWS):
        here = pl.ds(r, ROWS)
        total = normed[here, :].astype(F32) + acc[here, :] + vectors[4:5, :]
        hat, scale = norm_of(total)
        low_out[here, :] = (hat * vectors[2:3, :] + vectors[3:4, :]).astype(BF)
        value, gain, shift = norm_back(cot[here, :].astype(F32), hat, scale, vectors[2:3, :])
        acc[here, :] = value
        low = value.astype(BF)
        grad[here, :] = low
        grad_t[:, here] = low.T
        sums = [a + b for a, b in zip(sums, (gain, shift, jnp.sum(value, axis=0, keepdims=True)))]
    for k in range(3):
        put_vector(small, 2 + k, sums[k])


def put_vector(small, k, value):
    small[pl.ds(R_VEC + k, 1), :] = value[:, :512]
    small[pl.ds(R_VEC + 5 + k, 1), :] = jnp.concatenate(
        [value[:, 512:], jnp.zeros((1, 256), F32)], axis=1
    )


def hidden_back(part, c, grad, grad_t, normed_t, w1, w2, g1, g2, active, slope, acc, small):
    j = part * NCH + c
    start = pl.multiple_of(c * CH, CH)
    before = (dot(grad[...], cols(w2, part, start, CH)) * slope[j].astype(F32)).astype(BF)
    put_cols(g2, part, start, dot(grad_t[...], active[j]).astype(BF))
    small[pl.ds(R_HID + j, 1), :] = jnp.sum(before.astype(F32), axis=0, keepdims=True)
    acc[...] += dot(before, cols(w1, part, start, CH), NT)
    put_cols(g1, part, start, dot(normed_t[...], before).astype(BF))


def first_norm_back(acc, hat, scale, vectors, grad_low, small):
    sums = [0.0, 0.0]
    for r in range(0, WIN, ROWS):
        here = pl.ds(r, ROWS)
        grad = acc[here, :].astype(BF).astype(F32)
        value, gain, shift = norm_back(grad, hat[here, :], scale[here, 0:1], vectors[0:1, :])
        hat[here, :] = value
        grad_low[here, :] = value.astype(BF)
        sums = [a + b for a, b in zip(sums, (gain, shift))]
    for k in range(2):
        put_vector(small, k, sums[k])


def out_back(grad_low, context_t, wo, go, grad_context_t):
    for r in range(0, WIN, ROWS):
        here = pl.ds(r, ROWS)
        low = grad_low[here, :]
        value = 0.0
        for part in range(HALF):
            value = value + dot(cols(wo, part, 0, HD), low[:, part * HD : (part + 1) * HD], NT)
        grad_context_t[:, here] = value.astype(BF)
    for part in range(HALF):
        low = grad_low[:, pl.ds(part * HD, HD)]
        put_cols(go, part, 0, dot(context_t[...], low).astype(BF))


def attend_back_pair(part, g, mixed_t, mixed_n, attend, context_t, grad_context_t, scores, grad_mixed_t, small):
    values = mixed_n[part, :, pl.ds(pl.multiple_of(HD + g * 128, 128), 128)]
    for e in range(2):
        row = pl.multiple_of(g * 128 + e * HEAD, HEAD)
        h = part * (H // HALF) + g * 2 + e
        place = pl.ds(pl.multiple_of(part * HD + row, HEAD), HEAD)
        grad_c = grad_context_t[place, :]
        inner = jnp.sum(
            grad_c.astype(F32) * context_t[place, :].astype(F32), axis=0, keepdims=True
        )
        scores[...] = dot(values, pad_head(grad_c, e))
        tiles = [0.0] * 7
        for i in range(WIN // TILE):
            here = pl.ds(i * TILE, TILE)
            ds = attend[h, :, here].astype(F32) * (scores[:, here] - inner[:, i * TILE : (i + 1) * TILE])
            for j in range(WIN // TILE):
                d = i - j + 3
                tiles[d] = tiles[d] + ds[j * TILE : (j + 1) * TILE, :]
            scores[:, here] = ds
        low = scores[...].astype(BF)
        key = mixed_t[part, pl.ds(pl.multiple_of(HD + row, HEAD), HEAD), :]
        query = mixed_t[part, pl.ds(row, HEAD), :]
        gq = dot(key, low) * (HEAD**-0.5)
        gk = dot(query, low, NT)
        gv = dot(grad_c, attend[h], NT)
        grad_mixed_t[part, pl.ds(row, HEAD), :] = gq.astype(BF)
        grad_mixed_t[part, pl.ds(pl.multiple_of(HD + row, HEAD), HEAD), :] = gk.astype(BF)
        grad_mixed_t[part, pl.ds(pl.multiple_of(2 * HD + row, HEAD), HEAD), :] = gv.astype(BF)
        blocks = [0.0] * 8
        turn = lax.broadcasted_iota(jnp.int32, (TILE, TILE), 0) + lax.broadcasted_iota(
            jnp.int32, (TILE, TILE), 1
        )
        turn = jnp.where(turn == TILE - 1, 1.0, 0.0).astype(BF)
        turned = dot(turn, jnp.concatenate([t.astype(BF) for t in tiles], axis=1))
        for d in range(7):
            wide = turned[:, d * TILE : (d + 1) * TILE]
            wide = jnp.concatenate([wide, jnp.zeros((TILE, TILE), F32)], axis=1)
            wide = pltpu.roll(wide, 0, 1, stride=1, stride_axis=0)
            line = jnp.sum(wide, axis=0, keepdims=True)
            blocks[d] = blocks[d] + line[:, :TILE]
            blocks[d + 1] = blocks[d + 1] + line[:, TILE:]
        small[pl.ds(h, 1), :] = jnp.concatenate(blocks[:4], axis=1)
        small[pl.ds(H + h, 1), :] = jnp.concatenate(blocks[4:], axis=1)


def project_back(part, tok_t, grad_mixed_t, gi):
    for kind in range(3):
        value = dot(tok_t[...], grad_mixed_t[part, pl.ds(kind * HD, HD), :], NT)
        put_cols(gi, part, kind * HD, value.astype(BF))


def input_back(grad_mixed_t, wi, hat, out):
    for r in range(0, WIN, ROWS):
        here = pl.ds(r, ROWS)
        value = 0.0
        for part in range(HALF):
            value = value + dot(cols(wi, part, 0, 3 * HD), grad_mixed_t[part, :, here])
        out[here, :] = hat[here, :] + value.T


def layer_kernel(
    counts,
    tok,
    cot,
    pattern,
    gate,
    vectors,
    hidden,
    wi_in,
    wo_in,
    w1_in,
    w2_in,
    low_out,
    grad_out,
    small,
    gi_out,
    go_out,
    g1_out,
    g2_out,
    wi,
    wo,
    w1,
    w2,
    gi,
    tok_t,
    mixed_t,
    mixed_n,
    attend,
    scores,
    context_t,
    hat,
    scale,
    normed,
    acc,
    table,
    grad_low,
    grad_context_t,
    sems,
):
    copies = [
        pltpu.make_async_copy(src, dst, sems.at[k])
        for k, (src, dst) in enumerate(((wi_in, wi), (wo_in, wo), (w1_in, w1), (w2_in, w2)))
    ]
    for copy in copies:
        copy.start()
    tok_t[...] = tok[...].T

    def attention(bias, mask):
        build_mask(counts, pattern, mask)
        build_bias(gate, table, bias)
        copies[0].wait()
        for part in range(HALF):
            project_mixed(part, tok, wi, mixed_t, mixed_n)

            def one(g, _):
                attend_pair(part, g, mixed_t, mixed_n, bias, mask, scores, attend, context_t)
                return 0

            lax.fori_loop(0, PAIRS, one, 0)

    pl.run_scoped(attention, pltpu.VMEM((H, 7, TILE, TILE), F32), pltpu.VMEM((WIN, WIN), F32))

    def feed(active, slope, normed_t, grad, grad_t):
        copies[1].wait()
        out_project(tok, context_t, wo, vectors, hat, scale, normed, normed_t)
        copies[2].wait()
        for part in range(HALF):

            def one(c, _):
                hidden_step(part, c, normed, w1, hidden, active, slope)
                return 0

            lax.fori_loop(0, NCH, one, 0)
        copies[3].wait()
        acc[...] = jnp.zeros_like(acc)
        for part in range(HALF):

            def two(c, _):
                result_step(part, c, active, w2, acc)
                return 0

            lax.fori_loop(0, NCH, two, 0)
        second_norm(acc, normed, cot, vectors, low_out, grad, grad_t, small)
        for part in range(HALF):

            def three(c, _):
                hidden_back(
                    part, c, grad, grad_t, normed_t, w1, w2, w1, w2, active, slope, acc, small
                )
                return 0

            lax.fori_loop(0, NCH, three, 0)

    pl.run_scoped(
        feed,
        pltpu.VMEM((HALF * NCH, WIN, CH), BF),
        pltpu.VMEM((HALF * NCH, WIN, CH), BF),
        pltpu.VMEM((D, WIN), BF),
        pltpu.VMEM((WIN, D), BF),
        pltpu.VMEM((D, WIN), BF),
    )

    def last(grad_mixed_t):
        first_norm_back(acc, hat, scale, vectors, grad_low, small)
        out_back(grad_low, context_t, wo, wo, grad_context_t)
        for part in range(HALF):

            def one(g, _):
                attend_back_pair(
                    part,
                    g,
                    mixed_t,
                    mixed_n,
                    attend,
                    context_t,
                    grad_context_t,
                    scores,
                    grad_mixed_t,
                    small,
                )
                return 0

            lax.fori_loop(0, PAIRS, one, 0)
            project_back(part, tok_t, grad_mixed_t, gi)
        input_back(grad_mixed_t, wi, hat, grad_out)

    pl.run_scoped(last, pltpu.VMEM((HALF, 3 * HD, WIN), BF))
    outs = [
        pltpu.make_async_copy(src, dst, sems.at[k])
        for k, (src, dst) in enumerate(((gi, gi_out), (wo, go_out), (w1, g1_out), (w2, g2_out)))
    ]
    for copy in outs:
        copy.start()
    for copy in outs:
        copy.wait()


def layer_call(counts, tok, cot, pattern, gate, vectors, hidden, wi, wo, w1, w2):
    vmem = pl.BlockSpec(memory_space=pltpu.VMEM)
    hbm = pl.BlockSpec(memory_space=pl.ANY)
    lead = (HALF, 1, 1, 1, D)
    shapes = [lead + (w.shape[-1],) for w in (wi, wo, w1, w2)]
    weights = [w.reshape(s) for w, s in zip((wi, wo, w1, w2), shapes)]
    return pl.pallas_call(
        layer_kernel,
        out_shape=[
            jax.ShapeDtypeStruct((WIN, D), BF),
            jax.ShapeDtypeStruct((WIN, D), F32),
            jax.ShapeDtypeStruct((R_ALL, 512), F32),
        ]
        + [jax.ShapeDtypeStruct(s, BF) for s in shapes],
        in_specs=[pl.BlockSpec(memory_space=pltpu.SMEM)] + [vmem] * 6 + [hbm] * 4,
        out_specs=[vmem] * 3 + [hbm] * 4,
        scratch_shapes=[pltpu.VMEM(s, BF) for s in shapes]
        + [
            pltpu.VMEM(shapes[0], BF),
            pltpu.VMEM((D, WIN), BF),
            pltpu.VMEM((HALF, 3 * HD, WIN), BF),
            pltpu.VMEM((HALF, WIN, 2 * HD), BF),
            pltpu.VMEM((H, WIN, WIN), BF),
            pltpu.VMEM((WIN, WIN), F32),
            pltpu.VMEM((D, WIN), BF),
            pltpu.VMEM((WIN, D), F32),
            pltpu.VMEM((WIN, 128), F32),
            pltpu.VMEM((WIN, D), BF),
            pltpu.VMEM((WIN, D), F32),
            pltpu.VMEM((H, 2 * WIN), F32),
            pltpu.VMEM((WIN, D), BF),
            pltpu.VMEM((D, WIN), BF),
            pltpu.SemaphoreType.DMA((4,)),
        ],
        compiler_params=pltpu.CompilerParams(vmem_limit_bytes=62 * 2**20),
        cost_estimate=pl.CostEstimate(
            flops=25 * 10**9, bytes_accessed=40 * 2**20, transcendentals=10**7
        ),
        name="layer",
    )(counts, tok, cot, pattern, gate, vectors, hidden, *weights)


def local(
    tokens,
    cotangent,
    seq_counts,
    pattern,
    project_in,
    project_in_first,
    project_in_second,
    project_out,
    project_out_first,
    project_out_second,
    feed_forward,
    feed_forward_first,
    feed_forward_second,
    gate_logits,
    gate_logits_first,
    gate_logits_second,
    norm_vectors,
    norm_vectors_first,
    norm_vectors_second,
    hidden_bias,
    hidden_bias_first,
    hidden_bias_second,
):
    whole_in = lax.all_gather(project_in.astype(BF), "dp", axis=0, tiled=True)
    whole_out = lax.all_gather(project_out.astype(BF), "dp", axis=0, tiled=True)
    pair = lax.all_gather(feed_forward.astype(BF), "dp", axis=1, tiled=True)
    pair = lax.all_gather(pair, "mp", axis=2, tiled=True)
    wi = whole_in.reshape(D, 3, HALF, HD).transpose(2, 0, 1, 3).reshape(HALF, D, 3 * HD)
    wo = whole_out.reshape(D, HALF, HD).transpose(1, 0, 2)
    w1 = pair[0].reshape(D, HALF, HF).transpose(1, 0, 2)
    w2 = pair[1].reshape(D, HALF, HF).transpose(1, 0, 2)
    layer_out, input_grad, small, gi, go, g1, g2 = layer_call(
        seq_counts,
        tokens,
        cotangent,
        pattern,
        gate_logits,
        norm_vectors,
        hidden_bias.reshape(HALF * NCH, CH),
        wi,
        wo,
        w1,
        w2,
    )
    gi = gi.reshape(HALF, D, 3, HD).transpose(1, 2, 0, 3).reshape(D, 3 * D)
    go = go.reshape(HALF, D, HD).transpose(1, 0, 2).reshape(D, D)
    gf = jnp.stack(
        [g.reshape(HALF, D, HF).transpose(1, 0, 2).reshape(D, FF) for g in (g1, g2)]
    )
    sum_in = lax.psum(lax.psum_scatter(gi, "dp", scatter_dimension=0, tiled=True).astype(F32), "mp")
    sum_out = lax.psum(
        lax.psum_scatter(go, "dp", scatter_dimension=0, tiled=True).astype(F32), "mp"
    )
    sum_pair = lax.psum_scatter(gf, "dp", scatter_dimension=1, tiled=True)
    sum_pair = lax.psum_scatter(sum_pair, "mp", scatter_dimension=2, tiled=True).astype(F32)
    small = lax.psum(small, ("dp", "mp"))
    sum_gate = jnp.concatenate([small[:H], small[H : 2 * H]], axis=1)[:, : 2 * WIN - 1]
    sum_gate = sum_gate * jax.nn.sigmoid(-gate_logits)
    sum_vectors = jnp.concatenate(
        [small[R_VEC : R_VEC + 5], small[R_VEC + 5 : R_VEC + 10, :256]], axis=1
    )
    sum_bias = small[R_HID:].reshape(FF)
    outs = [layer_out, input_grad]
    for weight, first, second, grad, rate in (
        (project_in, project_in_first, project_in_second, sum_in, RATES[0]),
        (project_out, project_out_first, project_out_second, sum_out, RATES[1]),
        (feed_forward, feed_forward_first, feed_forward_second, sum_pair, RATES[2]),
        (gate_logits, gate_logits_first, gate_logits_second, sum_gate, RATES[3]),
        (norm_vectors, norm_vectors_first, norm_vectors_second, sum_vectors, RATES[4]),
        (hidden_bias, hidden_bias_first, hidden_bias_second, sum_bias, RATES[5]),
    ):
        outs.extend(adam_step(weight, first, second, grad, rate))
    return tuple(outs)


def solution(mesh):
    rows, whole = P(("dp", "mp"), None), P()
    split, pair = P("dp", None), P(None, "dp", "mp")
    return jax.shard_map(
        local,
        mesh=mesh,
        in_specs=(rows, rows, rows, whole) + (split,) * 6 + (pair,) * 3 + (whole,) * 9,
        out_specs=(rows, rows) + (split,) * 6 + (pair,) * 3 + (whole,) * 9,
        check_vma=False,
    )
```

```python
import functools
import math

import jax
import jax.numpy as jnp
from jax import lax
from jax.experimental import pallas as pl
from jax.experimental.pallas import tpu as pltpu
from jax.sharding import PartitionSpec as P

D = 768
H = 12
HEAD = 64
FF = 3072
TILE = 128
WIN = 512
STEP = 10
HALF = 2
HD = D // HALF
HF = FF // HALF
CH = 512
NCH = HF // CH
PAIRS = HD // 128
PC = 3 * 128

NORM_EPS = 1e-12
BETA_ONE = 0.9
BETA_TWO = 0.999
ADAM_EPS = 1e-08
DECAY = 0.01
MASKED = -1e30
RATES = (0.03, 0.25, 0.03, 1.0, 0.2, 0.2)

F32 = jnp.float32
BF = jnp.bfloat16
NN = ((1,), (0,))
NT = ((1,), (1,))
R_VEC, R_HID, R_ALL = 24, 34, 40


def dot(a, b, dims=NN):
    return lax.dot_general(a, b, (dims, ((), ())), preferred_element_type=F32)


def adam_step(weight, first, second, grad, rate):
    first = BETA_ONE * first + (1.0 - BETA_ONE) * grad
    second = BETA_TWO * second + (1.0 - BETA_TWO) * grad * grad
    update = first / (1.0 - BETA_ONE**STEP) / (jnp.sqrt(second / (1.0 - BETA_TWO**STEP)) + ADAM_EPS)
    return (weight - rate * (update + DECAY * weight), first, second)


def cols(ref, part, start, size):
    block = ref[part, :, :, :, :, pl.ds(start, size)]
    return block.reshape(D, size)


def put_cols(ref, part, start, value):
    shape = ref.shape[1:5] + (value.shape[1],)
    ref[part, :, :, :, :, pl.ds(start, value.shape[1])] = value.reshape(shape)


def build_mask(counts, pattern, mask):
    two, three, four = counts[0, 1], counts[0, 2], counts[0, 3]
    after_four = 4 * four
    after_three = after_four + 3 * three
    after_two = after_three + 2 * two
    tiles = WIN // TILE
    begins = []
    for tile in range(tiles):
        in_three = after_four + jnp.where(tile - after_four >= 3, 3, 0)
        in_two = after_three + jnp.where(tile - after_three >= 2, 2, 0)
        begin = jnp.where(
            tile < after_four,
            0,
            jnp.where(tile < after_three, in_three, jnp.where(tile < after_two, in_two, tile)),
        )
        begins.append(begin)
    starts = [
        [jnp.where(begins[tile] == b, 1.0, 0.0) for b in range(tile + 1)] for tile in range(tiles)
    ]
    for i in range(tiles):
        for j in range(tiles):
            allowed = jnp.zeros((TILE, TILE), F32)
            for b in range(min(i, j) + 1):
                block = pattern[pl.ds((i - b) * TILE, TILE), pl.ds((j - b) * TILE, TILE)]
                allowed = allowed + block.astype(F32) * (starts[i][b] * starts[j][b])
            allowed = jnp.where(allowed > 0.5, 0.0, MASKED)
            mask[pl.ds(j * TILE, TILE), pl.ds(i * TILE, TILE)] = allowed.T


def build_bias(gate, table, bias):
    x = gate[...]
    x = jnp.minimum(x, 0.0) - jnp.log(1.0 + jnp.exp(-jnp.abs(x)))
    table[:, pl.ds(0, x.shape[1])] = x

    def one(h, _):
        row = table[pl.ds(h, 1), :]
        for d in range(7):
            part = jnp.broadcast_to(row[:, d * TILE : d * TILE + 2 * TILE], (TILE, 2 * TILE))
            bias[h, d] = pltpu.roll(part, TILE + 1, 1, stride=1, stride_axis=0)[:, :TILE]
        return 0

    lax.fori_loop(0, H, one, 0)


def project_mixed(part, g, tok, wi, mixed_t, mixed_n):
    value = dot(tok[...], cols(wi, part, g * PC, PC)).astype(BF)
    mixed_n[part, :, pl.ds(g * 256, 256)] = value[:, 128:]
    query = value[:, :128] * jnp.asarray(HEAD**-0.5, BF)
    mixed_t[part, pl.ds(g * PC, PC), :] = jnp.concatenate([query.T, value[:, 128:].T], axis=0)


def pad_head(value, e):
    zero = jnp.zeros_like(value)
    return jnp.concatenate([value, zero] if e == 0 else [zero, value], axis=0)


def attend_pair(part, g, mixed_t, mixed_n, bias, mask, scores, attend, context_t):
    keys = mixed_n[part, :, pl.ds(g * 256, 128)]
    for e in range(2):
        row = g * PC + e * HEAD
        h = part * (H // HALF) + g * 2 + e
        query = pad_head(mixed_t[part, pl.ds(row, HEAD), :], e)
        scores[...] = dot(keys, query)
        for i in range(WIN // TILE):
            here = pl.ds(i * TILE, TILE)
            table = jnp.concatenate([bias[h, i - j + 3] for j in range(WIN // TILE)], axis=0)
            s = scores[:, here] + (table + mask[:, here])
            top = jnp.max(s, axis=0, keepdims=True)
            s = jnp.exp(s - top)
            total = jnp.sum(s, axis=0, keepdims=True)
            attend[h, :, here] = (s * (1.0 / total)).astype(BF)
        values = mixed_t[part, pl.ds(row + 256, HEAD), :]
        out = dot(values, attend[h])
        context_t[pl.ds(pl.multiple_of(h * HEAD, HEAD), HEAD), :] = out.astype(BF)


def norm_of(value):
    mean = jnp.mean(value, axis=-1, keepdims=True)
    center = value - mean
    spread = jnp.mean(center * center, axis=-1, keepdims=True)
    scale = lax.rsqrt(spread + NORM_EPS)
    return center * scale, scale


def norm_back(grad, hat, scale, gain):
    g = grad * gain
    first = jnp.mean(g, axis=-1, keepdims=True)
    second = jnp.mean(g * hat, axis=-1, keepdims=True)
    return (
        scale * (g - first - hat * second),
        jnp.sum(grad * hat, axis=0, keepdims=True),
        jnp.sum(grad, axis=0, keepdims=True),
    )


ROWS = 256


def out_project(tok, context_t, wo, vectors, hat, scale, normed, normed_t):
    for r in range(0, WIN, ROWS):
        here = pl.ds(r, ROWS)
        context = context_t[:, here].T
        branch = jnp.concatenate(
            [dot(context, cols(wo, part, 0, HD)) for part in range(HALF)], axis=1
        )
        h, s = norm_of(tok[here, :].astype(F32) + branch)
        hat[here, :] = h
        scale[here, :] = jnp.broadcast_to(s, (ROWS, 128))
        low = (h * vectors[0:1, :] + vectors[1:2, :]).astype(BF)
        normed[here, :] = low
        normed_t[:, here] = low.T


def hidden_step(part, c, normed, w1, hidden, active, slope):
    j = part * NCH + c
    before = dot(normed[...], cols(w1, part, c * CH, CH)) + hidden[pl.ds(j, 1), :]
    half = 0.5 + 0.5 * lax.erf(before * math.sqrt(0.5))
    active[j] = (before * half).astype(BF)
    bell = jnp.exp(-0.5 * before * before) * (1.0 / math.sqrt(2 * math.pi))
    slope[j] = (half + before * bell).astype(BF)


def result_step(c, active, w2, acc):
    value = 0.0
    for part in range(HALF):
        value = value + dot(active[part * NCH + c], cols(w2, part, c * CH, CH), NT)
    acc[...] = value if c == 0 else acc[...] + value


def second_norm(acc, normed, cot, vectors, low_out, grad, grad_t, small):
    sums = [0.0, 0.0, 0.0]
    for r in range(0, WIN, ROWS):
        here = pl.ds(r, ROWS)
        total = normed[here, :].astype(F32) + acc[here, :] + vectors[4:5, :]
        hat, scale = norm_of(total)
        low_out[here, :] = (hat * vectors[2:3, :] + vectors[3:4, :]).astype(BF)
        value, gain, shift = norm_back(cot[here, :].astype(F32), hat, scale, vectors[2:3, :])
        acc[here, :] = value
        low = value.astype(BF)
        grad[here, :] = low
        grad_t[:, here] = low.T
        sums = [a + b for a, b in zip(sums, (gain, shift, jnp.sum(value, axis=0, keepdims=True)))]
    for k in range(3):
        put_vector(small, 2 + k, sums[k])


def put_vector(small, k, value):
    small[pl.ds(R_VEC + k, 1), :] = value[:, :512]
    small[pl.ds(R_VEC + 5 + k, 1), :] = jnp.concatenate(
        [value[:, 512:], jnp.zeros((1, 256), F32)], axis=1
    )


def hidden_back(part, c, grad, grad_t, normed_t, w1, w2, g1, g2, active, slope, acc, small):
    j = part * NCH + c
    start = c * CH
    before = (dot(grad[...], cols(w2, part, start, CH)) * slope[j].astype(F32)).astype(BF)
    put_cols(g2, part, start, dot(grad_t[...], active[j]).astype(BF))
    small[pl.ds(R_HID + j, 1), :] = jnp.sum(before.astype(F32), axis=0, keepdims=True)
    acc[...] += dot(before, cols(w1, part, start, CH), NT)
    put_cols(g1, part, start, dot(normed_t[...], before).astype(BF))


def first_norm_back(acc, hat, scale, vectors, grad_low, small):
    sums = [0.0, 0.0]
    for r in range(0, WIN, ROWS):
        here = pl.ds(r, ROWS)
        grad = acc[here, :].astype(BF).astype(F32)
        value, gain, shift = norm_back(grad, hat[here, :], scale[here, 0:1], vectors[0:1, :])
        hat[here, :] = value
        grad_low[here, :] = value.astype(BF)
        sums = [a + b for a, b in zip(sums, (gain, shift))]
    for k in range(2):
        put_vector(small, k, sums[k])


def out_back(grad_low, context_t, wo, go, grad_context_t):
    for r in range(0, WIN, ROWS):
        here = pl.ds(r, ROWS)
        low = grad_low[here, :]
        value = 0.0
        for part in range(HALF):
            value = value + dot(cols(wo, part, 0, HD), low[:, part * HD : (part + 1) * HD], NT)
        grad_context_t[:, here] = value.astype(BF)
    for part in range(HALF):
        low = grad_low[:, pl.ds(part * HD, HD)]
        put_cols(go, part, 0, dot(context_t[...], low).astype(BF))


def attend_back_pair(part, g, mixed_t, mixed_n, attend, context_t, grad_context_t, scores, grad_mixed_t, small):
    values = mixed_n[part, :, pl.ds(g * 256 + 128, 128)]
    turn = lax.broadcasted_iota(jnp.int32, (TILE, TILE), 0) + lax.broadcasted_iota(
        jnp.int32, (TILE, TILE), 1
    )
    turn = jnp.where(turn == TILE - 1, 1.0, 0.0).astype(BF)
    for e in range(2):
        row = g * PC + e * HEAD
        h = part * (H // HALF) + g * 2 + e
        place = pl.ds(pl.multiple_of(h * HEAD, HEAD), HEAD)
        grad_c = grad_context_t[place, :]
        inner = jnp.sum(
            grad_c.astype(F32) * context_t[place, :].astype(F32), axis=0, keepdims=True
        )
        scores[...] = dot(values, pad_head(grad_c, e))
        tiles = [0.0] * 7
        for i in range(WIN // TILE):
            here = pl.ds(i * TILE, TILE)
            ds = attend[h, :, here].astype(F32) * (scores[:, here] - inner[:, i * TILE : (i + 1) * TILE])
            for j in range(WIN // TILE):
                d = i - j + 3
                tiles[d] = tiles[d] + ds[j * TILE : (j + 1) * TILE, :]
            scores[:, here] = ds
        low = scores[...].astype(BF)
        key = mixed_t[part, pl.ds(row + 128, HEAD), :]
        query = mixed_t[part, pl.ds(row, HEAD), :]
        gq = dot(key, low) * (HEAD**-0.5)
        gk = dot(query, low, NT)
        gv = dot(grad_c, attend[h], NT)
        grad_mixed_t[part, pl.ds(row, HEAD), :] = gq.astype(BF)
        grad_mixed_t[part, pl.ds(row + 128, HEAD), :] = gk.astype(BF)
        grad_mixed_t[part, pl.ds(row + 256, HEAD), :] = gv.astype(BF)
        blocks = [0.0] * 8
        turned = dot(turn, jnp.concatenate([t.astype(BF) for t in tiles], axis=1))
        for d in range(7):
            wide = turned[:, d * TILE : (d + 1) * TILE]
            wide = jnp.concatenate([wide, jnp.zeros((TILE, TILE), F32)], axis=1)
            wide = pltpu.roll(wide, 0, 1, stride=1, stride_axis=0)
            line = jnp.sum(wide, axis=0, keepdims=True)
            blocks[d] = blocks[d] + line[:, :TILE]
            blocks[d + 1] = blocks[d + 1] + line[:, TILE:]
        small[pl.ds(h, 1), :] = jnp.concatenate(blocks[:4], axis=1)
        small[pl.ds(H + h, 1), :] = jnp.concatenate(blocks[4:], axis=1)


def project_back(part, g, tok_t, grad_mixed_t, gi):
    value = dot(tok_t[...], grad_mixed_t[part, pl.ds(g * PC, PC), :], NT)
    put_cols(gi, part, g * PC, value.astype(BF))


def input_back(grad_mixed_t, wi, hat):
    for r in range(0, WIN, ROWS):
        here = pl.ds(r, ROWS)
        value = 0.0
        for part in range(HALF):
            value = value + dot(cols(wi, part, 0, 3 * HD), grad_mixed_t[part, :, here])
        hat[here, :] = hat[here, :] + value.T


MESH = pl.DeviceIdType.MESH
N_SEMS = 256
WI, WO, W1, W2, GI_ALL = range(5)
WI_A, WI_B, WO_B, W1_A, W1_B, W2_A, W2_B = range(7)
GATHER = {
    WI_A: (WI, 0, 768, "x"),
    WI_B: (WI, 768, 384, "y"),
    WO_B: (WO, 0, 384, "y"),
    W1_A: (W1, 0, 512, "x"),
    W1_B: (W1, 512, 1024, "y"),
    W2_A: (W2, 0, 1024, "x"),
    W2_B: (W2, 1024, 512, "y"),
}
G2 = range(0, 3)
G1 = range(3, 6)
GO = 6
GI = range(7, 11)
SMALL = 11
SCATTER = {
    G2[0]: (W2, 0, 512, "x"),
    G1[0]: (W1, 0, 512, "y"),
    G2[1]: (W2, 512, 512, "x"),
    G1[1]: (W1, 512, 512, "y"),
    G2[2]: (W2, 1024, 512, "x"),
    G1[2]: (W1, 1024, 512, "y"),
    GO: (WO, 0, 384, "x"),
    GI[0]: (GI_ALL, 0, 384, "y"),
    GI[1]: (GI_ALL, 384, 384, "x"),
    GI[2]: (GI_ALL, 768, 256, "y"),
    GI[3]: (GI_ALL, 1024, 128, "x"),
}


def scatter_buffers(depth, rows):
    out = {}
    for name, (_, _, width, first) in SCATTER.items():
        second = (depth, 2, rows, width) if first == "y" else (2, depth, rows, width)
        out[name] = (
            pltpu.VMEM((2, depth, 2, rows, width), BF),
            pltpu.VMEM(second, BF),
            pltpu.VMEM((depth, rows, width), BF),
            pltpu.VMEM((depth, rows, width), BF),
        )
    return out


class Exchange:
    def __init__(self, depth, send_sem, recv_sem):
        row = lax.axis_index("dp")
        y = lax.axis_index("mp")
        c, x, z = row % 2, (row // 2) % 2, row // 4
        self.depth = depth
        self.c, self.x, self.y, self.z = c, x, y, z
        self.c1_, self.x1, self.y1 = 1 - c, 1 - x, 1 - y
        self.up = [(z + k) % depth for k in range(depth)]
        self.down = [(z + depth - k) % depth for k in range(depth)]
        self.peers = {
            ("c", 1): ((z * 2 + x) * 2 + self.c1_, y),
            ("x", 1): ((z * 2 + self.x1) * 2 + c, y),
            ("y", 1): (row, self.y1),
        }
        for k in range(1, depth):
            self.peers["z", k] = ((self.up[k] * 2 + x) * 2 + c, y)
        self.around = dict(self.peers)
        half = self.half = depth // 2
        near = z // half * half
        self.starts = (half - near, near)
        self.goal, self.origin = {}, {}
        for g in range(2):
            for j in range(g, half):
                self.goal[g, j] = self.starts[g] + (z + j) % half
                self.origin[g, j] = self.starts[g] + (z + half - j) % half
                self.peers[g, j] = ((self.goal[g, j] * 2 + x) * 2 + c, y)
        self.send_sem, self.recv_sem = send_sem, recv_sem
        self.keys, self.flying = {}, []

    def greet(self):
        barrier = pltpu.get_barrier_semaphore()
        for peer in self.around.values():
            pl.semaphore_signal(barrier, inc=1, device_id=peer, device_id_type=MESH)
        pl.semaphore_wait(barrier, len(self.around))

    def copy(self, key, src, dst, axis, step=1):
        k = self.keys.setdefault(key, len(self.keys))
        return pltpu.make_async_remote_copy(
            src_ref=src,
            dst_ref=dst,
            send_sem=self.send_sem.at[k],
            recv_sem=self.recv_sem.at[k],
            device_id=self.peers[axis, step],
            device_id_type=MESH,
        )

    def send(self, key, src, dst, axis, step=1):
        dst = dst or src
        self.copy(key, src(), dst(), axis, step).start()
        self.flying.append((key, src, dst, axis, step))

    def recv(self, key, dst, axis, step=1):
        self.copy(key, dst, dst, axis, step).wait_recv()

    def land(self):
        for key, src, dst, axis, step in self.flying:
            self.copy(key, src(), dst(), axis, step).wait_send()
        self.flying = []


class Quiet:
    def __getattr__(self, name):
        return None


class Gather(Exchange):
    def use(self, refs):
        self.refs = refs

    def at(self, s, y, z, x, c):
        name, start, width, _ = GATHER[s]
        return self.refs[name].at[y, z, x, c, :, pl.ds(start, width)]

    def begin(self, s):
        for k in range(1, self.depth):
            self.send(
                (s, 0, k), lambda: self.at(s, self.y, self.z, self.x, self.c), None, "z", k
            )
        self.across(s, 0)

    def across(self, s, k):
        self.send(
            (s, 1, k),
            lambda: self.at(s, self.y, self.down[k], self.x, self.c),
            None,
            GATHER[s][3],
        )

    def zd(self, s, k):
        self.recv((s, 0, k), self.at(s, self.y, self.down[k], self.x, self.c), "z", k)
        self.across(s, k)

    def second(self, s):
        return "y" if GATHER[s][3] == "x" else "x"

    def pd(self, s, k):
        z, every = self.down[k], slice(None)
        if GATHER[s][3] == "x":
            piece = self.at(s, self.y, z, self.x1, self.c)
        else:
            piece = self.at(s, self.y1, z, self.x, self.c)
        self.recv((s, 1, k), piece, GATHER[s][3])

        def pair():
            if GATHER[s][3] == "x":
                return self.at(s, self.y, self.down[k], every, self.c)
            return self.at(s, every, self.down[k], self.x, self.c)

        self.send((s, 2, k), pair, None, self.second(s))

    def parts(self, s, c):
        every = slice(None)
        if GATHER[s][3] == "x":
            return self.at(s, self.y, every, every, c), self.at(s, self.y1, every, every, c)
        return self.at(s, every, every, self.x, c), self.at(s, every, every, self.x1, c)

    def c1(self, s):
        self.send((s, 3), lambda: self.parts(s, self.c)[0], None, "c")

    def qd(self, s):
        for k in range(self.depth):
            z, every = self.down[k], slice(None)
            if GATHER[s][3] == "x":
                pair = self.at(s, self.y1, z, every, self.c)
            else:
                pair = self.at(s, every, z, self.x1, self.c)
            self.recv((s, 2, k), pair, self.second(s))
        self.send((s, 4), lambda: self.parts(s, self.c)[1], None, "c")

    def f1(self, s):
        self.recv((s, 3), self.parts(s, self.c1_)[0], "c")

    def f2(self, s):
        self.recv((s, 4), self.parts(s, self.c1_)[1], "c")


class Scatter(Exchange):
    def use(self, refs, buffers, finish):
        self.refs, self.buffers, self.finish = refs, buffers, finish

    def at(self, s, y, z, x, c):
        name, start, width, _ = SCATTER[s]
        return self.refs[name].at[y, z, x, c, :, pl.ds(start, width)]

    def group(self, g):
        return pl.ds(self.starts[g], self.half)

    def s0(self, s):
        every = slice(None)
        self.send(
            (s, 0),
            lambda: self.at(s, every, every, every, self.c1_),
            lambda: self.buffers[s][0],
            "c",
        )

    def s1(self, s, g):
        every = slice(None)
        if g == 0:
            self.recv((s, 0), self.buffers[s][0], "c")
        own = self.at(s, every, self.group(g), every, self.c)
        own[...] = own[...] + self.buffers[s][0][:, self.group(g)]

        def away():
            if SCATTER[s][3] == "y":
                return self.at(s, self.y1, self.group(g), every, self.c)
            return self.at(s, every, self.group(g), self.x1, self.c)

        self.send((s, 1, g), away, lambda: self.landing(s, g), SCATTER[s][3])

    def landing(self, s, g):
        if SCATTER[s][3] == "y":
            return self.buffers[s][1].at[self.group(g)]
        return self.buffers[s][1].at[:, self.group(g)]

    def s2(self, s, g):
        every = slice(None)
        first = SCATTER[s][3]
        self.recv((s, 1, g), self.landing(s, g), first)
        if first == "y":
            own = self.at(s, self.y, self.group(g), every, self.c)
        else:
            own = self.at(s, every, self.group(g), self.x, self.c)
        own[...] = own[...] + self.landing(s, g)[...]

        def away():
            if first == "y":
                return self.at(s, self.y, self.group(g), self.x1, self.c)
            return self.at(s, self.y1, self.group(g), self.x, self.c)

        self.send(
            (s, 2, g),
            away,
            lambda: self.buffers[s][2].at[self.group(g)],
            "x" if first == "y" else "y",
        )

    def s3(self, s, g):
        got = self.buffers[s][2].at[self.group(g)]
        self.recv((s, 2, g), got, "x" if SCATTER[s][3] == "y" else "y")
        own = self.at(s, self.y, self.group(g), self.x, self.c)
        own[...] = own[...] + got[...]
        for j in range(g, self.half):
            self.send(
                (s, 3, g, j),
                lambda j=j: self.at(s, self.y, self.goal[g, j], self.x, self.c),
                lambda: self.buffers[s][3].at[self.z],
                g,
                j,
            )

    def s4(self, s):
        got = self.buffers[s][3]
        total = self.at(s, self.y, self.z, self.x, self.c)[...].astype(F32)
        for g in range(2):
            for j in range(g, self.half):
                self.recv((s, 3, g, j), got.at[self.origin[g, j]], g, j)
        for g in range(2):
            for j in range(g, self.half):
                total = total + got[self.origin[g, j]].astype(F32)
        self.finish(self, s, total)


def layer_kernel(comm, dims, names, *refs):
    r = dict(zip(names, refs))
    r.update(refs[len(names)])
    k = type("Refs", (), r)
    counts, gate, vectors, hidden, small = k.counts, k.gate, k.vectors, k.hidden, k.small
    tok, tok_t, wi, wo, w1, w2 = k.tok, k.tok_t, k.wi, k.wo, k.w1, k.w2
    mixed_t, mixed_n, attend, scores = k.mixed_t, k.mixed_n, k.attend, k.scores
    context_t, hat, scale, normed, acc = k.context_t, k.hat, k.scale, k.normed, k.acc

    def local_copy(j, src, dst):
        copy = pltpu.make_async_copy(src, dst, k.sems.at[j])
        copy.start()
        return copy

    depth, rows = dims
    matrices = {WI: wi, WO: wo, W1: w1, W2: w2}
    if comm:
        ag = Gather(depth, k.send_sem, k.recv_sem)
        ag.use(matrices)
        rs = Scatter(depth, k.send_sem, k.recv_sem)
        rs.keys = ag.keys
        own, other = ag.y, ag.y1
    else:
        ag = rs = Quiet()
        own, other = 0, 1

    def do(*steps):
        if comm:
            for step, *which in steps:
                step(*which)

    def attention(bias, mask, pattern, stage_i, stage_o, stage_f):
        get_tok = local_copy(0, k.tok_in, tok)
        get_pattern = local_copy(1, k.pattern_in, pattern)
        if comm:
            y, z, x, c = ag.y, ag.z, ag.x, ag.c
            gets = [
                local_copy(
                    2 + kind,
                    k.wi_in.at[:, pl.ds(pl.multiple_of(kind * D + y * HD, 128), HD)],
                    stage_i.at[kind],
                )
                for kind in range(3)
            ]
            get_f = local_copy(5, k.wf_in, stage_f)
            get_o = local_copy(6, k.wo_in.at[:, pl.ds(pl.multiple_of(y * HD, 128), HD)], stage_o)
            ag.greet()
            for kind in range(3):
                gets[kind].wait()
            for g in range(PAIRS):
                for kind in range(3):
                    wi[y, z, x, c, :, pl.ds(g * PC + kind * 128, 128)] = stage_i[
                        kind, :, pl.ds(g * 128, 128)
                    ].astype(BF)
            for s in (WI_A, WI_B):
                ag.begin(s)
            get_o.wait()
            wo[y, z, x, c] = stage_o[...].astype(BF)
            get_f.wait()
            w1[y, z, x, c] = stage_f[0].astype(BF)
            w2[y, z, x, c] = stage_f[1].astype(BF)
            for s in GATHER:
                if s not in (WI_A, WI_B):
                    ag.begin(s)
        else:
            plain = [
                local_copy(2 + j, src, dst)
                for j, (src, dst) in enumerate(
                    ((k.wi_in, wi), (k.wo_in, wo), (k.w1_in, w1), (k.w2_in, w2))
                )
            ]
        get_tok.wait()
        tok_t[...] = tok[...].T
        get_pattern.wait()
        build_mask(counts, pattern, mask)
        build_bias(gate, k.table, bias)
        if not comm:
            for copy in plain:
                copy.wait()

        def one(part, g):
            project_mixed(part, g, tok, wi, mixed_t, mixed_n)
            attend_pair(part, g, mixed_t, mixed_n, bias, mask, scores, attend, context_t)

        do((ag.pd, WI_B, 0), (ag.pd, WI_A, 0), (ag.zd, WI_A, 1), (ag.zd, WI_A, 2), (ag.pd, WO_B, 0), (ag.pd, W1_A, 0), (ag.zd, WI_A, 3), (ag.pd, W1_B, 0), (ag.pd, W2_A, 0), (ag.pd, W2_B, 0), (ag.zd, WI_B, 1), (ag.zd, WI_B, 2), (ag.pd, WI_A, 1), (ag.zd, WI_B, 3), (ag.zd, WO_B, 1), (ag.pd, WI_A, 2), (ag.zd, WO_B, 2), (ag.zd, WO_B, 3), (ag.pd, WI_A, 3), (ag.c1, WI_A), (ag.zd, W1_A, 1), (ag.zd, W1_A, 2), (ag.pd, WI_B, 1), (ag.pd, WI_B, 2), (ag.f1, WI_A))
        one(own, 0)
        do((ag.zd, W1_A, 3))
        one(own, 1)
        do((ag.pd, WI_B, 3), (ag.c1, WI_B), (ag.zd, W1_B, 1), (ag.pd, WO_B, 1), (ag.pd, W1_A, 1), (ag.pd, W1_A, 2), (ag.zd, W1_B, 2), (ag.pd, WO_B, 2), (ag.zd, W1_B, 3), (ag.pd, WO_B, 3), (ag.c1, WO_B), (ag.pd, W1_A, 3), (ag.c1, W1_A), (ag.qd, WI_B), (ag.zd, W2_A, 1), (ag.qd, WI_A), (ag.zd, W2_A, 2), (ag.pd, W1_B, 1), (ag.f2, WI_A))
        one(other, 0)
        do((ag.qd, WO_B))
        one(other, 1)
        do((ag.zd, W2_A, 3), (ag.pd, W2_A, 1), (ag.zd, W2_B, 1), (ag.f1, WI_B), (ag.f2, WI_B))
        one(own, 2)
        do((ag.pd, W1_B, 2), (ag.pd, W2_A, 2), (ag.zd, W2_B, 2), (ag.zd, W2_B, 3))
        one(other, 2)

    pl.run_scoped(
        attention,
        pltpu.VMEM((H, 7, TILE, TILE), F32),
        pltpu.VMEM((WIN, WIN), F32),
        pltpu.VMEM((WIN, WIN), jnp.int32),
        pltpu.VMEM((3, rows, HD), F32),
        pltpu.VMEM((rows, HD), F32),
        pltpu.VMEM((2, rows, HF), F32),
    )

    def feed(active, slope, normed_t, grad, grad_t):
        get_cot = local_copy(0, k.cot_in, grad)

        if comm:
            rs.use(dict(matrices), k.buffers, None)

        def back(part, c):
            hidden_back(part, c, grad, grad_t, normed_t, w1, w2, w1, w2, active, slope, acc, small)

        do((ag.pd, W1_B, 3), (ag.c1, W1_B), (ag.f1, WO_B), (ag.f2, WO_B))
        out_project(tok, context_t, wo, vectors, hat, scale, normed, normed_t)
        do((ag.qd, W1_A), (ag.pd, W2_A, 3), (ag.c1, W2_A), (ag.f1, W1_A), (ag.f2, W1_A))
        hidden_step(0, 0, normed, w1, hidden, active, slope)
        hidden_step(1, 0, normed, w1, hidden, active, slope)
        do((ag.pd, W2_B, 1), (ag.qd, W1_B), (ag.pd, W2_B, 2), (ag.pd, W2_B, 3), (ag.c1, W2_B), (ag.f1, W1_B), (ag.f2, W1_B))
        hidden_step(0, 1, normed, w1, hidden, active, slope)
        hidden_step(1, 1, normed, w1, hidden, active, slope)
        hidden_step(0, 2, normed, w1, hidden, active, slope)
        hidden_step(1, 2, normed, w1, hidden, active, slope)
        do((ag.qd, W2_A), (ag.qd, W2_B), (ag.f1, W2_A), (ag.f2, W2_A))
        result_step(0, active, w2, acc)
        result_step(1, active, w2, acc)
        do((ag.f1, W2_B), (ag.f2, W2_B))
        result_step(2, active, w2, acc)
        get_cot.wait()
        second_norm(acc, normed, grad, vectors, k.low, grad, grad_t, small)
        put_low = local_copy(7, k.low, k.low_out)
        if comm:
            ag.land()
        back(0, 0)
        back(1, 0)
        do((rs.s0, G2[0]), (rs.s0, G1[0]))
        back(0, 1)
        back(1, 1)
        do((rs.s1, G2[0], 0), (rs.s1, G2[0], 1), (rs.s1, G1[0], 0), (rs.s1, G1[0], 1), (rs.s0, G2[1]), (rs.s0, G1[1]))
        back(0, 2)
        back(1, 2)
        do((rs.s1, G2[1], 0), (rs.s1, G2[1], 1), (rs.s2, G2[0], 0), (rs.s1, G1[1], 0), (rs.s2, G1[0], 0), (rs.s1, G1[1], 1), (rs.s0, G2[2]), (rs.s0, G1[2]))
        put_low.wait()

    pl.run_scoped(
        feed,
        pltpu.VMEM((HALF * NCH, WIN, CH), BF),
        pltpu.VMEM((HALF * NCH, WIN, CH), BF),
        pltpu.VMEM((D, WIN), BF),
        pltpu.VMEM((WIN, D), BF),
        pltpu.VMEM((D, WIN), BF),
    )

    def finish(net, s, total):
        name, start, width, _ = SCATTER[s]
        here = pl.ds(start, width)
        if name in (W1, W2):
            k.gf_out[0 if name == W1 else 1, :, here] = total
        else:
            box = k.box_i if name == GI_ALL else k.box_o
            box[net.y, :, here] = total.astype(BF)
            net.send((s, 5), lambda: box.at[net.y, :, here], None, "y")

    def s5(s):
        name, start, width, _ = SCATTER[s]
        box = k.box_i if name == GI_ALL else k.box_o
        rs.recv((s, 5), box.at[rs.y1, :, pl.ds(start, width)], "y")

    def m0():
        rs.send((SMALL, 0), lambda: small, lambda: k.line.at[0], "c")

    def m1():
        rs.recv((SMALL, 0), k.line.at[0], "c")
        k.line[1] = small[...] + k.line[0]
        rs.send((SMALL, 1), lambda: k.line.at[1], lambda: k.line.at[2], "y")

    def m2():
        rs.recv((SMALL, 1), k.line.at[2], "y")
        k.line[3] = k.line[1] + k.line[2]
        rs.send((SMALL, 2), lambda: k.line.at[3], lambda: k.line.at[4], "x")

    def m3():
        rs.recv((SMALL, 2), k.line.at[4], "x")
        k.lines[rs.z] = k.line[3] + k.line[4]
        for j in range(1, depth):
            rs.send((SMALL, 3, j), lambda: k.lines.at[rs.z], None, "z", j)

    def m4():
        for j in range(1, depth):
            rs.recv((SMALL, 3, j), k.lines.at[rs.down[j]], "z", j)
        total = k.lines[0]
        for j in range(1, depth):
            total = total + k.lines[j]
        k.small_out[...] = total

    def last(grad_mixed_t, grad_context_t, gi):
        grad_low = normed
        if comm:
            rs.use({**matrices, GI_ALL: gi}, k.buffers, finish)

        def one(part, g):
            attend_back_pair(
                part, g, mixed_t, mixed_n, attend, context_t, grad_context_t, scores, grad_mixed_t, small
            )
            project_back(part, g, tok_t, grad_mixed_t, gi)

        first_norm_back(acc, hat, scale, vectors, grad_low, small)
        out_back(grad_low, context_t, wo, wo, grad_context_t)
        do((rs.s2, G2[0], 1), (rs.s1, G2[2], 0), (rs.s2, G1[0], 1), (rs.s1, G2[2], 1), (rs.s0, GO))
        one(0, 0)
        do((rs.s3, G2[0], 0), (rs.s1, G1[2], 0), (rs.s1, G1[2], 1), (rs.s2, G2[1], 0), (rs.s1, GO, 0), (rs.s1, GO, 1))
        one(1, 0)
        do((rs.s0, GI[0]), (rs.s2, G1[1], 0))
        one(0, 1)
        do((rs.s2, G2[1], 1), (rs.s1, GI[0], 0), (rs.s1, GI[0], 1))
        one(1, 1)
        do((rs.s3, G1[0], 0), (rs.s2, G1[1], 1), (rs.s0, GI[1]))
        one(0, 2)
        do((rs.s3, G2[0], 1))
        one(1, 2)
        do((rs.s2, G2[2], 0), (rs.s1, GI[1], 0), (rs.s3, G1[0], 1), (rs.s1, GI[1], 1), (rs.s0, GI[2]), (rs.s0, GI[3]), (rs.s2, G1[2], 0), (rs.s4, G2[0]), (m0,))
        input_back(grad_mixed_t, wi, hat)
        put_grad = local_copy(0, hat, k.grad_out)
        do((rs.s4, G1[0]), (rs.s2, G2[2], 1), (rs.s1, GI[2], 0), (rs.s1, GI[2], 1), (rs.s2, G1[2], 1), (rs.s1, GI[3], 0), (rs.s1, GI[3], 1), (m1,), (rs.s3, G2[1], 0), (rs.s2, GO, 0), (rs.s3, G2[1], 1), (rs.s2, GO, 1), (rs.s2, GI[0], 0), (rs.s3, G1[1], 0), (rs.s4, G2[1]), (rs.s3, G1[1], 1), (rs.s2, GI[0], 1), (rs.s3, G2[2], 0), (rs.s2, GI[1], 0), (rs.s4, G1[1]), (rs.s3, G2[2], 1), (rs.s2, GI[1], 1), (rs.s2, GI[2], 0), (rs.s3, G1[2], 0), (rs.s4, G2[2]), (rs.s2, GI[2], 1), (rs.s3, G1[2], 1), (m2,), (rs.s2, GI[3], 0), (rs.s3, GO, 0), (rs.s2, GI[3], 1), (rs.s3, GO, 1), (rs.s3, GI[0], 0), (rs.s4, G1[2]), (rs.s3, GI[1], 0), (rs.s3, GI[0], 1), (rs.s3, GI[2], 0), (rs.s3, GI[1], 1), (rs.s4, GO), (rs.s3, GI[3], 0), (rs.s3, GI[2], 1), (rs.s3, GI[3], 1), (m3,), (s5, GO), (rs.s4, GI[0]), (rs.s4, GI[1]), (s5, GI[0]), (rs.s4, GI[2]), (rs.s4, GI[3]), (s5, GI[1]), (s5, GI[2]), (s5, GI[3]), (m4,))
        if comm:
            k.gi_out[...] = k.box_i[...]
            k.go_out[...] = k.box_o[...]
            rs.land()
        else:
            k.small_out[...] = small[...]
            outs = [
                local_copy(1 + j, src, dst)
                for j, (src, dst) in enumerate(
                    ((gi, k.gi_out), (wo, k.go_out), (w1, k.g1_out), (w2, k.g2_out))
                )
            ]
            for copy in outs:
                copy.wait()
        put_grad.wait()

    pl.run_scoped(
        last,
        pltpu.VMEM((HALF, 3 * HD, WIN), BF),
        pltpu.VMEM((D, WIN), BF),
        pltpu.VMEM(wi.shape, BF),
    )


IN_NAMES = (
    "counts",
    "tok_in",
    "cot_in",
    "pattern_in",
    "gate",
    "vectors",
    "hidden",
    "wi_in",
    "wo_in",
    "w1_in",
    "w2_in",
)
OUT_NAMES_PLAIN = ("low_out", "grad_out", "small_out", "gi_out", "go_out", "g1_out", "g2_out")
OUT_NAMES = ("low_out", "grad_out", "small_out", "gi_out", "go_out", "gf_out")


def layer_call(comm, depth, rows, counts, tok, cot, pattern, gate, vectors, hidden, *weights):
    vmem = pl.BlockSpec(memory_space=pltpu.VMEM)
    hbm = pl.BlockSpec(memory_space=pl.ANY)
    lead = (HALF, depth, 2, 2, rows) if comm else (HALF, 1, 1, 1, D)
    shapes = [lead + (n,) for n in (3 * HD, HD, HF, HF)]
    scratch = dict(
        wi=pltpu.VMEM(shapes[0], BF),
        wo=pltpu.VMEM(shapes[1], BF),
        w1=pltpu.VMEM(shapes[2], BF),
        w2=pltpu.VMEM(shapes[3], BF),
        tok=pltpu.VMEM((WIN, D), BF),
        low=pltpu.VMEM((WIN, D), BF),
        tok_t=pltpu.VMEM((D, WIN), BF),
        mixed_t=pltpu.VMEM((HALF, 3 * HD, WIN), BF),
        mixed_n=pltpu.VMEM((HALF, WIN, 2 * HD), BF),
        attend=pltpu.VMEM((H, WIN, WIN), BF),
        scores=pltpu.VMEM((WIN, WIN), F32),
        context_t=pltpu.VMEM((D, WIN), BF),
        hat=pltpu.VMEM((WIN, D), F32),
        scale=pltpu.VMEM((WIN, 128), F32),
        normed=pltpu.VMEM((WIN, D), BF),
        acc=pltpu.VMEM((WIN, D), F32),
        table=pltpu.VMEM((H, 2 * WIN), F32),
        small=pltpu.VMEM((R_ALL, 512), F32),
        sems=pltpu.SemaphoreType.DMA((8,)),
    )
    outs = [
        jax.ShapeDtypeStruct((WIN, D), BF),
        jax.ShapeDtypeStruct((WIN, D), F32),
        jax.ShapeDtypeStruct((R_ALL, 512), F32),
    ]
    names = IN_NAMES
    if comm:
        outs += [
            jax.ShapeDtypeStruct((HALF, rows, 3 * HD), BF),
            jax.ShapeDtypeStruct((HALF, rows, HD), BF),
            jax.ShapeDtypeStruct((2, rows, HF), F32),
        ]
        out_specs = [hbm, hbm, vmem, vmem, vmem, vmem]
        scratch.update(
            box_i=pltpu.VMEM((HALF, rows, 3 * HD), BF),
            box_o=pltpu.VMEM((HALF, rows, HD), BF),
            line=pltpu.VMEM((5, R_ALL, 512), F32),
            lines=pltpu.VMEM((depth, R_ALL, 512), F32),
            buffers=scatter_buffers(depth, rows),
            send_sem=pltpu.SemaphoreType.DMA((N_SEMS,)),
            recv_sem=pltpu.SemaphoreType.DMA((N_SEMS,)),
        )
        names = names[:9] + ("wf_in",)
        params = dict(collective_id=0, has_side_effects=True)
    else:
        weights = [w.reshape(s) for w, s in zip(weights, shapes)]
        outs += [jax.ShapeDtypeStruct(s, BF) for s in shapes]
        out_specs = [hbm, hbm, vmem] + [hbm] * 4
        params = {}
    names = names + (OUT_NAMES if comm else OUT_NAMES_PLAIN)
    return pl.pallas_call(
        functools.partial(layer_kernel, comm, (depth, rows), names),
        out_shape=outs,
        in_specs=[pl.BlockSpec(memory_space=pltpu.SMEM)]
        + [hbm] * 3
        + [vmem] * 3
        + [hbm] * len(weights),
        out_specs=out_specs,
        scratch_shapes=[scratch],
        compiler_params=pltpu.CompilerParams(vmem_limit_bytes=62 * 2**20, **params),
        cost_estimate=pl.CostEstimate(
            flops=25 * 10**9, bytes_accessed=40 * 2**20, transcendentals=10**7
        ),
        name="layer",
    )(counts, tok, cot, pattern, gate, vectors, hidden, *weights)


def collect(w, width):
    return w.reshape(D, HALF, width).transpose(1, 0, 2)


def local(
    tokens,
    cotangent,
    seq_counts,
    pattern,
    project_in,
    project_in_first,
    project_in_second,
    project_out,
    project_out_first,
    project_out_second,
    feed_forward,
    feed_forward_first,
    feed_forward_second,
    gate_logits,
    gate_logits_first,
    gate_logits_second,
    norm_vectors,
    norm_vectors_first,
    norm_vectors_second,
    hidden_bias,
    hidden_bias_first,
    hidden_bias_second,
):
    rows = project_in.shape[0]
    groups, halves = lax.axis_size("dp"), lax.axis_size("mp")
    comm = halves == HALF and groups % 8 == 0 and rows % 16 == 0
    shared = (
        seq_counts,
        tokens,
        cotangent,
        pattern,
        gate_logits,
        norm_vectors,
        hidden_bias.reshape(HALF * NCH, CH),
    )
    if comm:
        layer_out, input_grad, small, gi, go, sum_pair = layer_call(
            True, groups // 4, rows, *shared, project_in, project_out, feed_forward
        )
        gi = gi.reshape(HALF, rows, PAIRS, 3, 128).transpose(1, 3, 0, 2, 4).reshape(rows, 3 * D)
        sum_in = gi.astype(F32)
        sum_out = go.transpose(1, 0, 2).reshape(rows, D).astype(F32)
    else:
        whole_in = lax.all_gather(project_in.astype(BF), "dp", axis=0, tiled=True)
        whole_out = lax.all_gather(project_out.astype(BF), "dp", axis=0, tiled=True)
        pair = lax.all_gather(feed_forward.astype(BF), "dp", axis=1, tiled=True)
        pair = lax.all_gather(pair, "mp", axis=2, tiled=True)
        wi = whole_in.reshape(D, 3, HALF, PAIRS, 128).transpose(2, 0, 3, 1, 4)
        wi = wi.reshape(HALF, D, 3 * HD)
        layer_out, input_grad, small, gi, go, g1, g2 = layer_call(
            False,
            1,
            D,
            *shared,
            wi,
            collect(whole_out, HD),
            collect(pair[0], HF),
            collect(pair[1], HF),
        )
        gi = gi.reshape(HALF, D, PAIRS, 3, 128).transpose(1, 3, 0, 2, 4).reshape(D, 3 * D)
        go = go.reshape(HALF, D, HD).transpose(1, 0, 2).reshape(D, D)
        gf = jnp.stack([g.reshape(HALF, D, HF).transpose(1, 0, 2).reshape(D, FF) for g in (g1, g2)])
        sum_in = lax.psum_scatter(gi, "dp", scatter_dimension=0, tiled=True)
        sum_in = lax.psum(sum_in.astype(F32), "mp")
        sum_out = lax.psum_scatter(go, "dp", scatter_dimension=0, tiled=True)
        sum_out = lax.psum(sum_out.astype(F32), "mp")
        sum_pair = lax.psum_scatter(gf, "dp", scatter_dimension=1, tiled=True)
        sum_pair = lax.psum_scatter(sum_pair, "mp", scatter_dimension=2, tiled=True).astype(F32)
        small = lax.psum(small, ("dp", "mp"))
    sum_gate = jnp.concatenate([small[:H], small[H : 2 * H]], axis=1)[:, : 2 * WIN - 1]
    sum_gate = sum_gate * jax.nn.sigmoid(-gate_logits)
    sum_vectors = jnp.concatenate(
        [small[R_VEC : R_VEC + 5], small[R_VEC + 5 : R_VEC + 10, :256]], axis=1
    )
    sum_bias = small[R_HID:].reshape(FF)
    outs = [layer_out, input_grad]
    for weight, first, second, grad, rate in (
        (project_in, project_in_first, project_in_second, sum_in, RATES[0]),
        (project_out, project_out_first, project_out_second, sum_out, RATES[1]),
        (feed_forward, feed_forward_first, feed_forward_second, sum_pair, RATES[2]),
        (gate_logits, gate_logits_first, gate_logits_second, sum_gate, RATES[3]),
        (norm_vectors, norm_vectors_first, norm_vectors_second, sum_vectors, RATES[4]),
        (hidden_bias, hidden_bias_first, hidden_bias_second, sum_bias, RATES[5]),
    ):
        outs.extend(adam_step(weight, first, second, grad, rate))
    return tuple(outs)


def solution(mesh):
    rows, whole = P(("dp", "mp"), None), P()
    split, pair = P("dp", None), P(None, "dp", "mp")
    return jax.shard_map(
        local,
        mesh=mesh,
        in_specs=(rows, rows, rows, whole) + (split,) * 6 + (pair,) * 3 + (whole,) * 9,
        out_specs=(rows, rows) + (split,) * 6 + (pair,) * 3 + (whole,) * 9,
        check_vma=False,
    )
```

```python
import functools
import math

import jax
import jax.numpy as jnp
from jax import lax
from jax.experimental import pallas as pl
from jax.experimental.pallas import tpu as pltpu
from jax.sharding import PartitionSpec as P

D = 768
H = 12
HEAD = 64
FF = 3072
TILE = 128
WIN = 512
STEP = 10
HALF = 2
HD = D // HALF
HF = FF // HALF
CH = 512
NCH = HF // CH
PAIRS = HD // 128
PC = 3 * 128

NORM_EPS = 1e-12
BETA_ONE = 0.9
BETA_TWO = 0.999
ADAM_EPS = 1e-08
DECAY = 0.01
MASKED = -1e30
RATES = (0.03, 0.25, 0.03, 1.0, 0.2, 0.2)

F32 = jnp.float32
BF = jnp.bfloat16
NN = ((1,), (0,))
NT = ((1,), (1,))
R_VEC, R_HID, R_ALL = 24, 34, 40


def dot(a, b, dims=NN):
    return lax.dot_general(a, b, (dims, ((), ())), preferred_element_type=F32)


def adam_step(weight, first, second, grad, rate):
    first = BETA_ONE * first + (1.0 - BETA_ONE) * grad
    second = BETA_TWO * second + (1.0 - BETA_TWO) * grad * grad
    update = first / (1.0 - BETA_ONE**STEP) / (jnp.sqrt(second / (1.0 - BETA_TWO**STEP)) + ADAM_EPS)
    return (weight - rate * (update + DECAY * weight), first, second)


def cols(ref, part, start, size):
    block = ref[part, :, :, :, :, pl.ds(start, size)]
    return block.reshape(D, size)


def put_cols(ref, part, start, value):
    shape = ref.shape[1:5] + (value.shape[1],)
    ref[part, :, :, :, :, pl.ds(start, value.shape[1])] = value.reshape(shape)


def build_mask(counts, pattern, mask):
    two, three, four = counts[0, 1], counts[0, 2], counts[0, 3]
    after_four = 4 * four
    after_three = after_four + 3 * three
    after_two = after_three + 2 * two
    tiles = WIN // TILE
    begins = []
    for tile in range(tiles):
        in_three = after_four + jnp.where(tile - after_four >= 3, 3, 0)
        in_two = after_three + jnp.where(tile - after_three >= 2, 2, 0)
        begin = jnp.where(
            tile < after_four,
            0,
            jnp.where(tile < after_three, in_three, jnp.where(tile < after_two, in_two, tile)),
        )
        begins.append(begin)
    starts = [
        [jnp.where(begins[tile] == b, 1.0, 0.0) for b in range(tile + 1)] for tile in range(tiles)
    ]
    for i in range(tiles):
        for j in range(tiles):
            allowed = jnp.zeros((TILE, TILE), F32)
            for b in range(min(i, j) + 1):
                block = pattern[pl.ds((i - b) * TILE, TILE), pl.ds((j - b) * TILE, TILE)]
                allowed = allowed + block.astype(F32) * (starts[i][b] * starts[j][b])
            allowed = jnp.where(allowed > 0.5, 0.0, MASKED)
            mask[pl.ds(j * TILE, TILE), pl.ds(i * TILE, TILE)] = allowed.T


def build_bias(gate, table, bias):
    x = gate[...]
    x = jnp.minimum(x, 0.0) - jnp.log(1.0 + jnp.exp(-jnp.abs(x)))
    table[:, pl.ds(0, x.shape[1])] = x

    def one(h, _):
        row = table[pl.ds(h, 1), :]
        for d in range(7):
            part = jnp.broadcast_to(row[:, d * TILE : d * TILE + 2 * TILE], (TILE, 2 * TILE))
            bias[h, d] = pltpu.roll(part, TILE + 1, 1, stride=1, stride_axis=0)[:, :TILE]
        return 0

    lax.fori_loop(0, H, one, 0)


def project_mixed(part, g, tok, wi, mixed_t, mixed_n):
    value = dot(tok[...], cols(wi, part, g * PC, PC)).astype(BF)
    mixed_n[part, :, pl.ds(g * 256, 256)] = value[:, 128:]
    query = value[:, :128] * jnp.asarray(HEAD**-0.5, BF)
    mixed_t[part, pl.ds(g * PC, PC), :] = jnp.concatenate([query.T, value[:, 128:].T], axis=0)


def pad_head(value, e):
    zero = jnp.zeros_like(value)
    return jnp.concatenate([value, zero] if e == 0 else [zero, value], axis=0)


def attend_pair(part, g, mixed_t, mixed_n, bias, mask, scores, attend, context_t):
    keys = mixed_n[part, :, pl.ds(g * 256, 128)]
    for e in range(2):
        row = g * PC + e * HEAD
        h = part * (H // HALF) + g * 2 + e
        query = pad_head(mixed_t[part, pl.ds(row, HEAD), :], e)
        scores[...] = dot(keys, query)
        for i in range(WIN // TILE):
            here = pl.ds(i * TILE, TILE)
            table = jnp.concatenate([bias[h, i - j + 3] for j in range(WIN // TILE)], axis=0)
            s = scores[:, here] + (table + mask[:, here])
            top = jnp.max(s, axis=0, keepdims=True)
            s = jnp.exp(s - top)
            total = jnp.sum(s, axis=0, keepdims=True)
            attend[h, :, here] = (s * (1.0 / total)).astype(BF)
        values = mixed_t[part, pl.ds(row + 256, HEAD), :]
        out = dot(values, attend[h])
        context_t[pl.ds(pl.multiple_of(h * HEAD, HEAD), HEAD), :] = out.astype(BF)


def norm_of(value):
    mean = jnp.mean(value, axis=-1, keepdims=True)
    center = value - mean
    spread = jnp.mean(center * center, axis=-1, keepdims=True)
    scale = lax.rsqrt(spread + NORM_EPS)
    return center * scale, scale


def norm_back(grad, hat, scale, gain):
    g = grad * gain
    first = jnp.mean(g, axis=-1, keepdims=True)
    second = jnp.mean(g * hat, axis=-1, keepdims=True)
    return (
        scale * (g - first - hat * second),
        jnp.sum(grad * hat, axis=0, keepdims=True),
        jnp.sum(grad, axis=0, keepdims=True),
    )


ROWS = 256


def out_project(tok, context_t, wo, vectors, hat, scale, normed, normed_t):
    for r in range(0, WIN, ROWS):
        here = pl.ds(r, ROWS)
        context = context_t[:, here].T
        branch = jnp.concatenate(
            [dot(context, cols(wo, part, 0, HD)) for part in range(HALF)], axis=1
        )
        h, s = norm_of(tok[here, :].astype(F32) + branch)
        hat[here, :] = h
        scale[here, :] = jnp.broadcast_to(s, (ROWS, 128))
        low = (h * vectors[0:1, :] + vectors[1:2, :]).astype(BF)
        normed[here, :] = low
        normed_t[:, here] = low.T


def hidden_step(part, c, normed, w1, hidden, active, slope):
    j = part * NCH + c
    bias = [hidden[pl.ds(j * (CH // 128) + q, 1), :] for q in range(CH // 128)]
    before = dot(normed[...], cols(w1, part, c * CH, CH)) + jnp.concatenate(bias, axis=1)
    half = 0.5 + 0.5 * lax.erf(before * math.sqrt(0.5))
    active[j] = (before * half).astype(BF)
    bell = jnp.exp(-0.5 * before * before) * (1.0 / math.sqrt(2 * math.pi))
    slope[j] = (half + before * bell).astype(BF)


def result_step(c, active, w2, acc):
    value = 0.0
    for part in range(HALF):
        value = value + dot(active[part * NCH + c], cols(w2, part, c * CH, CH), NT)
    acc[...] = value if c == 0 else acc[...] + value


def second_norm(acc, normed, cot, vectors, low_out, grad, grad_t, small):
    sums = [0.0, 0.0, 0.0]
    for r in range(0, WIN, ROWS):
        here = pl.ds(r, ROWS)
        total = normed[here, :].astype(F32) + acc[here, :] + vectors[4:5, :]
        hat, scale = norm_of(total)
        low_out[here, :] = (hat * vectors[2:3, :] + vectors[3:4, :]).astype(BF)
        value, gain, shift = norm_back(cot[here, :].astype(F32), hat, scale, vectors[2:3, :])
        acc[here, :] = value
        low = value.astype(BF)
        grad[here, :] = low
        grad_t[:, here] = low.T
        sums = [a + b for a, b in zip(sums, (gain, shift, jnp.sum(value, axis=0, keepdims=True)))]
    for k in range(3):
        put_vector(small, 2 + k, sums[k])


def put_vector(small, k, value):
    small[pl.ds(R_VEC + k, 1), :] = value[:, :512]
    small[pl.ds(R_VEC + 5 + k, 1), :] = jnp.concatenate(
        [value[:, 512:], jnp.zeros((1, 256), F32)], axis=1
    )


def hidden_back(part, start, width, grad, grad_t, w2, active, slope, small):
    j, here = part * NCH + start // CH, pl.ds(start % CH, width)
    before = dot(grad[...], cols(w2, part, start, width)) * slope[j, :, here].astype(F32)
    before = before.astype(BF)
    slope[j, :, here] = before
    put_cols(w2, part, start, dot(grad_t[...], active[j, :, here]).astype(BF))
    small[pl.ds(R_HID + j, 1), here] = jnp.sum(before.astype(F32), axis=0, keepdims=True)


def hidden_back_up(part, start, width, normed_t, w1, slope, acc):
    before = slope[part * NCH + start // CH, :, pl.ds(start % CH, width)]
    acc[...] += dot(before, cols(w1, part, start, width), NT)
    put_cols(w1, part, start, dot(normed_t[...], before).astype(BF))


def first_norm_back(acc, hat, scale, vectors, grad_low, small):
    sums = [0.0, 0.0]
    for r in range(0, WIN, ROWS):
        here = pl.ds(r, ROWS)
        grad = acc[here, :].astype(BF).astype(F32)
        value, gain, shift = norm_back(grad, hat[here, :], scale[here, 0:1], vectors[0:1, :])
        hat[here, :] = value
        grad_low[here, :] = value.astype(BF)
        sums = [a + b for a, b in zip(sums, (gain, shift))]
    for k in range(2):
        put_vector(small, k, sums[k])


def out_back(grad_low, context_t, wo, go, grad_context_t):
    for r in range(0, WIN, ROWS):
        here = pl.ds(r, ROWS)
        low = grad_low[here, :]
        value = 0.0
        for part in range(HALF):
            value = value + dot(cols(wo, part, 0, HD), low[:, part * HD : (part + 1) * HD], NT)
        grad_context_t[:, here] = value.astype(BF)
    for part in range(HALF):
        low = grad_low[:, pl.ds(part * HD, HD)]
        put_cols(go, part, 0, dot(context_t[...], low).astype(BF))


def attend_back_pair(part, g, mixed_t, mixed_n, attend, context_t, grad_context_t, scores, grad_mixed_t, small):
    values = mixed_n[part, :, pl.ds(g * 256 + 128, 128)]
    turn = lax.broadcasted_iota(jnp.int32, (TILE, TILE), 0) + lax.broadcasted_iota(
        jnp.int32, (TILE, TILE), 1
    )
    turn = jnp.where(turn == TILE - 1, 1.0, 0.0).astype(BF)
    for e in range(2):
        row = g * PC + e * HEAD
        h = part * (H // HALF) + g * 2 + e
        place = pl.ds(pl.multiple_of(h * HEAD, HEAD), HEAD)
        grad_c = grad_context_t[place, :]
        inner = jnp.sum(
            grad_c.astype(F32) * context_t[place, :].astype(F32), axis=0, keepdims=True
        )
        scores[...] = dot(values, pad_head(grad_c, e))
        tiles = [0.0] * 7
        for i in range(WIN // TILE):
            here = pl.ds(i * TILE, TILE)
            ds = attend[h, :, here].astype(F32) * (scores[:, here] - inner[:, i * TILE : (i + 1) * TILE])
            for j in range(WIN // TILE):
                d = i - j + 3
                tiles[d] = tiles[d] + ds[j * TILE : (j + 1) * TILE, :]
            scores[:, here] = ds
        low = scores[...].astype(BF)
        key = mixed_t[part, pl.ds(row + 128, HEAD), :]
        query = mixed_t[part, pl.ds(row, HEAD), :]
        gq = dot(key, low) * (HEAD**-0.5)
        gk = dot(query, low, NT)
        gv = dot(grad_c, attend[h], NT)
        grad_mixed_t[part, pl.ds(row, HEAD), :] = gq.astype(BF)
        grad_mixed_t[part, pl.ds(row + 128, HEAD), :] = gk.astype(BF)
        grad_mixed_t[part, pl.ds(row + 256, HEAD), :] = gv.astype(BF)
        blocks = [0.0] * 8
        turned = dot(turn, jnp.concatenate([t.astype(BF) for t in tiles], axis=1))
        for d in range(7):
            wide = turned[:, d * TILE : (d + 1) * TILE]
            wide = jnp.concatenate([wide, jnp.zeros((TILE, TILE), F32)], axis=1)
            wide = pltpu.roll(wide, 0, 1, stride=1, stride_axis=0)
            line = jnp.sum(wide, axis=0, keepdims=True)
            blocks[d] = blocks[d] + line[:, :TILE]
            blocks[d + 1] = blocks[d + 1] + line[:, TILE:]
        small[pl.ds(h, 1), :] = jnp.concatenate(blocks[:4], axis=1)
        small[pl.ds(H + h, 1), :] = jnp.concatenate(blocks[4:], axis=1)


def project_back(part, g, tok_t, grad_mixed_t, gi):
    value = dot(tok_t[...], grad_mixed_t[part, pl.ds(g * PC, PC), :], NT)
    put_cols(gi, part, g * PC, value.astype(BF))


def input_back(grad_mixed_t, wi, hat):
    for r in range(0, WIN, ROWS):
        here = pl.ds(r, ROWS)
        value = 0.0
        for part in range(HALF):
            value = value + dot(cols(wi, part, 0, 3 * HD), grad_mixed_t[part, :, here])
        hat[here, :] = hat[here, :] + value.T


MESH = pl.DeviceIdType.MESH
N_SEND, N_RECV = 105, 174
WI, WO, W1, W2, GI_ALL = range(5)
WI_A, WO_B, W1_A, W1_B, WI_B, W2_A, W2_B = range(7)
GATHER = {
    WI_A: (WI, 0, 768, "x", 0),
    WO_B: (WO, 0, 384, "y", 0),
    W1_A: (W1, 0, 512, "x", 0),
    W1_B: (W1, 512, 1024, "y", 0),
    WI_B: (WI, 768, 384, "y", 0),
    W2_A: (W2, 0, 896, "x", 0),
    W2_B: (W2, 896, 640, "y", 0),
}
G2 = range(0, 6)
G1 = range(6, 12)
GO = 12
GI = range(13, 17)
SMALL = 17
SCATTER = {
    G2[0]: (W2, 0, 256, "x", 1),
    G1[0]: (W1, 0, 256, "y", 0),
    G2[1]: (W2, 256, 256, "x", 1),
    G1[1]: (W1, 256, 256, "y", 1),
    G2[2]: (W2, 512, 256, "y", 0),
    G1[2]: (W1, 512, 256, "x", 0),
    G2[3]: (W2, 768, 256, "x", 0),
    G1[3]: (W1, 768, 256, "y", 1),
    G2[4]: (W2, 1024, 256, "x", 0),
    G1[4]: (W1, 1024, 256, "x", 1),
    G2[5]: (W2, 1280, 256, "y", 1),
    G1[5]: (W1, 1280, 256, "y", 1),
    GO: (WO, 0, 384, "x", 0),
    GI[0]: (GI_ALL, 0, 384, "y", 0),
    GI[1]: (GI_ALL, 384, 384, "x", 0),
    GI[2]: (GI_ALL, 768, 256, "x", 0),
    GI[3]: (GI_ALL, 1024, 128, "x", 0),
}


def scatter_buffers(depth, rows):
    out = {}
    for name, (_, _, width, first, late) in SCATTER.items():
        second = (depth, 2, rows, width) if first == "y" else (2, depth, rows, width)
        out[name] = (
            pltpu.VMEM((2, depth, 2, rows, width), BF),
            pltpu.VMEM(second, BF),
            pltpu.VMEM((rows, width) if late else (depth, rows, width), BF),
            pltpu.VMEM((depth, 2, rows, width) if late else (depth, rows, width), BF),
        )
    return out


class Exchange:
    def __init__(self, depth, send_sem, recv_sem):
        row = lax.axis_index("dp")
        y = lax.axis_index("mp")
        c, x, z = row % 2, (row // 2) % 2, row // 4
        self.depth = depth
        self.c, self.x, self.y, self.z = c, x, y, z
        self.c1_, self.x1, self.y1 = 1 - c, 1 - x, 1 - y
        self.up = [(z + k) % depth for k in range(depth)]
        self.down = [(z + depth - k) % depth for k in range(depth)]
        self.peers = {
            ("c", 1): ((z * 2 + x) * 2 + self.c1_, y),
            ("x", 1): ((z * 2 + self.x1) * 2 + c, y),
            ("y", 1): (row, self.y1),
        }
        for k in range(1, depth):
            self.peers["z", k] = ((self.up[k] * 2 + x) * 2 + c, y)
        self.around = dict(self.peers)
        half = self.half = depth // 2
        near = z // half * half
        self.starts = (half - near, near)
        self.goal, self.origin = {}, {}
        for g in range(2):
            for j in range(g, half):
                self.goal[g, j] = self.starts[g] + (z + j) % half
                self.origin[g, j] = self.starts[g] + (z + half - j) % half
                self.peers[g, j] = ((self.goal[g, j] * 2 + x) * 2 + c, y)
        self.send_sem, self.recv_sem = send_sem, recv_sem
        self.keys, self.sent = {}, {}

    def greet(self):
        barrier = pltpu.get_barrier_semaphore()
        for peer in self.around.values():
            pl.semaphore_signal(barrier, inc=1, device_id=peer, device_id_type=MESH)
        pl.semaphore_wait(barrier, len(self.around))

    def slot(self, keys, key, most):
        k = keys.setdefault(key, len(keys))
        assert k < most, k
        return k

    def copy(self, key, sent, src, dst, axis, step=1):
        return pltpu.make_async_remote_copy(
            src_ref=src,
            dst_ref=dst,
            send_sem=self.send_sem.at[self.slot(self.sent, sent, N_SEND)],
            recv_sem=self.recv_sem.at[self.slot(self.keys, key, N_RECV)],
            device_id=self.peers[axis, step],
            device_id_type=MESH,
        )

    def send(self, key, sent, src, dst, axis, step=1):
        self.copy(key, sent, src, dst, axis, step).start()

    def recv(self, key, dst, axis="c", step=1):
        k = self.recv_sem.at[self.slot(self.keys, key, N_RECV)]
        pltpu.make_async_remote_copy(
            src_ref=dst,
            dst_ref=dst,
            send_sem=k,
            recv_sem=k,
            device_id=self.peers[axis, step],
            device_id_type=MESH,
        ).wait_recv()

    def gone(self, sent, ref):
        k = self.send_sem.at[self.slot(self.sent, sent, N_SEND)]
        pltpu.make_async_remote_copy(
            src_ref=ref,
            dst_ref=ref,
            send_sem=k,
            recv_sem=k,
            device_id=self.peers["c", 1],
            device_id_type=MESH,
        ).wait_send()


class Quiet:
    def __getattr__(self, name):
        return None


class Gather(Exchange):
    def use(self, refs):
        self.refs = refs

    def at(self, s, y, z, x, c):
        name, start, width, _, _ = GATHER[s]
        return self.refs[name].at[y, z, x, c, :, pl.ds(start, width)]

    def send(self, s, phase, k, src, axis, step=1):
        super().send((s, phase, k), (s, phase), src, src, axis, step)

    def begin(self, s):
        own = self.at(s, self.y, self.z, self.x, self.c)
        if GATHER[s][4]:
            self.across(s, 0)
        for k in range(1, self.depth):
            self.send(s, 0, k, own, "z", k)
        if not GATHER[s][4]:
            self.across(s, 0)

    def across(self, s, k):
        self.send(s, 1, k, self.at(s, self.y, self.down[k], self.x, self.c), GATHER[s][3])

    def zd(self, s, k):
        self.recv((s, 0, k), self.at(s, self.y, self.down[k], self.x, self.c))
        self.across(s, k)

    def beside(self, s, k):
        if GATHER[s][3] == "x":
            return self.at(s, self.y, self.down[k], self.x1, self.c)
        return self.at(s, self.y1, self.down[k], self.x, self.c)

    def pair(self, s, k):
        every = slice(None)
        if GATHER[s][3] == "x":
            return self.at(s, self.y, self.down[k], every, self.c)
        return self.at(s, every, self.down[k], self.x, self.c)

    def second(self, s, k):
        self.send(s, 2, 0, self.pair(s, k), "y" if GATHER[s][3] == "x" else "x")

    def pd(self, s, k):
        self.recv((s, 1, k), self.beside(s, k))
        self.second(s, k)

    def ad(self, s):
        self.recv((s, 1, 0), self.beside(s, 0))
        for k in range(1, self.depth):
            self.send(s, 0, k, self.beside(s, 0), "z", k)
        self.second(s, 0)

    def pz(self, s, k):
        self.recv((s, 0, k), self.pair(s, k))
        self.second(s, k)

    def parts(self, s, c):
        every = slice(None)
        if GATHER[s][3] == "x":
            return self.at(s, self.y, every, every, c), self.at(s, self.y1, every, every, c)
        return self.at(s, every, every, self.x, c), self.at(s, every, every, self.x1, c)

    def c1(self, s):
        self.send(s, 3, 0, self.parts(s, self.c)[0], "c")

    def qd(self, s):
        far = self.parts(s, self.c)[1]
        self.recv((s, 2, 0), far)
        self.send(s, 3, 1, far, "c")

    def f1(self, s):
        self.recv((s, 3, 0), self.parts(s, self.c1_)[0])

    def f2(self, s):
        self.recv((s, 3, 1), self.parts(s, self.c1_)[1])

    def land(self):
        every, most = slice(None), pl.ds(0, self.depth - 1)
        for s in GATHER:
            if GATHER[s][4]:
                self.gone((s, 0), self.at(s, every, most, self.x, self.c))
                self.gone((s, 1), self.at(s, self.y, self.z, self.x, self.c))
            else:
                self.gone((s, 0), self.at(s, self.y, most, self.x, self.c))
                self.gone((s, 1), self.at(s, self.y, every, self.x, self.c))
            self.gone((s, 2), self.at(s, self.y, every, every, self.c))
            self.gone((s, 3), self.at(s, every, every, every, self.c))


class Scatter(Exchange):
    def use(self, refs, buffers, finish):
        self.refs, self.buffers, self.finish = refs, buffers, finish

    def at(self, s, y, z, x, c):
        name, start, width, _, _ = SCATTER[s]
        return self.refs[name].at[y, z, x, c, :, pl.ds(start, width)]

    def send(self, s, phase, k, src, dst, axis, step=1):
        super().send((~s, phase, k), (~s, phase), src, dst, axis, step)

    def group(self, g):
        return pl.ds(self.starts[g], self.half)

    def s0(self, s):
        every = slice(None)
        away = self.at(s, every, every, every, self.c1_)
        self.send(s, 0, 0, away, self.buffers[s][0], "c")

    def landing(self, s, g):
        if SCATTER[s][3] == "y":
            return self.buffers[s][1].at[self.group(g)]
        return self.buffers[s][1].at[:, self.group(g)]

    def s1(self, s, g):
        every = slice(None)
        if g == 0:
            self.recv((~s, 0, 0), self.buffers[s][0])
        own = self.at(s, every, self.group(g), every, self.c)
        own[...] = own[...] + self.buffers[s][0][:, self.group(g)]
        if SCATTER[s][3] == "y":
            away = self.at(s, self.y1, self.group(g), every, self.c)
        else:
            away = self.at(s, every, self.group(g), self.x1, self.c)
        self.send(s, 1, g, away, self.landing(s, g), SCATTER[s][3])

    def both(self, s, z):
        every = slice(None)
        if SCATTER[s][3] == "y":
            return self.at(s, self.y, z, every, self.c)
        return self.at(s, every, z, self.x, self.c)

    def away(self, s, z):
        if SCATTER[s][3] == "y":
            return self.at(s, self.y, z, self.x1, self.c)
        return self.at(s, self.y1, z, self.x, self.c)

    def near(self, s, g):
        self.recv((~s, 1, g), self.landing(s, g))
        own = self.both(s, self.group(g))
        own[...] = own[...] + self.landing(s, g)[...]

    def s2(self, s, g):
        self.near(s, g)
        landing = self.buffers[s][2].at[self.group(g)]
        axis = "x" if SCATTER[s][3] == "y" else "y"
        self.send(s, 2, g, self.away(s, self.group(g)), landing, axis)

    def t2(self, s, g):
        self.near(s, g)
        for j in range(g, self.half):
            away = self.both(s, self.goal[g, j])
            self.send(s, 3, 0, away, self.buffers[s][3].at[self.z], g, j)

    def s3(self, s, g):
        got = self.buffers[s][2].at[self.group(g)]
        self.recv((~s, 2, g), got)
        own = self.at(s, self.y, self.group(g), self.x, self.c)
        own[...] = own[...] + got[...]
        for j in range(g, self.half):
            away = self.at(s, self.y, self.goal[g, j], self.x, self.c)
            self.send(s, 3, 0, away, self.buffers[s][3].at[self.z], g, j)

    def from_z(self, s, own):
        got = self.buffers[s][3]
        total = own[...].astype(F32)
        self.recv((~s, 3, 0), got.at[pl.ds(0, self.depth - 1)])
        for g in range(2):
            for j in range(g, self.half):
                total = total + got[self.origin[g, j]].astype(F32)
        return total

    def t3(self, s):
        own = self.both(s, self.z)
        own[...] = self.from_z(s, own).astype(BF)
        axis = "x" if SCATTER[s][3] == "y" else "y"
        self.send(s, 2, 0, self.away(s, self.z), self.buffers[s][2], axis)

    def s4(self, s):
        own = self.at(s, self.y, self.z, self.x, self.c)
        if SCATTER[s][4]:
            got = self.buffers[s][2]
            self.recv((~s, 2, 0), got)
            total = own[...].astype(F32) + got[...].astype(F32)
        else:
            total = self.from_z(s, own)
        self.finish(self, s, total)

    def land(self):
        every, most = slice(None), pl.ds(0, self.depth - 1)
        for s in SCATTER:
            self.gone((~s, 0), self.at(s, every, every, every, self.c))
            self.gone((~s, 1), self.at(s, self.y, every, every, self.c))
            if SCATTER[s][4]:
                self.gone((~s, 2), self.at(s, self.y, self.z, self.x, self.c))
                self.gone((~s, 3), self.at(s, every, most, self.x, self.c))
            else:
                self.gone((~s, 2), self.at(s, self.y, every, self.x, self.c))
                self.gone((~s, 3), self.at(s, self.y, most, self.x, self.c))
            if SCATTER[s][0] not in (W1, W2):
                self.gone((~s, 4), self.at(s, self.y, self.z, self.x, self.c))


def layer_kernel(comm, dims, names, *refs):
    r = dict(zip(names, refs))
    r.update(refs[len(names)])
    k = type("Refs", (), r)
    counts, gate, vectors, hidden, small = k.counts, k.gate, k.vectors, k.hidden, k.small
    tok, tok_t, wi, wo, w1, w2 = k.tok, k.tok_t, k.wi, k.wo, k.w1, k.w2
    mixed_t, mixed_n, attend, scores = k.mixed_t, k.mixed_n, k.attend, k.scores
    context_t, hat, scale, normed, acc = k.context_t, k.hat, k.scale, k.normed, k.acc

    def local_copy(j, src, dst):
        copy = pltpu.make_async_copy(src, dst, k.sems.at[j])
        copy.start()
        return copy

    depth, rows = dims
    matrices = {WI: wi, WO: wo, W1: w1, W2: w2}
    if comm:
        ag = Gather(depth, k.send_sem, k.recv_sem)
        ag.use(matrices)
        rs = Scatter(depth, k.send_sem, k.recv_sem)
        rs.keys, rs.sent = ag.keys, ag.sent
        own, other = ag.y, ag.y1
    else:
        ag = rs = Quiet()
        own, other = 0, 1

    def do(*steps):
        if comm:
            for step, *which in steps:
                step(*which)

    def attention(bias, mask, pattern, stage_i, stage_o, stage_f):

        def others():
            pairs = (k.counts_in, counts), (k.pattern_in, pattern), (k.gate_in, gate)
            pairs = pairs + ((k.tok_in, tok), (k.vectors_in, vectors), (k.hidden_in, hidden))
            return [local_copy(j, src, dst) for j, (src, dst) in enumerate(pairs)]

        if comm:
            y, z, x, c = ag.y, ag.z, ag.x, ag.c
            gets = [
                local_copy(
                    6 + kind,
                    k.wi_in.at[:, pl.ds(pl.multiple_of(kind * D + y * HD, 128), HD)],
                    stage_i.at[kind],
                )
                for kind in range(3)
            ]
            get_f = local_copy(9, k.wf_in, stage_f)
            get_o = local_copy(10, k.wo_in.at[:, pl.ds(pl.multiple_of(y * HD, 128), HD)], stage_o)
            more = others()
            ag.greet()
            for kind in range(3):
                gets[kind].wait()
            for g in range(PAIRS):
                for kind in range(3):
                    wi[y, z, x, c, :, pl.ds(g * PC + kind * 128, 128)] = stage_i[
                        kind, :, pl.ds(g * 128, 128)
                    ].astype(BF)
            for s in (WI_A, WI_B):
                ag.begin(s)
            get_o.wait()
            wo[y, z, x, c] = stage_o[...].astype(BF)
            get_f.wait()
            w1[y, z, x, c] = stage_f[0].astype(BF)
            w2[y, z, x, c] = stage_f[1].astype(BF)
            for s in GATHER:
                if s not in (WI_A, WI_B):
                    ag.begin(s)
        else:
            more = others()
            plain = [
                local_copy(6 + j, src, dst)
                for j, (src, dst) in enumerate(
                    ((k.wi_in, wi), (k.wo_in, wo), (k.w1_in, w1), (k.w2_in, w2))
                )
            ]
        for copy in more:
            copy.wait()
        tok_t[...] = tok[...].T
        build_mask(counts, pattern, mask)
        build_bias(gate, k.table, bias)
        if not comm:
            for copy in plain:
                copy.wait()

        def one(part, g):
            project_mixed(part, g, tok, wi, mixed_t, mixed_n)
            attend_pair(part, g, mixed_t, mixed_n, bias, mask, scores, attend, context_t)

        do((ag.zd, WI_A, 1), (ag.pd, WI_A, 0), (ag.pd, WO_B, 0), (ag.pd, W1_A, 0), (ag.pd, W1_B, 0), (ag.pd, WI_B, 0), (ag.zd, WI_A, 2), (ag.pd, W2_A, 0), (ag.pd, W2_B, 0), (ag.zd, WI_A, 3), (ag.zd, WI_B, 1), (ag.pd, WI_A, 1), (ag.zd, WI_B, 2), (ag.zd, WI_B, 3), (ag.zd, WO_B, 1), (ag.zd, WO_B, 2), (ag.zd, WO_B, 3), (ag.zd, W1_A, 1), (ag.zd, W1_A, 2), (ag.pd, WI_B, 1), (ag.pd, WI_A, 2), (ag.zd, W1_A, 3), (ag.zd, W1_B, 1), (ag.pd, WI_B, 2), (ag.pd, WI_B, 3), (ag.c1, WI_B), (ag.pd, WI_A, 3), (ag.c1, WI_A), (ag.pd, WO_B, 1), (ag.pd, W1_A, 1), (ag.pd, WO_B, 2), (ag.zd, W1_B, 2), (ag.pd, W1_A, 2), (ag.pd, WO_B, 3), (ag.c1, WO_B), (ag.f1, WI_A))
        one(own, 0)
        do((ag.pd, W1_A, 3), (ag.c1, W1_A), (ag.zd, W1_B, 3))
        one(own, 1)
        do((ag.pd, W1_B, 1), (ag.zd, W2_A, 1), (ag.qd, WI_B), (ag.zd, W2_A, 2), (ag.qd, WI_A), (ag.zd, W2_A, 3), (ag.qd, WO_B), (ag.f2, WI_A))
        one(other, 0)
        do((ag.pd, W1_B, 2), (ag.zd, W2_B, 1), (ag.zd, W2_B, 2))
        one(other, 1)
        do((ag.zd, W2_B, 3), (ag.f1, WI_B), (ag.f2, WI_B))
        one(own, 2)
        do((ag.qd, W1_A), (ag.pd, W2_A, 1))
        one(other, 2)

    pl.run_scoped(
        attention,
        pltpu.VMEM((H, 7, TILE, TILE), F32),
        pltpu.VMEM((WIN, WIN), F32),
        pltpu.VMEM((WIN, WIN), jnp.int32),
        pltpu.VMEM((3, rows, HD), F32),
        pltpu.VMEM((rows, HD), F32),
        pltpu.VMEM((2, rows, HF), F32),
    )

    def feed(active, slope, normed_t, grad, grad_t):
        get_cot = local_copy(0, k.cot_in, grad)

        if comm:
            rs.use(dict(matrices), k.buffers, None)

        def down(part, start, width):
            hidden_back(part, start, width, grad, grad_t, w2, active, slope, small)

        def up(part, start, width):
            hidden_back_up(part, start, width, normed_t, w1, slope, acc)

        do((ag.pd, W1_B, 3), (ag.c1, W1_B), (ag.pd, W2_A, 2), (ag.pd, W2_A, 3), (ag.c1, W2_A), (ag.pd, W2_B, 1), (ag.f1, WO_B), (ag.f2, WO_B))
        out_project(tok, context_t, wo, vectors, hat, scale, normed, normed_t)
        do((ag.pd, W2_B, 2), (ag.f1, W1_A), (ag.f2, W1_A))
        hidden_step(0, 0, normed, w1, hidden, active, slope)
        do((ag.pd, W2_B, 3), (ag.c1, W2_B))
        hidden_step(1, 0, normed, w1, hidden, active, slope)
        do((ag.qd, W1_B), (ag.f1, W1_B), (ag.f2, W1_B))
        hidden_step(0, 1, normed, w1, hidden, active, slope)
        hidden_step(1, 1, normed, w1, hidden, active, slope)
        hidden_step(0, 2, normed, w1, hidden, active, slope)
        do((ag.qd, W2_A))
        hidden_step(1, 2, normed, w1, hidden, active, slope)
        do((ag.qd, W2_B), (ag.f1, W2_A), (ag.f2, W2_A))
        result_step(0, active, w2, acc)
        do((ag.f1, W2_B), (ag.f2, W2_B))
        result_step(1, active, w2, acc)
        result_step(2, active, w2, acc)
        get_cot.wait()
        second_norm(acc, normed, grad, vectors, k.low, grad, grad_t, small)
        put_low = local_copy(7, k.low, k.low_out)
        if comm:
            ag.land()
        down(0, 0, 256)
        down(1, 0, 256)
        do((rs.s0, G2[0]))
        up(0, 0, 256)
        up(1, 0, 256)
        do((rs.s0, G1[0]))
        down(0, 256, 256)
        down(1, 256, 256)
        do((rs.s1, G2[0], 0), (rs.s1, G2[0], 1), (rs.s0, G2[1]))
        up(0, 256, 256)
        do((rs.s1, G1[0], 0), (rs.s1, G1[0], 1))
        up(1, 256, 256)
        do((rs.s0, G1[1]))
        down(0, 512, 256)
        do((rs.s1, G2[1], 0), (rs.s1, G2[1], 1))
        down(1, 512, 256)
        do((rs.s0, G2[2]))
        up(0, 512, 256)
        do((rs.s1, G1[1], 0), (rs.s1, G1[1], 1))
        up(1, 512, 256)
        do((rs.s0, G1[2]), (rs.t2, G2[0], 0))
        down(0, 768, 256)
        do((rs.s2, G1[0], 0), (rs.s1, G2[2], 0), (rs.s1, G2[2], 1))
        down(1, 768, 256)
        do((rs.t2, G2[0], 1), (rs.s0, G2[3]))
        up(0, 768, 256)
        do((rs.s1, G1[2], 0), (rs.s1, G1[2], 1), (rs.s2, G1[0], 1))
        up(1, 768, 256)
        do((rs.s0, G1[3]))
        down(0, 1024, 256)
        do((rs.t2, G2[1], 0), (rs.s1, G2[3], 0), (rs.s1, G2[3], 1))
        down(1, 1024, 256)
        do((rs.s0, G2[4]), (rs.t2, G1[1], 0))
        up(0, 1024, 256)
        do((rs.s1, G1[3], 0), (rs.s1, G1[3], 1), (rs.t2, G2[1], 1))
        up(1, 1024, 256)
        do((rs.t3, G2[0]), (rs.s3, G1[0], 0), (rs.s0, G1[4]), (rs.t2, G1[1], 1))
        down(0, 1280, 256)
        do((rs.s1, G2[4], 0), (rs.s1, G2[4], 1))
        down(1, 1280, 256)
        do((rs.s0, G2[5]))
        up(0, 1280, 256)
        do((rs.s2, G1[2], 0), (rs.s2, G2[2], 0), (rs.s1, G1[4], 0), (rs.s1, G1[4], 1))
        up(1, 1280, 256)
        do((rs.s0, G1[5]))
        put_low.wait()

    pl.run_scoped(
        feed,
        pltpu.VMEM((HALF * NCH, WIN, CH), BF),
        pltpu.VMEM((HALF * NCH, WIN, CH), BF),
        pltpu.VMEM((D, WIN), BF),
        pltpu.VMEM((WIN, D), BF),
        pltpu.VMEM((D, WIN), BF),
    )

    def finish(net, s, total):
        name, start, width, _, _ = SCATTER[s]
        here = pl.ds(start, width)
        if name in (W1, W2):
            k.box_f[0 if name == W1 else 1, :, here] = total
        else:
            box = k.box_i if name == GI_ALL else k.box_o
            box[net.y, :, here] = total.astype(BF)
            own = box.at[net.y, :, here]
            net.send(s, 4, 0, own, own, "y")

    def s5(s):
        name, start, width, _, _ = SCATTER[s]
        box = k.box_i if name == GI_ALL else k.box_o
        rs.recv((~s, 4, 0), box.at[rs.y1, :, pl.ds(start, width)])

    def spread(j, src, dst, axis, step=1):
        Exchange.send(rs, (SMALL, j), (SMALL, j), src, dst, axis, step)

    def m0():
        spread(0, small, k.line.at[0], "c")

    def m1():
        rs.recv((SMALL, 0), k.line.at[0])
        k.line[1] = small[...] + k.line[0]
        spread(1, k.line.at[1], k.line.at[2], "y")

    def m2():
        rs.recv((SMALL, 1), k.line.at[2])
        k.line[3] = k.line[1] + k.line[2]
        spread(2, k.line.at[3], k.line.at[4], "x")

    def m3():
        rs.recv((SMALL, 2), k.line.at[4])
        k.lines[rs.z] = k.line[3] + k.line[4]
        for j in range(1, depth):
            spread(3, k.lines.at[rs.z], k.lines.at[rs.z], "z", j)

    def m4():
        rs.recv((SMALL, 3), k.lines.at[pl.ds(0, depth - 1)])
        total = k.lines[0]
        for j in range(1, depth):
            total = total + k.lines[j]
        k.line[0] = total

    def last(grad_mixed_t, grad_context_t, gi):
        grad_low = normed
        if comm:
            rs.use({**matrices, GI_ALL: gi}, k.buffers, finish)

        def one(part, g):
            attend_back_pair(
                part, g, mixed_t, mixed_n, attend, context_t, grad_context_t, scores, grad_mixed_t, small
            )
            project_back(part, g, tok_t, grad_mixed_t, gi)

        first_norm_back(acc, hat, scale, vectors, grad_low, small)
        do((rs.s2, G1[2], 1), (rs.s2, G2[2], 1), (rs.s1, G2[5], 0), (rs.s1, G2[5], 1))
        out_back(grad_low, context_t, wo, wo, grad_context_t)
        do((rs.s0, GO), (rs.s3, G1[0], 1), (rs.t2, G1[3], 0), (rs.t3, G2[1]), (rs.s1, G1[5], 0), (rs.s1, G1[5], 1), (rs.s2, G2[3], 0))
        one(0, 0)
        do((rs.s1, GO, 0), (rs.s1, GO, 1), (rs.s3, G1[2], 0), (rs.s4, G2[0]), (rs.s4, G1[0]), (rs.t2, G1[3], 1), (rs.t3, G1[1]), (rs.s2, G2[3], 1))
        one(1, 0)
        do((rs.s3, G1[2], 1), (rs.s0, GI[0]), (rs.s2, G2[4], 0), (rs.t2, G2[5], 0))
        one(0, 1)
        do((rs.s3, G2[2], 0), (rs.t2, G2[5], 1), (rs.s1, GI[0], 0), (rs.s1, GI[0], 1), (rs.t3, G1[3]), (rs.s4, G2[1]), (rs.s2, G2[4], 1))
        one(1, 1)
        do((rs.s0, GI[1]), (rs.s4, G1[2]), (rs.t2, G1[4], 0), (rs.t2, G1[5], 0))
        one(0, 2)
        do((rs.s3, G2[2], 1), (rs.s1, GI[1], 0), (rs.s1, GI[1], 1), (rs.t2, G1[4], 1), (rs.t2, G1[5], 1), (rs.s3, G2[3], 0))
        one(1, 2)
        do((rs.s2, GO, 0), (rs.s0, GI[2]), (rs.s0, GI[3]), (rs.t3, G2[5]), (rs.s3, G2[4], 0), (rs.s3, G2[3], 1), (m0,))
        input_back(grad_mixed_t, wi, hat)
        put_grad = local_copy(0, hat, k.grad_out)
        do((rs.s2, GO, 1), (rs.s2, GI[0], 0), (rs.s4, G1[3]), (rs.s1, GI[2], 0), (rs.s1, GI[3], 0), (rs.s1, GI[2], 1), (rs.s1, GI[3], 1), (rs.s4, G1[1]), (rs.s4, G2[2]), (m1,), (rs.s2, GI[0], 1), (rs.t3, G1[4]), (rs.s3, G2[4], 1), (rs.s2, GI[1], 0), (rs.t3, G1[5]), (rs.s3, GO, 0), (rs.s3, GO, 1), (rs.s2, GI[1], 1), (rs.s4, G2[5]), (rs.s4, G2[3]), (rs.s4, G2[4]), (m2,), (rs.s3, GI[0], 0), (rs.s4, G1[4]), (rs.s3, GI[1], 0), (rs.s2, GI[2], 0), (rs.s4, GO), (rs.s2, GI[3], 0), (rs.s3, GI[1], 1), (rs.s3, GI[2], 0), (rs.s2, GI[2], 1), (s5, GO), (rs.s2, GI[3], 1), (rs.s3, GI[3], 0), (rs.s3, GI[0], 1), (rs.s4, GI[1]), (rs.s3, GI[2], 1), (rs.s4, G1[5]), (rs.s3, GI[3], 1), (m3,), (s5, GI[1]), (rs.s4, GI[0]), (rs.s4, GI[2]), (rs.s4, GI[3]), (s5, GI[0]), (s5, GI[2]), (s5, GI[3]), (m4,))
        if comm:
            outs = ((k.line.at[0], k.small_out), (k.box_i, k.gi_out), (k.box_o, k.go_out))
            outs = outs + ((k.box_f, k.gf_out),)
        else:
            outs = ((small, k.small_out), (gi, k.gi_out), (wo, k.go_out))
            outs = outs + ((w1, k.g1_out), (w2, k.g2_out))
        outs = [local_copy(1 + j, src, dst) for j, (src, dst) in enumerate(outs)]
        if comm:
            rs.land()
            for j in range(3):
                rs.gone((SMALL, j), small)
            rs.gone((SMALL, 3), k.lines.at[pl.ds(0, depth - 1)])
        for copy in outs:
            copy.wait()
        put_grad.wait()

    pl.run_scoped(
        last,
        pltpu.VMEM((HALF, 3 * HD, WIN), BF),
        pltpu.VMEM((D, WIN), BF),
        pltpu.VMEM(wi.shape, BF),
    )


IN_NAMES = (
    "counts_in",
    "tok_in",
    "cot_in",
    "pattern_in",
    "gate_in",
    "vectors_in",
    "hidden_in",
    "wi_in",
    "wo_in",
    "w1_in",
    "w2_in",
)
OUT_NAMES_PLAIN = ("low_out", "grad_out", "small_out", "gi_out", "go_out", "g1_out", "g2_out")
OUT_NAMES = ("low_out", "grad_out", "small_out", "gi_out", "go_out", "gf_out")


def layer_call(comm, depth, rows, counts, tok, cot, pattern, gate, vectors, hidden, *weights):
    hbm = pl.BlockSpec(memory_space=pl.ANY)
    lead = (HALF, depth, 2, 2, rows) if comm else (HALF, 1, 1, 1, D)
    shapes = [lead + (n,) for n in (3 * HD, HD, HF, HF)]
    scratch = dict(
        wi=pltpu.VMEM(shapes[0], BF),
        wo=pltpu.VMEM(shapes[1], BF),
        w1=pltpu.VMEM(shapes[2], BF),
        w2=pltpu.VMEM(shapes[3], BF),
        tok=pltpu.VMEM((WIN, D), BF),
        low=pltpu.VMEM((WIN, D), BF),
        tok_t=pltpu.VMEM((D, WIN), BF),
        mixed_t=pltpu.VMEM((HALF, 3 * HD, WIN), BF),
        mixed_n=pltpu.VMEM((HALF, WIN, 2 * HD), BF),
        attend=pltpu.VMEM((H, WIN, WIN), BF),
        scores=pltpu.VMEM((WIN, WIN), F32),
        context_t=pltpu.VMEM((D, WIN), BF),
        hat=pltpu.VMEM((WIN, D), F32),
        scale=pltpu.VMEM((WIN, 128), F32),
        normed=pltpu.VMEM((WIN, D), BF),
        acc=pltpu.VMEM((WIN, D), F32),
        table=pltpu.VMEM((H, 2 * WIN), F32),
        small=pltpu.VMEM((R_ALL, 512), F32),
        counts=pltpu.SMEM((1, 4), jnp.int32),
        gate=pltpu.VMEM(gate.shape, F32),
        vectors=pltpu.VMEM(vectors.shape, F32),
        hidden=pltpu.VMEM(hidden.shape, F32),
        sems=pltpu.SemaphoreType.DMA((12,)),
    )
    outs = [
        jax.ShapeDtypeStruct((WIN, D), BF),
        jax.ShapeDtypeStruct((WIN, D), F32),
        jax.ShapeDtypeStruct((R_ALL, 512), F32),
    ]
    names = IN_NAMES
    if comm:
        outs += [
            jax.ShapeDtypeStruct((HALF, rows, 3 * HD), BF),
            jax.ShapeDtypeStruct((HALF, rows, HD), BF),
            jax.ShapeDtypeStruct((2, rows, HF), F32),
        ]
        out_specs = [hbm] * 6
        scratch.update(
            box_i=pltpu.VMEM((HALF, rows, 3 * HD), BF),
            box_o=pltpu.VMEM((HALF, rows, HD), BF),
            box_f=pltpu.VMEM((2, rows, HF), F32),
            line=pltpu.VMEM((5, R_ALL, 512), F32),
            lines=pltpu.VMEM((depth, R_ALL, 512), F32),
            buffers=scatter_buffers(depth, rows),
            send_sem=pltpu.SemaphoreType.DMA((N_SEND,)),
            recv_sem=pltpu.SemaphoreType.DMA((N_RECV,)),
        )
        names = names[:9] + ("wf_in",)
        params = dict(collective_id=0, has_side_effects=True)
    else:
        weights = [w.reshape(s) for w, s in zip(weights, shapes)]
        outs += [jax.ShapeDtypeStruct(s, BF) for s in shapes]
        out_specs = [hbm] * 7
        params = {}
    names = names + (OUT_NAMES if comm else OUT_NAMES_PLAIN)
    return pl.pallas_call(
        functools.partial(layer_kernel, comm, (depth, rows), names),
        out_shape=outs,
        in_specs=[hbm] * (7 + len(weights)),
        out_specs=out_specs,
        scratch_shapes=[scratch],
        compiler_params=pltpu.CompilerParams(vmem_limit_bytes=62 * 2**20, **params),
        cost_estimate=pl.CostEstimate(
            flops=25 * 10**9, bytes_accessed=40 * 2**20, transcendentals=10**7
        ),
        name="layer",
    )(counts, tok, cot, pattern, gate, vectors, hidden, *weights)


def update_kernel(*refs):
    ins, outs, (low, grad, small, gi, go, gf, *held), sems = refs[:24], refs[24:44], refs[44:-1], refs[-1]

    def copy(j, src, dst):
        one = pltpu.make_async_copy(src, dst, sems.at[j])
        one.start()
        return one

    passing = [copy(0, ins[0], low), copy(1, ins[1], grad)]
    sums = [copy(2 + j, src, dst) for j, (src, dst) in enumerate(zip(ins[2:6], (small, gi, go, gf)))]
    gets = {}
    for j in (6, 7, 8, 0, 1, 2, 3, 4, 5) + tuple(range(9, 18)):
        gets[j] = copy(6 + j, ins[6 + j], held[j])
    puts = []
    for j in range(2):
        passing[j].wait()
        puts.append(copy(j, (low, grad)[j], outs[j]))
    for one in sums:
        one.wait()

    def step(n, here, value):
        p, m, v = (held[3 * n + j] for j in range(3))
        p[here], m[here], v[here] = adam_step(p[here], m[here], v[here], value, RATES[n])

    def ready(n):
        for j in range(3 * n, 3 * n + 3):
            gets[j].wait()

    def done(n):
        for j in range(3 * n, 3 * n + 3):
            puts.append(copy(6 + j, held[j], outs[2 + j]))

    every = slice(None)
    ready(2)
    for part in range(2):
        for c in range(HF // HD):
            here = (part, every, pl.ds(c * HD, HD))
            step(2, here, gf[here])
    done(2)
    ready(0)
    for kind in range(3):
        for part in range(HALF):
            value = [gi[part, :, pl.ds(g * PC + kind * 128, 128)] for g in range(PAIRS)]
            value = jnp.concatenate(value, axis=1).astype(F32)
            step(0, (every, pl.ds(kind * D + part * HD, HD)), value)
    done(0)
    ready(1)
    for part in range(HALF):
        step(1, (every, pl.ds(part * HD, HD)), go[part].astype(F32))
    done(1)
    for n in (3, 4, 5):
        ready(n)
    value = jnp.concatenate([small[pl.ds(0, H), :], small[pl.ds(H, H), :]], axis=1)
    value = value[:, : held[9].shape[1]] / (1.0 + jnp.exp(held[9][...]))
    step(3, (every, every), value)
    value = [small[pl.ds(R_VEC, 5), :], small[pl.ds(R_VEC + 5, 5), pl.ds(0, 256)]]
    step(4, (every, every), jnp.concatenate(value, axis=1))
    value = [
        small[pl.ds(R_HID + j, 1), pl.ds(q * 128, 128)]
        for j in range(HALF * NCH)
        for q in range(CH // 128)
    ]
    step(5, (every, every), jnp.concatenate(value, axis=0))
    for n in (3, 4, 5):
        done(n)
    for one in puts:
        one.wait()


def update_call(layer, weights):
    hbm = pl.BlockSpec(memory_space=pl.ANY)
    ins = list(layer) + list(weights)
    shapes = [jax.ShapeDtypeStruct(x.shape, x.dtype) for x in list(layer[:2]) + list(weights)]
    return pl.pallas_call(
        update_kernel,
        out_shape=shapes,
        in_specs=[hbm] * len(ins),
        out_specs=[hbm] * len(shapes),
        scratch_shapes=[pltpu.VMEM(x.shape, x.dtype) for x in ins]
        + [pltpu.SemaphoreType.DMA((len(ins),))],
        compiler_params=pltpu.CompilerParams(vmem_limit_bytes=62 * 2**20),
        cost_estimate=pl.CostEstimate(flops=10**7, bytes_accessed=12 * 10**6, transcendentals=10**6),
        name="update",
    )(*ins)


def collect(w, width):
    return w.reshape(D, HALF, width).transpose(1, 0, 2)


def local(
    tokens,
    cotangent,
    seq_counts,
    pattern,
    project_in,
    project_in_first,
    project_in_second,
    project_out,
    project_out_first,
    project_out_second,
    feed_forward,
    feed_forward_first,
    feed_forward_second,
    gate_logits,
    gate_logits_first,
    gate_logits_second,
    norm_vectors,
    norm_vectors_first,
    norm_vectors_second,
    hidden_bias,
    hidden_bias_first,
    hidden_bias_second,
):
    rows = project_in.shape[0]
    groups, halves = lax.axis_size("dp"), lax.axis_size("mp")
    comm = halves == HALF and groups % 8 == 0 and rows % 16 == 0
    shared = (
        seq_counts,
        tokens,
        cotangent,
        pattern,
        gate_logits,
        norm_vectors,
        hidden_bias.reshape(FF // 128, 128),
    )
    if comm:
        layer = layer_call(True, groups // 4, rows, *shared, project_in, project_out, feed_forward)
        weights = (
            project_in,
            project_in_first,
            project_in_second,
            project_out,
            project_out_first,
            project_out_second,
            feed_forward,
            feed_forward_first,
            feed_forward_second,
            gate_logits,
            gate_logits_first,
            gate_logits_second,
            norm_vectors,
            norm_vectors_first,
            norm_vectors_second,
        )
        flat = [w.reshape(-1, 128) for w in (hidden_bias, hidden_bias_first, hidden_bias_second)]
        outs = update_call(layer, weights + tuple(flat))
        return tuple(outs[:-3]) + tuple(w.reshape(FF) for w in outs[-3:])

    whole_in = lax.all_gather(project_in.astype(BF), "dp", axis=0, tiled=True)
    whole_out = lax.all_gather(project_out.astype(BF), "dp", axis=0, tiled=True)
    pair = lax.all_gather(feed_forward.astype(BF), "dp", axis=1, tiled=True)
    pair = lax.all_gather(pair, "mp", axis=2, tiled=True)
    wi = whole_in.reshape(D, 3, HALF, PAIRS, 128).transpose(2, 0, 3, 1, 4)
    wi = wi.reshape(HALF, D, 3 * HD)
    layer_out, input_grad, small, gi, go, g1, g2 = layer_call(
        False,
        1,
        D,
        *shared,
        wi,
        collect(whole_out, HD),
        collect(pair[0], HF),
        collect(pair[1], HF),
    )
    gi = gi.reshape(HALF, D, PAIRS, 3, 128).transpose(1, 3, 0, 2, 4).reshape(D, 3 * D)
    go = go.reshape(HALF, D, HD).transpose(1, 0, 2).reshape(D, D)
    gf = jnp.stack([g.reshape(HALF, D, HF).transpose(1, 0, 2).reshape(D, FF) for g in (g1, g2)])
    sum_in = lax.psum_scatter(gi, "dp", scatter_dimension=0, tiled=True)
    sum_in = lax.psum(sum_in.astype(F32), "mp")
    sum_out = lax.psum_scatter(go, "dp", scatter_dimension=0, tiled=True)
    sum_out = lax.psum(sum_out.astype(F32), "mp")
    sum_pair = lax.psum_scatter(gf, "dp", scatter_dimension=1, tiled=True)
    sum_pair = lax.psum_scatter(sum_pair, "mp", scatter_dimension=2, tiled=True).astype(F32)
    small = lax.psum(small, ("dp", "mp"))
    sum_gate = jnp.concatenate([small[:H], small[H : 2 * H]], axis=1)[:, : 2 * WIN - 1]
    sum_gate = sum_gate * jax.nn.sigmoid(-gate_logits)
    sum_vectors = jnp.concatenate(
        [small[R_VEC : R_VEC + 5], small[R_VEC + 5 : R_VEC + 10, :256]], axis=1
    )
    sum_bias = small[R_HID:].reshape(FF)
    outs = [layer_out, input_grad]
    for weight, first, second, grad, rate in (
        (project_in, project_in_first, project_in_second, sum_in, RATES[0]),
        (project_out, project_out_first, project_out_second, sum_out, RATES[1]),
        (feed_forward, feed_forward_first, feed_forward_second, sum_pair, RATES[2]),
        (gate_logits, gate_logits_first, gate_logits_second, sum_gate, RATES[3]),
        (norm_vectors, norm_vectors_first, norm_vectors_second, sum_vectors, RATES[4]),
        (hidden_bias, hidden_bias_first, hidden_bias_second, sum_bias, RATES[5]),
    ):
        outs.extend(adam_step(weight, first, second, grad, rate))
    return tuple(outs)


def solution(mesh):
    rows, whole = P(("dp", "mp"), None), P()
    split, pair = P("dp", None), P(None, "dp", "mp")
    return jax.shard_map(
        local,
        mesh=mesh,
        in_specs=(rows, rows, rows, whole) + (split,) * 6 + (pair,) * 3 + (whole,) * 9,
        out_specs=(rows, rows) + (split,) * 6 + (pair,) * 3 + (whole,) * 9,
        check_vma=False,
    )
```

```python
import functools
import math

import jax
import jax.numpy as jnp
from jax import lax
from jax.experimental import pallas as pl
from jax.experimental.pallas import tpu as pltpu
from jax.sharding import PartitionSpec as P

D = 768
H = 12
HEAD = 64
FF = 3072
TILE = 128
WIN = 512
STEP = 10
HALF = 2
HD = D // HALF
HF = FF // HALF
CH = 512
NCH = HF // CH
PAIRS = HD // 128
PC = 3 * 128

NORM_EPS = 1e-12
BETA_ONE = 0.9
BETA_TWO = 0.999
ADAM_EPS = 1e-08
DECAY = 0.01
MASKED = -1e30
RATES = (0.03, 0.25, 0.03, 1.0, 0.2, 0.2)

F32 = jnp.float32
BF = jnp.bfloat16
NN = ((1,), (0,))
NT = ((1,), (1,))
R_VEC, R_HID, R_ALL = 24, 34, 40


def dot(a, b, dims=NN):
    return lax.dot_general(a, b, (dims, ((), ())), preferred_element_type=F32)


def adam_step(weight, first, second, grad, rate):
    first = BETA_ONE * first + (1.0 - BETA_ONE) * grad
    second = BETA_TWO * second + (1.0 - BETA_TWO) * grad * grad
    update = first / (1.0 - BETA_ONE**STEP) / (jnp.sqrt(second / (1.0 - BETA_TWO**STEP)) + ADAM_EPS)
    return (weight - rate * (update + DECAY * weight), first, second)


def cols(ref, part, start, size):
    block = ref[part, :, :, :, :, pl.ds(start, size)]
    return block.reshape(D, size)


def put_cols(ref, part, start, value):
    shape = ref.shape[1:5] + (value.shape[1],)
    ref[part, :, :, :, :, pl.ds(start, value.shape[1])] = value.reshape(shape)


def build_mask(counts, pattern, mask):
    two, three, four = counts[0, 1], counts[0, 2], counts[0, 3]
    after_four = 4 * four
    after_three = after_four + 3 * three
    after_two = after_three + 2 * two
    tiles = WIN // TILE
    begins = []
    for tile in range(tiles):
        in_three = after_four + jnp.where(tile - after_four >= 3, 3, 0)
        in_two = after_three + jnp.where(tile - after_three >= 2, 2, 0)
        begin = jnp.where(
            tile < after_four,
            0,
            jnp.where(tile < after_three, in_three, jnp.where(tile < after_two, in_two, tile)),
        )
        begins.append(begin)
    starts = [
        [jnp.where(begins[tile] == b, 1.0, 0.0) for b in range(tile + 1)] for tile in range(tiles)
    ]
    for i in range(tiles):
        for j in range(tiles):
            allowed = jnp.zeros((TILE, TILE), F32)
            for b in range(min(i, j) + 1):
                block = pattern[pl.ds((i - b) * TILE, TILE), pl.ds((j - b) * TILE, TILE)]
                allowed = allowed + block.astype(F32) * (starts[i][b] * starts[j][b])
            allowed = jnp.where(allowed > 0.5, 0.0, MASKED)
            mask[pl.ds(j * TILE, TILE), pl.ds(i * TILE, TILE)] = allowed.T


def build_table(gate, table):
    x = gate[...]
    x = jnp.minimum(x, 0.0) - jnp.log(1.0 + jnp.exp(-jnp.abs(x)))
    table[:, pl.ds(0, x.shape[1])] = x


def build_bias(first, count, table, bias):
    def one(h, _):
        row = table[pl.ds(h, 1), :]
        for d in range(7):
            part = jnp.broadcast_to(row[:, d * TILE : d * TILE + 2 * TILE], (TILE, 2 * TILE))
            bias[h, d] = pltpu.roll(part, TILE + 1, 1, stride=1, stride_axis=0)[:, :TILE]
        return 0

    lax.fori_loop(first, first + count, one, 0)


def project_mixed(part, g, tok, wi, mixed_t, mixed_n):
    value = dot(tok[...], cols(wi, part, g * PC, PC)).astype(BF)
    mixed_n[part, :, pl.ds(g * 256, 256)] = value[:, 128:]
    query = value[:, :128] * jnp.asarray(HEAD**-0.5, BF)
    mixed_t[part, pl.ds(g * PC, PC), :] = jnp.concatenate([query.T, value[:, 128:].T], axis=0)


def pad_head(value, e):
    zero = jnp.zeros_like(value)
    return jnp.concatenate([value, zero] if e == 0 else [zero, value], axis=0)


def attend_head(part, g, e, mixed_t, mixed_n, bias, mask, scores, attend, context_t):
    keys = mixed_n[part, :, pl.ds(g * 256, 128)]
    row = g * PC + e * HEAD
    h = part * (H // HALF) + g * 2 + e
    query = pad_head(mixed_t[part, pl.ds(row, HEAD), :], e)
    scores[...] = dot(keys, query)
    for i in range(WIN // TILE):
        here = pl.ds(i * TILE, TILE)
        table = jnp.concatenate([bias[h, i - j + 3] for j in range(WIN // TILE)], axis=0)
        s = scores[:, here] + (table + mask[:, here])
        top = jnp.max(s, axis=0, keepdims=True)
        s = jnp.exp(s - top)
        total = jnp.sum(s, axis=0, keepdims=True)
        attend[h, :, here] = (s * (1.0 / total)).astype(BF)
    values = mixed_t[part, pl.ds(row + 256, HEAD), :]
    out = dot(values, attend[h])
    context_t[pl.ds(pl.multiple_of(h * HEAD, HEAD), HEAD), :] = out.astype(BF)


def norm_of(value):
    mean = jnp.mean(value, axis=-1, keepdims=True)
    center = value - mean
    spread = jnp.mean(center * center, axis=-1, keepdims=True)
    scale = lax.rsqrt(spread + NORM_EPS)
    return center * scale, scale


def norm_back(grad, hat, scale, gain):
    g = grad * gain
    first = jnp.mean(g, axis=-1, keepdims=True)
    second = jnp.mean(g * hat, axis=-1, keepdims=True)
    return (
        scale * (g - first - hat * second),
        jnp.sum(grad * hat, axis=0, keepdims=True),
        jnp.sum(grad, axis=0, keepdims=True),
    )


ROWS = 256


def out_project(r, tok, context_t, wo, vectors, hat, scale, normed, normed_t):
    here = pl.ds(r, ROWS)
    context = context_t[:, here].T
    branch = jnp.concatenate(
        [dot(context, cols(wo, part, 0, HD)) for part in range(HALF)], axis=1
    )
    h, s = norm_of(tok[here, :].astype(F32) + branch)
    hat[here, :] = h
    scale[here, :] = jnp.broadcast_to(s, (ROWS, 128))
    low = (h * vectors[0:1, :] + vectors[1:2, :]).astype(BF)
    normed[here, :] = low
    normed_t[:, here] = low.T


def hidden_step(part, c, normed, w1, hidden, active, slope):
    j = part * NCH + c
    bias = [hidden[pl.ds(j * (CH // 128) + q, 1), :] for q in range(CH // 128)]
    before = dot(normed[...], cols(w1, part, c * CH, CH)) + jnp.concatenate(bias, axis=1)
    half = 0.5 + 0.5 * lax.erf(before * math.sqrt(0.5))
    active[j] = (before * half).astype(BF)
    bell = jnp.exp(-0.5 * before * before) * (1.0 / math.sqrt(2 * math.pi))
    slope[j] = (half + before * bell).astype(BF)


def result_step(part, start, width, active, w2, acc):
    j, here = part * NCH + start // CH, pl.ds(start % CH, width)
    value = dot(active[j, :, here], cols(w2, part, start, width), NT)
    acc[...] = value if part == 0 and start == 0 else acc[...] + value


def second_norm(r, acc, normed, cot, vectors, low_out, grad, grad_t, small):
    here = pl.ds(r, ROWS)
    total = normed[here, :].astype(F32) + acc[here, :] + vectors[4:5, :]
    hat, scale = norm_of(total)
    low_out[here, :] = (hat * vectors[2:3, :] + vectors[3:4, :]).astype(BF)
    value, gain, shift = norm_back(cot[here, :].astype(F32), hat, scale, vectors[2:3, :])
    acc[here, :] = value
    low = value.astype(BF)
    grad[here, :] = low
    grad_t[:, here] = low.T
    sums = (gain, shift, jnp.sum(value, axis=0, keepdims=True))
    for k in range(3):
        put_vector(small, 2 + k, sums[k], r > 0)


def put_vector(small, k, value, more):
    one, two = pl.ds(R_VEC + k, 1), pl.ds(R_VEC + 5 + k, 1)
    left = value[:, :512]
    right = jnp.concatenate([value[:, 512:], jnp.zeros((1, 256), F32)], axis=1)
    small[one, :] = small[one, :] + left if more else left
    small[two, :] = small[two, :] + right if more else right


def hidden_back(part, start, width, grad, grad_t, w2, active, slope, small):
    j, here = part * NCH + start // CH, pl.ds(start % CH, width)
    before = dot(grad[...], cols(w2, part, start, width)) * slope[j, :, here].astype(F32)
    before = before.astype(BF)
    slope[j, :, here] = before
    put_cols(w2, part, start, dot(grad_t[...], active[j, :, here]).astype(BF))
    small[pl.ds(R_HID + j, 1), here] = jnp.sum(before.astype(F32), axis=0, keepdims=True)


def hidden_back_up(part, start, width, normed_t, w1, slope, acc):
    before = slope[part * NCH + start // CH, :, pl.ds(start % CH, width)]
    acc[...] += dot(before, cols(w1, part, start, width), NT)
    put_cols(w1, part, start, dot(normed_t[...], before).astype(BF))


def first_norm_back(r, acc, hat, scale, vectors, grad_low, small):
    here = pl.ds(r, ROWS)
    grad = acc[here, :].astype(BF).astype(F32)
    value, gain, shift = norm_back(grad, hat[here, :], scale[here, 0:1], vectors[0:1, :])
    hat[here, :] = value
    grad_low[here, :] = value.astype(BF)
    for k, total in enumerate((gain, shift)):
        put_vector(small, k, total, r > 0)


def context_back(r, grad_low, wo, grad_context_t):
    here = pl.ds(r, ROWS)
    low = grad_low[here, :]
    value = 0.0
    for part in range(HALF):
        value = value + dot(cols(wo, part, 0, HD), low[:, part * HD : (part + 1) * HD], NT)
    grad_context_t[:, here] = value.astype(BF)


def out_back(part, grad_low, context_t, go):
    low = grad_low[:, pl.ds(part * HD, HD)]
    put_cols(go, part, 0, dot(context_t[...], low).astype(BF))


def attend_back_head(part, g, e, mixed_t, mixed_n, attend, context_t, grad_context_t, scores, grad_mixed_t, small):
    values = mixed_n[part, :, pl.ds(g * 256 + 128, 128)]
    turn = lax.broadcasted_iota(jnp.int32, (TILE, TILE), 0) + lax.broadcasted_iota(
        jnp.int32, (TILE, TILE), 1
    )
    turn = jnp.where(turn == TILE - 1, 1.0, 0.0).astype(BF)
    row = g * PC + e * HEAD
    h = part * (H // HALF) + g * 2 + e
    place = pl.ds(pl.multiple_of(h * HEAD, HEAD), HEAD)
    grad_c = grad_context_t[place, :]
    inner = jnp.sum(
        grad_c.astype(F32) * context_t[place, :].astype(F32), axis=0, keepdims=True
    )
    scores[...] = dot(values, pad_head(grad_c, e))
    tiles = [0.0] * 7
    for i in range(WIN // TILE):
        here = pl.ds(i * TILE, TILE)
        ds = attend[h, :, here].astype(F32) * (scores[:, here] - inner[:, i * TILE : (i + 1) * TILE])
        for j in range(WIN // TILE):
            d = i - j + 3
            tiles[d] = tiles[d] + ds[j * TILE : (j + 1) * TILE, :]
        scores[:, here] = ds
    low = scores[...].astype(BF)
    key = mixed_t[part, pl.ds(row + 128, HEAD), :]
    query = mixed_t[part, pl.ds(row, HEAD), :]
    gq = dot(key, low) * (HEAD**-0.5)
    gk = dot(query, low, NT)
    gv = dot(grad_c, attend[h], NT)
    grad_mixed_t[part, pl.ds(row, HEAD), :] = gq.astype(BF)
    grad_mixed_t[part, pl.ds(row + 128, HEAD), :] = gk.astype(BF)
    grad_mixed_t[part, pl.ds(row + 256, HEAD), :] = gv.astype(BF)
    blocks = [0.0] * 8
    turned = dot(turn, jnp.concatenate([t.astype(BF) for t in tiles], axis=1))
    for d in range(7):
        wide = turned[:, d * TILE : (d + 1) * TILE]
        wide = jnp.concatenate([wide, jnp.zeros((TILE, TILE), F32)], axis=1)
        wide = pltpu.roll(wide, 0, 1, stride=1, stride_axis=0)
        line = jnp.sum(wide, axis=0, keepdims=True)
        blocks[d] = blocks[d] + line[:, :TILE]
        blocks[d + 1] = blocks[d + 1] + line[:, TILE:]
    small[pl.ds(h, 1), :] = jnp.concatenate(blocks[:4], axis=1)
    small[pl.ds(H + h, 1), :] = jnp.concatenate(blocks[4:], axis=1)


def project_back(part, g, tok_t, grad_mixed_t, gi):
    value = dot(tok_t[...], grad_mixed_t[part, pl.ds(g * PC, PC), :], NT)
    put_cols(gi, part, g * PC, value.astype(BF))


def input_back(r, grad_mixed_t, wi, hat):
    here = pl.ds(r, ROWS)
    value = 0.0
    for part in range(HALF):
        value = value + dot(cols(wi, part, 0, 3 * HD), grad_mixed_t[part, :, here])
    hat[here, :] = hat[here, :] + value.T


MESH = pl.DeviceIdType.MESH
N_SEND, N_RECV = 121, 206
WI, WO, W1, W2, GI_ALL = range(5)
WI_A, WO_A, W1_A, W2_A, WI_B, WI_D, WI_C, W2_B, W1_B, W2_C, W2_D = range(11)
GATHER = {
    WI_A: (WI, 0, 512, "x", 0),
    WO_A: (WO, 0, 384, "x", 0),
    W1_A: (W1, 0, 1024, "y", 0),
    W2_A: (W2, 0, 256, "x", 0),
    WI_B: (WI, 512, 384, "y", 0),
    WI_D: (WI, 896, 128, "y", 0),
    WI_C: (WI, 1024, 128, "x", 0),
    W2_B: (W2, 256, 768, "y", 0),
    W1_B: (W1, 1024, 512, "x", 1),
    W2_C: (W2, 1024, 384, "x", 1),
    W2_D: (W2, 1408, 128, "y", 1),
}
G2 = range(0, 6)
G1 = range(6, 12)
GO = 12
GI = range(13, 17)
SMALL = 17
SCATTER = {
    G2[0]: (W2, 0, 256, "x", 1),
    G1[0]: (W1, 0, 256, "x", 1),
    G2[1]: (W2, 256, 256, "y", 0),
    G1[1]: (W1, 256, 256, "x", 1),
    G2[2]: (W2, 512, 256, "y", 0),
    G1[2]: (W1, 512, 256, "y", 0),
    G2[3]: (W2, 768, 256, "y", 0),
    G1[3]: (W1, 768, 256, "x", 1),
    G2[4]: (W2, 1024, 256, "y", 0),
    G1[4]: (W1, 1024, 256, "y", 0),
    G2[5]: (W2, 1280, 256, "y", 0),
    G1[5]: (W1, 1280, 256, "x", 1),
    GO: (WO, 0, 384, "y", 1),
    GI[0]: (GI_ALL, 0, 384, "x", 0),
    GI[1]: (GI_ALL, 384, 384, "x", 0),
    GI[2]: (GI_ALL, 768, 256, "x", 0),
    GI[3]: (GI_ALL, 1024, 128, "x", 0),
}


def scatter_buffers(depth, rows):
    out = {}
    for name, (_, _, width, first, late) in SCATTER.items():
        second = (depth, 2, rows, width) if first == "y" else (2, depth, rows, width)
        out[name] = (
            pltpu.VMEM((2, depth, 2, rows, width), BF),
            pltpu.VMEM(second, BF),
            pltpu.VMEM((rows, width) if late else (depth, rows, width), BF),
            pltpu.VMEM((depth, 2, rows, width) if late else (depth, rows, width), BF),
        )
    return out


class Exchange:
    def __init__(self, depth, send_sem, recv_sem):
        row = lax.axis_index("dp")
        y = lax.axis_index("mp")
        c, x, z = row % 2, (row // 2) % 2, row // 4
        self.depth = depth
        self.c, self.x, self.y, self.z = c, x, y, z
        self.c1_, self.x1, self.y1 = 1 - c, 1 - x, 1 - y
        self.up = [(z + k) % depth for k in range(depth)]
        self.down = [(z + depth - k) % depth for k in range(depth)]
        self.peers = {
            ("c", 1): ((z * 2 + x) * 2 + self.c1_, y),
            ("x", 1): ((z * 2 + self.x1) * 2 + c, y),
            ("y", 1): (row, self.y1),
        }
        for k in range(1, depth):
            self.peers["z", k] = ((self.up[k] * 2 + x) * 2 + c, y)
        self.around = dict(self.peers)
        half = self.half = depth // 2
        near = z // half * half
        self.starts = (half - near, near)
        self.goal, self.origin = {}, {}
        for g in range(2):
            for j in range(g, half):
                self.goal[g, j] = self.starts[g] + (z + j) % half
                self.origin[g, j] = self.starts[g] + (z + half - j) % half
                self.peers[g, j] = ((self.goal[g, j] * 2 + x) * 2 + c, y)
        self.send_sem, self.recv_sem = send_sem, recv_sem
        self.keys, self.sent = {}, {}

    def greet(self):
        barrier = pltpu.get_barrier_semaphore()
        for peer in self.around.values():
            pl.semaphore_signal(barrier, inc=1, device_id=peer, device_id_type=MESH)
        pl.semaphore_wait(barrier, len(self.around))

    def slot(self, keys, key, most):
        k = keys.setdefault(key, len(keys))
        assert k < most, k
        return k

    def copy(self, key, sent, src, dst, axis, step=1):
        return pltpu.make_async_remote_copy(
            src_ref=src,
            dst_ref=dst,
            send_sem=self.send_sem.at[self.slot(self.sent, sent, N_SEND)],
            recv_sem=self.recv_sem.at[self.slot(self.keys, key, N_RECV)],
            device_id=self.peers[axis, step],
            device_id_type=MESH,
        )

    def send(self, key, sent, src, dst, axis, step=1):
        self.copy(key, sent, src, dst, axis, step).start()

    def recv(self, key, dst, axis="c", step=1):
        k = self.recv_sem.at[self.slot(self.keys, key, N_RECV)]
        pltpu.make_async_remote_copy(
            src_ref=dst,
            dst_ref=dst,
            send_sem=k,
            recv_sem=k,
            device_id=self.peers[axis, step],
            device_id_type=MESH,
        ).wait_recv()

    def gone(self, sent, ref):
        k = self.send_sem.at[self.slot(self.sent, sent, N_SEND)]
        pltpu.make_async_remote_copy(
            src_ref=ref,
            dst_ref=ref,
            send_sem=k,
            recv_sem=k,
            device_id=self.peers["c", 1],
            device_id_type=MESH,
        ).wait_send()


class Quiet:
    def __getattr__(self, name):
        return None


class Gather(Exchange):
    def use(self, refs):
        self.refs = refs

    def at(self, s, y, z, x, c):
        name, start, width, _, _ = GATHER[s]
        return self.refs[name].at[y, z, x, c, :, pl.ds(start, width)]

    def send(self, s, phase, k, src, axis, step=1):
        super().send((s, phase, k), (s, phase), src, src, axis, step)

    def begin(self, s):
        own = self.at(s, self.y, self.z, self.x, self.c)
        if GATHER[s][4]:
            self.across(s, 0)
        for k in range(1, self.depth):
            self.send(s, 0, k, own, "z", k)
        if not GATHER[s][4]:
            self.across(s, 0)

    def across(self, s, k):
        self.send(s, 1, k, self.at(s, self.y, self.down[k], self.x, self.c), GATHER[s][3])

    def zd(self, s, k):
        self.recv((s, 0, k), self.at(s, self.y, self.down[k], self.x, self.c))
        self.across(s, k)

    def beside(self, s, k):
        if GATHER[s][3] == "x":
            return self.at(s, self.y, self.down[k], self.x1, self.c)
        return self.at(s, self.y1, self.down[k], self.x, self.c)

    def pair(self, s, k):
        every = slice(None)
        if GATHER[s][3] == "x":
            return self.at(s, self.y, self.down[k], every, self.c)
        return self.at(s, every, self.down[k], self.x, self.c)

    def second(self, s, k):
        self.send(s, 2, 0, self.pair(s, k), "y" if GATHER[s][3] == "x" else "x")

    def pd(self, s, k):
        self.recv((s, 1, k), self.beside(s, k))
        self.second(s, k)

    def ad(self, s):
        self.recv((s, 1, 0), self.beside(s, 0))
        for k in range(1, self.depth):
            self.send(s, 0, k, self.beside(s, 0), "z", k)
        self.second(s, 0)

    def pz(self, s, k):
        self.recv((s, 0, k), self.pair(s, k))
        self.second(s, k)

    def parts(self, s, c):
        every = slice(None)
        if GATHER[s][3] == "x":
            return self.at(s, self.y, every, every, c), self.at(s, self.y1, every, every, c)
        return self.at(s, every, every, self.x, c), self.at(s, every, every, self.x1, c)

    def c1(self, s):
        self.send(s, 3, 0, self.parts(s, self.c)[0], "c")

    def qd(self, s):
        far = self.parts(s, self.c)[1]
        self.recv((s, 2, 0), far)
        self.send(s, 3, 1, far, "c")

    def f1(self, s):
        self.recv((s, 3, 0), self.parts(s, self.c1_)[0])

    def f2(self, s):
        self.recv((s, 3, 1), self.parts(s, self.c1_)[1])

    def land(self):
        every, most = slice(None), pl.ds(0, self.depth - 1)
        for s in GATHER:
            if GATHER[s][4]:
                self.gone((s, 0), self.at(s, every, most, self.x, self.c))
                self.gone((s, 1), self.at(s, self.y, self.z, self.x, self.c))
            else:
                self.gone((s, 0), self.at(s, self.y, most, self.x, self.c))
                self.gone((s, 1), self.at(s, self.y, every, self.x, self.c))
            self.gone((s, 2), self.at(s, self.y, every, every, self.c))
            self.gone((s, 3), self.at(s, every, every, every, self.c))


class Scatter(Exchange):
    def use(self, refs, buffers, finish):
        self.refs, self.buffers, self.finish = refs, buffers, finish

    def at(self, s, y, z, x, c):
        name, start, width, _, _ = SCATTER[s]
        return self.refs[name].at[y, z, x, c, :, pl.ds(start, width)]

    def send(self, s, phase, k, src, dst, axis, step=1):
        super().send((~s, phase, k), (~s, phase), src, dst, axis, step)

    def group(self, g):
        return pl.ds(self.starts[g], self.half)

    def s0(self, s):
        every = slice(None)
        away = self.at(s, every, every, every, self.c1_)
        self.send(s, 0, 0, away, self.buffers[s][0], "c")

    def landing(self, s, g):
        if SCATTER[s][3] == "y":
            return self.buffers[s][1].at[self.group(g)]
        return self.buffers[s][1].at[:, self.group(g)]

    def s1(self, s, g):
        every = slice(None)
        if g == 0:
            self.recv((~s, 0, 0), self.buffers[s][0])
        own = self.at(s, every, self.group(g), every, self.c)
        own[...] = own[...] + self.buffers[s][0][:, self.group(g)]
        if SCATTER[s][3] == "y":
            away = self.at(s, self.y1, self.group(g), every, self.c)
        else:
            away = self.at(s, every, self.group(g), self.x1, self.c)
        self.send(s, 1, g, away, self.landing(s, g), SCATTER[s][3])

    def both(self, s, z):
        every = slice(None)
        if SCATTER[s][3] == "y":
            return self.at(s, self.y, z, every, self.c)
        return self.at(s, every, z, self.x, self.c)

    def away(self, s, z):
        if SCATTER[s][3] == "y":
            return self.at(s, self.y, z, self.x1, self.c)
        return self.at(s, self.y1, z, self.x, self.c)

    def near(self, s, g):
        self.recv((~s, 1, g), self.landing(s, g))
        own = self.both(s, self.group(g))
        own[...] = own[...] + self.landing(s, g)[...]

    def s2(self, s, g):
        self.near(s, g)
        landing = self.buffers[s][2].at[self.group(g)]
        axis = "x" if SCATTER[s][3] == "y" else "y"
        self.send(s, 2, g, self.away(s, self.group(g)), landing, axis)

    def t2(self, s, g):
        self.near(s, g)
        for j in range(g, self.half):
            away = self.both(s, self.goal[g, j])
            self.send(s, 3, 0, away, self.buffers[s][3].at[self.z], g, j)

    def s3(self, s, g):
        got = self.buffers[s][2].at[self.group(g)]
        self.recv((~s, 2, g), got)
        own = self.at(s, self.y, self.group(g), self.x, self.c)
        own[...] = own[...] + got[...]
        for j in range(g, self.half):
            away = self.at(s, self.y, self.goal[g, j], self.x, self.c)
            self.send(s, 3, 0, away, self.buffers[s][3].at[self.z], g, j)

    def from_z(self, s, own):
        got = self.buffers[s][3]
        total = own[...].astype(F32)
        self.recv((~s, 3, 0), got.at[pl.ds(0, self.depth - 1)])
        for g in range(2):
            for j in range(g, self.half):
                total = total + got[self.origin[g, j]].astype(F32)
        return total

    def t3(self, s):
        own = self.both(s, self.z)
        own[...] = self.from_z(s, own).astype(BF)
        axis = "x" if SCATTER[s][3] == "y" else "y"
        self.send(s, 2, 0, self.away(s, self.z), self.buffers[s][2], axis)

    def s4(self, s):
        own = self.at(s, self.y, self.z, self.x, self.c)
        if SCATTER[s][4]:
            got = self.buffers[s][2]
            self.recv((~s, 2, 0), got)
            total = own[...].astype(F32) + got[...].astype(F32)
        else:
            total = self.from_z(s, own)
        self.finish(self, s, total)

    def land(self):
        every, most = slice(None), pl.ds(0, self.depth - 1)
        for s in SCATTER:
            self.gone((~s, 0), self.at(s, every, every, every, self.c))
            self.gone((~s, 1), self.at(s, self.y, every, every, self.c))
            if SCATTER[s][4]:
                self.gone((~s, 2), self.at(s, self.y, self.z, self.x, self.c))
                self.gone((~s, 3), self.at(s, every, most, self.x, self.c))
            else:
                self.gone((~s, 2), self.at(s, self.y, every, self.x, self.c))
                self.gone((~s, 3), self.at(s, self.y, most, self.x, self.c))
            if SCATTER[s][0] not in (W1, W2):
                self.gone((~s, 4), self.at(s, self.y, self.z, self.x, self.c))


def layer_kernel(comm, dims, names, *refs):
    r = dict(zip(names, refs))
    r.update(refs[len(names)])
    k = type("Refs", (), r)
    counts, gate, vectors, hidden, small = k.counts, k.gate, k.vectors, k.hidden, k.small
    tok, tok_t, wi, wo, w1, w2 = k.tok, k.tok_t, k.wi, k.wo, k.w1, k.w2
    mixed_t, mixed_n, attend, scores = k.mixed_t, k.mixed_n, k.attend, k.scores
    context_t, hat, scale, normed, acc = k.context_t, k.hat, k.scale, k.normed, k.acc

    def local_copy(j, src, dst):
        copy = pltpu.make_async_copy(src, dst, k.sems.at[j])
        copy.start()
        return copy

    depth, rows = dims
    matrices = {WI: wi, WO: wo, W1: w1, W2: w2}
    if comm:
        ag = Gather(depth, k.send_sem, k.recv_sem)
        ag.use(matrices)
        rs = Scatter(depth, k.send_sem, k.recv_sem)
        rs.keys, rs.sent = ag.keys, ag.sent
        own, other = ag.y, ag.y1
    else:
        ag = rs = Quiet()
        own, other = 0, 1

    def do(*steps):
        if comm:
            for step, *which in steps:
                step(*which)

    def attention(bias, mask, pattern, stage_i, stage_o, stage_f):

        def others():
            pairs = (k.counts_in, counts), (k.pattern_in, pattern), (k.gate_in, gate)
            pairs = pairs + ((k.tok_in, tok), (k.vectors_in, vectors), (k.hidden_in, hidden))
            return [local_copy(j, src, dst) for j, (src, dst) in enumerate(pairs)]

        if comm:
            y, z, x, c = ag.y, ag.z, ag.x, ag.c
            gets = [
                local_copy(
                    6 + kind,
                    k.wi_in.at[:, pl.ds(pl.multiple_of(kind * D + y * HD, 128), HD)],
                    stage_i.at[kind],
                )
                for kind in range(3)
            ]
            get_f = local_copy(9, k.wf_in, stage_f)
            get_o = local_copy(10, k.wo_in.at[:, pl.ds(pl.multiple_of(y * HD, 128), HD)], stage_o)
            more = others()
            ag.greet()
            for kind in range(3):
                gets[kind].wait()
            for g in range(PAIRS):
                for kind in range(3):
                    wi[y, z, x, c, :, pl.ds(g * PC + kind * 128, 128)] = stage_i[
                        kind, :, pl.ds(g * 128, 128)
                    ].astype(BF)
            for s in (WI_A, WI_B, WI_D, WI_C):
                ag.begin(s)
            get_o.wait()
            wo[y, z, x, c] = stage_o[...].astype(BF)
            get_f.wait()
            w1[y, z, x, c] = stage_f[0].astype(BF)
            w2[y, z, x, c] = stage_f[1].astype(BF)
            for s in GATHER:
                if s not in (WI_A, WI_B, WI_D, WI_C):
                    ag.begin(s)
        else:
            more = others()
            plain = [
                local_copy(6 + j, src, dst)
                for j, (src, dst) in enumerate(
                    ((k.wi_in, wi), (k.wo_in, wo), (k.w1_in, w1), (k.w2_in, w2))
                )
            ]
        for copy in more:
            copy.wait()
        if not comm:
            for copy in plain:
                copy.wait()

        def head(part, g, e):
            attend_head(part, g, e, mixed_t, mixed_n, bias, mask, scores, attend, context_t)

        tok_t[...] = tok[...].T
        build_mask(counts, pattern, mask)
        build_table(gate, k.table)
        build_bias(0, 3, k.table, bias)
        do((ag.pd, WI_A, 0), (ag.pd, WI_B, 0), (ag.pd, WI_D, 0))
        build_bias(3, 3, k.table, bias)
        do((ag.zd, WI_A, 1), (ag.pd, WO_A, 0), (ag.pd, WI_C, 0))
        build_bias(6, 3, k.table, bias)
        do((ag.zd, WI_A, 2))
        build_bias(9, 3, k.table, bias)
        do((ag.pd, W1_A, 0), (ag.zd, WI_A, 3), (ag.zd, WI_B, 1), (ag.pd, WI_A, 1), (ag.zd, WI_B, 2), (ag.pd, WI_A, 2), (ag.zd, WI_B, 3), (ag.zd, WI_D, 1), (ag.zd, WI_D, 2), (ag.pd, WI_B, 1), (ag.zd, WI_D, 3), (ag.zd, WI_C, 1), (ag.zd, WI_C, 2), (ag.zd, WI_C, 3), (ag.zd, WO_A, 1), (ag.pd, WI_B, 2), (ag.zd, WO_A, 2), (ag.pd, WI_A, 3), (ag.c1, WI_A), (ag.pd, W2_A, 0), (ag.zd, WO_A, 3), (ag.pd, WI_B, 3), (ag.c1, WI_B), (ag.pd, WI_D, 1), (ag.f1, WI_A))
        project_mixed(own, 0, tok, wi, mixed_t, mixed_n)
        do((ag.pd, WI_D, 2), (ag.pd, WI_D, 3), (ag.c1, WI_D), (ag.pd, WI_C, 1), (ag.pd, WI_C, 2), (ag.pd, WI_C, 3), (ag.c1, WI_C))
        head(own, 0, 0)
        do((ag.pd, WO_A, 1), (ag.zd, W1_A, 1), (ag.pd, W2_B, 0))
        head(own, 0, 1)
        do((ag.pd, WO_A, 2), (ag.qd, WI_A), (ag.zd, W1_A, 2), (ag.pd, WO_A, 3), (ag.c1, WO_A), (ag.qd, WI_B), (ag.qd, WI_C), (ag.zd, W1_A, 3), (ag.qd, WI_D), (ag.zd, W2_A, 1), (ag.f1, WI_B), (ag.f2, WI_B))
        project_mixed(own, 1, tok, wi, mixed_t, mixed_n)
        do((ag.zd, W2_A, 2))
        head(own, 1, 0)
        do((ag.zd, W2_A, 3))
        head(own, 1, 1)
        do((ag.pd, W1_A, 1), (ag.ad, W1_B), (ag.f2, WI_A))
        project_mixed(other, 0, tok, wi, mixed_t, mixed_n)
        do((ag.zd, W2_B, 1))
        head(other, 0, 0)
        head(other, 0, 1)
        do((ag.pd, W2_A, 1))
        project_mixed(other, 1, tok, wi, mixed_t, mixed_n)
        do((ag.pd, W1_A, 2), (ag.pd, W2_A, 2), (ag.pd, W2_A, 3), (ag.c1, W2_A))
        head(other, 1, 0)
        do((ag.zd, W2_B, 2))
        head(other, 1, 1)
        do((ag.qd, WO_A), (ag.zd, W2_B, 3), (ag.f1, WI_D), (ag.f2, WI_D), (ag.f1, WI_C))
        project_mixed(own, 2, tok, wi, mixed_t, mixed_n)
        head(own, 2, 0)
        do((ag.pd, W1_A, 3), (ag.c1, W1_A), (ag.ad, W2_C))
        head(own, 2, 1)
        do((ag.ad, W2_D), (ag.f2, WI_C))
        project_mixed(other, 2, tok, wi, mixed_t, mixed_n)
        head(other, 2, 0)
        head(other, 2, 1)

    pl.run_scoped(
        attention,
        pltpu.VMEM((H, 7, TILE, TILE), F32),
        pltpu.VMEM((WIN, WIN), F32),
        pltpu.VMEM((WIN, WIN), jnp.int32),
        pltpu.VMEM((3, rows, HD), F32),
        pltpu.VMEM((rows, HD), F32),
        pltpu.VMEM((2, rows, HF), F32),
    )

    def feed(active, slope, normed_t, grad, grad_t):
        get_cot = local_copy(0, k.cot_in, grad)

        if comm:
            rs.use(dict(matrices), k.buffers, None)

        def down(part, start, width):
            hidden_back(part, start, width, grad, grad_t, w2, active, slope, small)

        def up(part, start, width):
            hidden_back_up(part, start, width, normed_t, w1, slope, acc)

        do((ag.f1, WO_A), (ag.f2, WO_A))
        out_project(0, tok, context_t, wo, vectors, hat, scale, normed, normed_t)
        do((ag.pd, W2_B, 1))
        out_project(256, tok, context_t, wo, vectors, hat, scale, normed, normed_t)
        do((ag.qd, W2_A), (ag.pd, W2_B, 2), (ag.pz, W1_B, 1), (ag.qd, W1_A), (ag.pd, W2_B, 3), (ag.c1, W2_B), (ag.pz, W1_B, 2), (ag.pz, W1_B, 3), (ag.c1, W1_B), (ag.f1, W1_A), (ag.f2, W1_A))
        hidden_step(0, 0, normed, w1, hidden, active, slope)
        do((ag.pz, W2_C, 1))
        hidden_step(1, 0, normed, w1, hidden, active, slope)
        do((ag.pz, W2_C, 2))
        hidden_step(0, 1, normed, w1, hidden, active, slope)
        do((ag.pz, W2_C, 3), (ag.c1, W2_C), (ag.pz, W2_D, 1))
        hidden_step(1, 1, normed, w1, hidden, active, slope)
        do((ag.pz, W2_D, 2), (ag.pz, W2_D, 3), (ag.c1, W2_D), (ag.qd, W1_B), (ag.qd, W2_B), (ag.f1, W1_B), (ag.f2, W1_B))
        hidden_step(0, 2, normed, w1, hidden, active, slope)
        do((ag.qd, W2_D))
        hidden_step(1, 2, normed, w1, hidden, active, slope)
        do((ag.f1, W2_A), (ag.f2, W2_A), (ag.f1, W2_B), (ag.f2, W2_B))
        result_step(0, 0, 512, active, w2, acc)
        do((ag.qd, W2_C))
        result_step(1, 0, 512, active, w2, acc)
        result_step(0, 512, 512, active, w2, acc)
        result_step(1, 512, 512, active, w2, acc)
        do((ag.f1, W2_C), (ag.f2, W2_C), (ag.f1, W2_D), (ag.f2, W2_D))
        result_step(0, 1024, 512, active, w2, acc)
        result_step(1, 1024, 512, active, w2, acc)
        get_cot.wait()
        second_norm(0, acc, normed, grad, vectors, k.low, grad, grad_t, small)
        second_norm(256, acc, normed, grad, vectors, k.low, grad, grad_t, small)
        put_low = local_copy(7, k.low, k.low_out)
        if comm:
            ag.land()
        down(0, 0, 256)
        down(1, 0, 256)
        do((rs.s0, G2[0]))
        up(0, 0, 256)
        up(1, 0, 256)
        do((rs.s0, G1[0]))
        down(0, 256, 256)
        down(1, 256, 256)
        do((rs.s1, G2[0], 0), (rs.s1, G2[0], 1), (rs.s0, G2[1]))
        up(0, 256, 256)
        up(1, 256, 256)
        do((rs.s0, G1[1]), (rs.s1, G1[0], 0), (rs.s1, G1[0], 1))
        down(0, 512, 256)
        down(1, 512, 256)
        do((rs.s0, G2[2]), (rs.s1, G2[1], 0), (rs.s1, G2[1], 1))
        up(0, 512, 256)
        do((rs.s1, G1[1], 0), (rs.s1, G1[1], 1))
        up(1, 512, 256)
        do((rs.t2, G2[0], 0), (rs.s0, G1[2]))
        down(0, 768, 256)
        do((rs.s1, G2[2], 0), (rs.s1, G2[2], 1))
        down(1, 768, 256)
        do((rs.t2, G2[0], 1), (rs.s0, G2[3]))
        up(0, 768, 256)
        do((rs.s1, G1[2], 0), (rs.s1, G1[2], 1), (rs.s2, G2[1], 0))
        up(1, 768, 256)
        do((rs.s0, G1[3]))
        down(0, 1024, 256)
        do((rs.t2, G1[0], 0), (rs.s1, G2[3], 0))
        down(1, 1024, 256)
        do((rs.s2, G2[1], 1), (rs.s1, G2[3], 1), (rs.s0, G2[4]))
        up(0, 1024, 256)
        do((rs.s1, G1[3], 0), (rs.t2, G1[0], 1), (rs.s1, G1[3], 1))
        up(1, 1024, 256)
        do((rs.s0, G1[4]))
        down(0, 1280, 256)
        do((rs.s2, G2[2], 0), (rs.t3, G2[0]), (rs.s1, G2[4], 0))
        down(1, 1280, 256)
        do((rs.t2, G1[1], 0), (rs.s0, G2[5]))
        up(0, 1280, 256)
        do((rs.s2, G2[2], 1))
        up(1, 1280, 256)
        do((rs.s1, G1[4], 0), (rs.s0, G1[5]))
        put_low.wait()

    pl.run_scoped(
        feed,
        pltpu.VMEM((HALF * NCH, WIN, CH), BF),
        pltpu.VMEM((HALF * NCH, WIN, CH), BF),
        pltpu.VMEM((D, WIN), BF),
        pltpu.VMEM((WIN, D), BF),
        pltpu.VMEM((D, WIN), BF),
    )

    def finish(net, s, total):
        name, start, width, _, _ = SCATTER[s]
        here = pl.ds(start, width)
        if name in (W1, W2):
            k.box_f[0 if name == W1 else 1, :, here] = total
        else:
            box = k.box_i if name == GI_ALL else k.box_o
            box[net.y, :, here] = total.astype(BF)
            own = box.at[net.y, :, here]
            net.send(s, 4, 0, own, own, "y")

    def s5(s):
        name, start, width, _, _ = SCATTER[s]
        box = k.box_i if name == GI_ALL else k.box_o
        rs.recv((~s, 4, 0), box.at[rs.y1, :, pl.ds(start, width)])

    def spread(j, src, dst, axis, step=1):
        Exchange.send(rs, (SMALL, j), (SMALL, j), src, dst, axis, step)

    def m0():
        spread(0, small, k.line.at[0], "c")

    def m1():
        rs.recv((SMALL, 0), k.line.at[0])
        k.line[1] = small[...] + k.line[0]
        spread(1, k.line.at[1], k.line.at[2], "y")

    def m2():
        rs.recv((SMALL, 1), k.line.at[2])
        k.line[3] = k.line[1] + k.line[2]
        spread(2, k.line.at[3], k.line.at[4], "x")

    def m3():
        rs.recv((SMALL, 2), k.line.at[4])
        k.lines[rs.z] = k.line[3] + k.line[4]
        for j in range(1, depth):
            spread(3, k.lines.at[rs.z], k.lines.at[rs.z], "z", j)

    def m4():
        rs.recv((SMALL, 3), k.lines.at[pl.ds(0, depth - 1)])
        total = k.lines[0]
        for j in range(1, depth):
            total = total + k.lines[j]
        k.line[0] = total

    def last(grad_mixed_t, grad_context_t, gi):
        grad_low = normed
        if comm:
            rs.use({**matrices, GI_ALL: gi}, k.buffers, finish)

        def head(part, g, e):
            attend_back_head(
                part,
                g,
                e,
                mixed_t,
                mixed_n,
                attend,
                context_t,
                grad_context_t,
                scores,
                grad_mixed_t,
                small,
            )

        first_norm_back(0, acc, hat, scale, vectors, grad_low, small)
        do((rs.t2, G1[1], 1))
        first_norm_back(256, acc, hat, scale, vectors, grad_low, small)
        do((rs.s3, G2[1], 0), (rs.s2, G1[2], 0))
        context_back(0, grad_low, wo, grad_context_t)
        do((rs.s1, G1[4], 1), (rs.s3, G2[1], 1), (rs.s1, G1[5], 0), (rs.s1, G1[5], 1))
        context_back(256, grad_low, wo, grad_context_t)
        out_back(0, grad_low, context_t, wo)
        do((rs.s2, G1[2], 1))
        out_back(1, grad_low, context_t, wo)
        do((rs.s0, GO), (rs.t3, G1[0]), (rs.t2, G1[3], 0), (rs.s1, G2[5], 0))
        head(0, 0, 0)
        do((rs.s2, G2[3], 0))
        head(0, 0, 1)
        do((rs.t3, G1[1]), (rs.t2, G1[3], 1))
        project_back(0, 0, tok_t, grad_mixed_t, gi)
        do((rs.s1, GO, 0), (rs.s3, G2[2], 0), (rs.s2, G2[3], 1))
        head(1, 0, 0)
        do((rs.s3, G2[2], 1), (rs.s4, G2[0]), (rs.s4, G2[1]))
        head(1, 0, 1)
        do((rs.s3, G1[2], 0))
        project_back(1, 0, tok_t, grad_mixed_t, gi)
        do((rs.s1, GO, 1), (rs.s0, GI[0]), (rs.s2, G2[4], 0))
        head(0, 1, 0)
        do((rs.t2, G1[5], 0))
        head(0, 1, 1)
        do((rs.s2, G1[4], 0))
        project_back(0, 1, tok_t, grad_mixed_t, gi)
        do((rs.s1, GI[0], 0), (rs.s1, G2[5], 1), (rs.s1, GI[0], 1), (rs.t2, G1[5], 1))
        head(1, 1, 0)
        do((rs.s4, G2[2]), (rs.s4, G1[0]), (rs.s2, G1[4], 1), (rs.s3, G1[2], 1))
        head(1, 1, 1)
        do((rs.s3, G2[3], 0), (rs.t3, G1[3]), (rs.s1, G2[4], 1))
        project_back(1, 1, tok_t, grad_mixed_t, gi)
        do((rs.s2, G2[5], 0), (rs.s3, G2[3], 1), (rs.s0, GI[1]))
        head(0, 2, 0)
        do((rs.s4, G1[1]), (rs.s3, G2[4], 0))
        head(0, 2, 1)
        do((rs.s3, G1[4], 0))
        project_back(0, 2, tok_t, grad_mixed_t, gi)
        do((rs.s1, GI[1], 0))
        head(1, 2, 0)
        do((rs.t2, GO, 0), (rs.t3, G1[5]), (rs.s1, GI[1], 1), (rs.s4, G1[2]))
        head(1, 2, 1)
        do((m0,), (rs.s2, GI[0], 0))
        project_back(1, 2, tok_t, grad_mixed_t, gi)
        do((rs.s0, GI[2]), (rs.s0, GI[3]))
        input_back(0, grad_mixed_t, wi, hat)
        do((m1,), (rs.t2, GO, 1), (rs.s4, G2[3]))
        input_back(256, grad_mixed_t, wi, hat)
        put_grad = local_copy(0, hat, k.grad_out)
        do((rs.s3, G1[4], 1), (rs.s2, G2[5], 1), (rs.s4, G1[3]), (rs.s2, GI[0], 1), (rs.s1, GI[2], 0), (rs.s3, G2[5], 0), (rs.s1, GI[3], 0), (rs.s1, GI[2], 1), (rs.s4, G1[5]), (rs.s1, GI[3], 1), (rs.s3, GI[0], 0), (rs.s2, GI[1], 0), (rs.s2, G2[4], 1), (m2,), (rs.t3, GO), (rs.s2, GI[1], 1), (rs.s3, GI[0], 1), (rs.s4, G1[4]), (rs.s3, G2[5], 1), (rs.s3, GI[1], 0), (rs.s2, GI[2], 0), (rs.s3, GI[1], 1), (rs.s2, GI[3], 0), (rs.s4, GI[0]), (rs.s4, G2[5]), (rs.s2, GI[2], 1), (rs.s3, GI[2], 0), (rs.s3, GI[3], 0), (rs.s2, GI[3], 1), (s5, GI[0]), (rs.s3, G2[4], 1), (rs.s4, GI[1]), (rs.s3, GI[2], 1), (rs.s3, GI[3], 1), (m3,), (rs.s4, GO), (rs.s4, G2[4]), (s5, GI[1]), (rs.s4, GI[2]), (rs.s4, GI[3]), (s5, GO), (s5, GI[2]), (s5, GI[3]), (m4,))
        if comm:
            outs = ((k.line.at[0], k.small_out), (k.box_i, k.gi_out), (k.box_o, k.go_out))
            outs = outs + ((k.box_f, k.gf_out),)
        else:
            outs = ((small, k.small_out), (gi, k.gi_out), (wo, k.go_out))
            outs = outs + ((w1, k.g1_out), (w2, k.g2_out))
        outs = [local_copy(1 + j, src, dst) for j, (src, dst) in enumerate(outs)]
        if comm:
            rs.land()
            for j in range(3):
                rs.gone((SMALL, j), small)
            rs.gone((SMALL, 3), k.lines.at[pl.ds(0, depth - 1)])
        for copy in outs:
            copy.wait()
        put_grad.wait()

    pl.run_scoped(
        last,
        pltpu.VMEM((HALF, 3 * HD, WIN), BF),
        pltpu.VMEM((D, WIN), BF),
        pltpu.VMEM(wi.shape, BF),
    )


IN_NAMES = (
    "counts_in",
    "tok_in",
    "cot_in",
    "pattern_in",
    "gate_in",
    "vectors_in",
    "hidden_in",
    "wi_in",
    "wo_in",
    "w1_in",
    "w2_in",
)
OUT_NAMES_PLAIN = ("low_out", "grad_out", "small_out", "gi_out", "go_out", "g1_out", "g2_out")
OUT_NAMES = ("low_out", "grad_out", "small_out", "gi_out", "go_out", "gf_out")


def layer_call(comm, depth, rows, counts, tok, cot, pattern, gate, vectors, hidden, *weights):
    hbm = pl.BlockSpec(memory_space=pl.ANY)
    lead = (HALF, depth, 2, 2, rows) if comm else (HALF, 1, 1, 1, D)
    shapes = [lead + (n,) for n in (3 * HD, HD, HF, HF)]
    scratch = dict(
        wi=pltpu.VMEM(shapes[0], BF),
        wo=pltpu.VMEM(shapes[1], BF),
        w1=pltpu.VMEM(shapes[2], BF),
        w2=pltpu.VMEM(shapes[3], BF),
        tok=pltpu.VMEM((WIN, D), BF),
        low=pltpu.VMEM((WIN, D), BF),
        tok_t=pltpu.VMEM((D, WIN), BF),
        mixed_t=pltpu.VMEM((HALF, 3 * HD, WIN), BF),
        mixed_n=pltpu.VMEM((HALF, WIN, 2 * HD), BF),
        attend=pltpu.VMEM((H, WIN, WIN), BF),
        scores=pltpu.VMEM((WIN, WIN), F32),
        context_t=pltpu.VMEM((D, WIN), BF),
        hat=pltpu.VMEM((WIN, D), F32),
        scale=pltpu.VMEM((WIN, 128), F32),
        normed=pltpu.VMEM((WIN, D), BF),
        acc=pltpu.VMEM((WIN, D), F32),
        table=pltpu.VMEM((H, 2 * WIN), F32),
        small=pltpu.VMEM((R_ALL, 512), F32),
        counts=pltpu.SMEM((1, 4), jnp.int32),
        gate=pltpu.VMEM(gate.shape, F32),
        vectors=pltpu.VMEM(vectors.shape, F32),
        hidden=pltpu.VMEM(hidden.shape, F32),
        sems=pltpu.SemaphoreType.DMA((12,)),
    )
    outs = [
        jax.ShapeDtypeStruct((WIN, D), BF),
        jax.ShapeDtypeStruct((WIN, D), F32),
        jax.ShapeDtypeStruct((R_ALL, 512), F32),
    ]
    names = IN_NAMES
    if comm:
        outs += [
            jax.ShapeDtypeStruct((HALF, rows, 3 * HD), BF),
            jax.ShapeDtypeStruct((HALF, rows, HD), BF),
            jax.ShapeDtypeStruct((2, rows, HF), F32),
        ]
        out_specs = [hbm] * 6
        scratch.update(
            box_i=pltpu.VMEM((HALF, rows, 3 * HD), BF),
            box_o=pltpu.VMEM((HALF, rows, HD), BF),
            box_f=pltpu.VMEM((2, rows, HF), F32),
            line=pltpu.VMEM((5, R_ALL, 512), F32),
            lines=pltpu.VMEM((depth, R_ALL, 512), F32),
            buffers=scatter_buffers(depth, rows),
            send_sem=pltpu.SemaphoreType.DMA((N_SEND,)),
            recv_sem=pltpu.SemaphoreType.DMA((N_RECV,)),
        )
        names = names[:9] + ("wf_in",)
        params = dict(collective_id=0, has_side_effects=True)
    else:
        weights = [w.reshape(s) for w, s in zip(weights, shapes)]
        outs += [jax.ShapeDtypeStruct(s, BF) for s in shapes]
        out_specs = [hbm] * 7
        params = {}
    names = names + (OUT_NAMES if comm else OUT_NAMES_PLAIN)
    return pl.pallas_call(
        functools.partial(layer_kernel, comm, (depth, rows), names),
        out_shape=outs,
        in_specs=[hbm] * (7 + len(weights)),
        out_specs=out_specs,
        scratch_shapes=[scratch],
        compiler_params=pltpu.CompilerParams(vmem_limit_bytes=62 * 2**20, **params),
        cost_estimate=pl.CostEstimate(
            flops=25 * 10**9, bytes_accessed=40 * 2**20, transcendentals=10**7
        ),
        name="layer",
    )(counts, tok, cot, pattern, gate, vectors, hidden, *weights)


def update_kernel(*refs):
    ins, outs, (low, grad, small, gi, go, gf, *held), sems = refs[:24], refs[24:44], refs[44:-1], refs[-1]

    def copy(j, src, dst):
        one = pltpu.make_async_copy(src, dst, sems.at[j])
        one.start()
        return one

    passing = [copy(0, ins[0], low), copy(1, ins[1], grad)]
    sums = [copy(2 + j, src, dst) for j, (src, dst) in enumerate(zip(ins[2:6], (small, gi, go, gf)))]
    gets = {}
    for j in (6, 7, 8, 0, 1, 2, 3, 4, 5) + tuple(range(9, 18)):
        gets[j] = copy(6 + j, ins[6 + j], held[j])
    puts = []
    for j in range(2):
        passing[j].wait()
        puts.append(copy(j, (low, grad)[j], outs[j]))
    for one in sums:
        one.wait()

    def step(n, here, value):
        p, m, v = (held[3 * n + j] for j in range(3))
        p[here], m[here], v[here] = adam_step(p[here], m[here], v[here], value, RATES[n])

    def ready(n):
        for j in range(3 * n, 3 * n + 3):
            gets[j].wait()

    def done(n):
        for j in range(3 * n, 3 * n + 3):
            puts.append(copy(6 + j, held[j], outs[2 + j]))

    every = slice(None)
    ready(2)
    for part in range(2):
        for c in range(HF // HD):
            here = (part, every, pl.ds(c * HD, HD))
            step(2, here, gf[here])
    done(2)
    ready(0)
    for kind in range(3):
        for part in range(HALF):
            value = [gi[part, :, pl.ds(g * PC + kind * 128, 128)] for g in range(PAIRS)]
            value = jnp.concatenate(value, axis=1).astype(F32)
            step(0, (every, pl.ds(kind * D + part * HD, HD)), value)
    done(0)
    ready(1)
    for part in range(HALF):
        step(1, (every, pl.ds(part * HD, HD)), go[part].astype(F32))
    done(1)
    for n in (3, 4, 5):
        ready(n)
    value = jnp.concatenate([small[pl.ds(0, H), :], small[pl.ds(H, H), :]], axis=1)
    value = value[:, : held[9].shape[1]] / (1.0 + jnp.exp(held[9][...]))
    step(3, (every, every), value)
    value = [small[pl.ds(R_VEC, 5), :], small[pl.ds(R_VEC + 5, 5), pl.ds(0, 256)]]
    step(4, (every, every), jnp.concatenate(value, axis=1))
    value = [
        small[pl.ds(R_HID + j, 1), pl.ds(q * 128, 128)]
        for j in range(HALF * NCH)
        for q in range(CH // 128)
    ]
    step(5, (every, every), jnp.concatenate(value, axis=0))
    for n in (3, 4, 5):
        done(n)
    for one in puts:
        one.wait()


def update_call(layer, weights):
    hbm = pl.BlockSpec(memory_space=pl.ANY)
    ins = list(layer) + list(weights)
    shapes = [jax.ShapeDtypeStruct(x.shape, x.dtype) for x in list(layer[:2]) + list(weights)]
    return pl.pallas_call(
        update_kernel,
        out_shape=shapes,
        in_specs=[hbm] * len(ins),
        out_specs=[hbm] * len(shapes),
        scratch_shapes=[pltpu.VMEM(x.shape, x.dtype) for x in ins]
        + [pltpu.SemaphoreType.DMA((len(ins),))],
        compiler_params=pltpu.CompilerParams(vmem_limit_bytes=62 * 2**20),
        cost_estimate=pl.CostEstimate(flops=10**7, bytes_accessed=12 * 10**6, transcendentals=10**6),
        name="update",
    )(*ins)


def collect(w, width):
    return w.reshape(D, HALF, width).transpose(1, 0, 2)


def local(
    tokens,
    cotangent,
    seq_counts,
    pattern,
    project_in,
    project_in_first,
    project_in_second,
    project_out,
    project_out_first,
    project_out_second,
    feed_forward,
    feed_forward_first,
    feed_forward_second,
    gate_logits,
    gate_logits_first,
    gate_logits_second,
    norm_vectors,
    norm_vectors_first,
    norm_vectors_second,
    hidden_bias,
    hidden_bias_first,
    hidden_bias_second,
):
    rows = project_in.shape[0]
    groups, halves = lax.axis_size("dp"), lax.axis_size("mp")
    comm = halves == HALF and groups == 16 and rows % 16 == 0
    shared = (
        seq_counts,
        tokens,
        cotangent,
        pattern,
        gate_logits,
        norm_vectors,
        hidden_bias.reshape(FF // 128, 128),
    )
    if comm:
        layer = layer_call(True, groups // 4, rows, *shared, project_in, project_out, feed_forward)
        weights = (
            project_in,
            project_in_first,
            project_in_second,
            project_out,
            project_out_first,
            project_out_second,
            feed_forward,
            feed_forward_first,
            feed_forward_second,
            gate_logits,
            gate_logits_first,
            gate_logits_second,
            norm_vectors,
            norm_vectors_first,
            norm_vectors_second,
        )
        flat = [w.reshape(-1, 128) for w in (hidden_bias, hidden_bias_first, hidden_bias_second)]
        outs = update_call(layer, weights + tuple(flat))
        return tuple(outs[:-3]) + tuple(w.reshape(FF) for w in outs[-3:])

    whole_in = lax.all_gather(project_in.astype(BF), "dp", axis=0, tiled=True)
    whole_out = lax.all_gather(project_out.astype(BF), "dp", axis=0, tiled=True)
    pair = lax.all_gather(feed_forward.astype(BF), "dp", axis=1, tiled=True)
    pair = lax.all_gather(pair, "mp", axis=2, tiled=True)
    wi = whole_in.reshape(D, 3, HALF, PAIRS, 128).transpose(2, 0, 3, 1, 4)
    wi = wi.reshape(HALF, D, 3 * HD)
    layer_out, input_grad, small, gi, go, g1, g2 = layer_call(
        False,
        1,
        D,
        *shared,
        wi,
        collect(whole_out, HD),
        collect(pair[0], HF),
        collect(pair[1], HF),
    )
    gi = gi.reshape(HALF, D, PAIRS, 3, 128).transpose(1, 3, 0, 2, 4).reshape(D, 3 * D)
    go = go.reshape(HALF, D, HD).transpose(1, 0, 2).reshape(D, D)
    gf = jnp.stack([g.reshape(HALF, D, HF).transpose(1, 0, 2).reshape(D, FF) for g in (g1, g2)])
    sum_in = lax.psum_scatter(gi, "dp", scatter_dimension=0, tiled=True)
    sum_in = lax.psum(sum_in.astype(F32), "mp")
    sum_out = lax.psum_scatter(go, "dp", scatter_dimension=0, tiled=True)
    sum_out = lax.psum(sum_out.astype(F32), "mp")
    sum_pair = lax.psum_scatter(gf, "dp", scatter_dimension=1, tiled=True)
    sum_pair = lax.psum_scatter(sum_pair, "mp", scatter_dimension=2, tiled=True).astype(F32)
    small = lax.psum(small, ("dp", "mp"))
    sum_gate = jnp.concatenate([small[:H], small[H : 2 * H]], axis=1)[:, : 2 * WIN - 1]
    sum_gate = sum_gate * jax.nn.sigmoid(-gate_logits)
    sum_vectors = jnp.concatenate(
        [small[R_VEC : R_VEC + 5], small[R_VEC + 5 : R_VEC + 10, :256]], axis=1
    )
    sum_bias = small[R_HID:].reshape(FF)
    outs = [layer_out, input_grad]
    for weight, first, second, grad, rate in (
        (project_in, project_in_first, project_in_second, sum_in, RATES[0]),
        (project_out, project_out_first, project_out_second, sum_out, RATES[1]),
        (feed_forward, feed_forward_first, feed_forward_second, sum_pair, RATES[2]),
        (gate_logits, gate_logits_first, gate_logits_second, sum_gate, RATES[3]),
        (norm_vectors, norm_vectors_first, norm_vectors_second, sum_vectors, RATES[4]),
        (hidden_bias, hidden_bias_first, hidden_bias_second, sum_bias, RATES[5]),
    ):
        outs.extend(adam_step(weight, first, second, grad, rate))
    return tuple(outs)


def solution(mesh):
    rows, whole = P(("dp", "mp"), None), P()
    split, pair = P("dp", None), P(None, "dp", "mp")
    return jax.shard_map(
        local,
        mesh=mesh,
        in_specs=(rows, rows, rows, whole) + (split,) * 6 + (pair,) * 3 + (whole,) * 9,
        out_specs=(rows, rows) + (split,) * 6 + (pair,) * 3 + (whole,) * 9,
        check_vma=False,
    )
```

```python
import functools
import math

import jax
import jax.numpy as jnp
from jax import lax
from jax.experimental import pallas as pl
from jax.experimental.pallas import tpu as pltpu
from jax.sharding import PartitionSpec as P

D = 768
H = 12
HEAD = 64
FF = 3072
TILE = 128
WIN = 512
STEP = 10
HALF = 2
HD = D // HALF
HF = FF // HALF
CH = 512
NCH = HF // CH
PAIRS = HD // 128
PC = 3 * 128

NORM_EPS = 1e-12
BETA_ONE = 0.9
BETA_TWO = 0.999
ADAM_EPS = 1e-08
DECAY = 0.01
MASKED = -1e30
RATES = (0.03, 0.25, 0.03, 1.0, 0.2, 0.2)

F32 = jnp.float32
BF = jnp.bfloat16
NN = ((1,), (0,))
NT = ((1,), (1,))
R_VEC, R_HID, R_ALL = 24, 34, 40


def dot(a, b, dims=NN):
    return lax.dot_general(a, b, (dims, ((), ())), preferred_element_type=F32)


def adam_step(weight, first, second, grad, rate):
    first = BETA_ONE * first + (1.0 - BETA_ONE) * grad
    second = BETA_TWO * second + (1.0 - BETA_TWO) * grad * grad
    update = first / (1.0 - BETA_ONE**STEP) / (jnp.sqrt(second / (1.0 - BETA_TWO**STEP)) + ADAM_EPS)
    return (weight - rate * (update + DECAY * weight), first, second)


def cols(ref, part, start, size):
    block = ref[part, :, :, :, :, pl.ds(start, size)]
    return block.reshape(D, size)


def put_cols(ref, part, start, value):
    shape = ref.shape[1:5] + (value.shape[1],)
    ref[part, :, :, :, :, pl.ds(start, value.shape[1])] = value.reshape(shape)


def build_mask(counts, pattern, mask):
    two, three, four = counts[0, 1], counts[0, 2], counts[0, 3]
    after_four = 4 * four
    after_three = after_four + 3 * three
    after_two = after_three + 2 * two
    tiles = WIN // TILE
    begins = []
    for tile in range(tiles):
        in_three = after_four + jnp.where(tile - after_four >= 3, 3, 0)
        in_two = after_three + jnp.where(tile - after_three >= 2, 2, 0)
        begin = jnp.where(
            tile < after_four,
            0,
            jnp.where(tile < after_three, in_three, jnp.where(tile < after_two, in_two, tile)),
        )
        begins.append(begin)
    starts = [
        [jnp.where(begins[tile] == b, 1.0, 0.0) for b in range(tile + 1)] for tile in range(tiles)
    ]
    for i in range(tiles):
        for j in range(tiles):
            allowed = jnp.zeros((TILE, TILE), F32)
            for b in range(min(i, j) + 1):
                block = pattern[pl.ds((i - b) * TILE, TILE), pl.ds((j - b) * TILE, TILE)]
                allowed = allowed + block.astype(F32) * (starts[i][b] * starts[j][b])
            allowed = jnp.where(allowed > 0.5, 0.0, MASKED)
            mask[pl.ds(j * TILE, TILE), pl.ds(i * TILE, TILE)] = allowed.T


def build_table(gate, table):
    x = gate[...]
    x = jnp.minimum(x, 0.0) - jnp.log(1.0 + jnp.exp(-jnp.abs(x)))
    table[:, pl.ds(0, x.shape[1])] = x


def build_bias(first, count, table, bias):
    def one(h, _):
        row = table[pl.ds(h, 1), :]
        for d in range(7):
            part = jnp.broadcast_to(row[:, d * TILE : d * TILE + 2 * TILE], (TILE, 2 * TILE))
            bias[h, d] = pltpu.roll(part, TILE + 1, 1, stride=1, stride_axis=0)[:, :TILE]
        return 0

    lax.fori_loop(first, first + count, one, 0)


def project_mixed(part, g, tok, wi, mixed_t, mixed_n):
    value = dot(tok[...], cols(wi, part, g * PC, PC)).astype(BF)
    mixed_n[part, :, pl.ds(g * 256, 256)] = value[:, 128:]
    query = value[:, :128] * jnp.asarray(HEAD**-0.5, BF)
    mixed_t[part, pl.ds(g * PC, PC), :] = jnp.concatenate([query.T, value[:, 128:].T], axis=0)


def pad_head(value, e):
    zero = jnp.zeros_like(value)
    return jnp.concatenate([value, zero] if e == 0 else [zero, value], axis=0)


def attend_head(part, g, e, mixed_t, mixed_n, bias, mask, scores, attend, context_t):
    keys = mixed_n[part, :, pl.ds(g * 256, 128)]
    row = g * PC + e * HEAD
    h = part * (H // HALF) + g * 2 + e
    query = pad_head(mixed_t[part, pl.ds(row, HEAD), :], e)
    scores[...] = dot(keys, query)
    for i in range(WIN // TILE):
        here = pl.ds(i * TILE, TILE)
        table = jnp.concatenate([bias[h, i - j + 3] for j in range(WIN // TILE)], axis=0)
        s = scores[:, here] + (table + mask[:, here])
        top = jnp.max(s, axis=0, keepdims=True)
        s = jnp.exp(s - top)
        total = jnp.sum(s, axis=0, keepdims=True)
        attend[h, :, here] = (s * (1.0 / total)).astype(BF)
    values = mixed_t[part, pl.ds(row + 256, HEAD), :]
    out = dot(values, attend[h])
    context_t[pl.ds(pl.multiple_of(h * HEAD, HEAD), HEAD), :] = out.astype(BF)


def norm_of(value):
    mean = jnp.mean(value, axis=-1, keepdims=True)
    center = value - mean
    spread = jnp.mean(center * center, axis=-1, keepdims=True)
    scale = lax.rsqrt(spread + NORM_EPS)
    return center * scale, scale


def norm_back(grad, hat, scale, gain):
    g = grad * gain
    first = jnp.mean(g, axis=-1, keepdims=True)
    second = jnp.mean(g * hat, axis=-1, keepdims=True)
    return (
        scale * (g - first - hat * second),
        jnp.sum(grad * hat, axis=0, keepdims=True),
        jnp.sum(grad, axis=0, keepdims=True),
    )


ROWS = 256


def out_project(r, tok, context_t, wo, vectors, hat, scale, normed, normed_t):
    here = pl.ds(r, ROWS)
    context = context_t[:, here].T
    branch = jnp.concatenate(
        [dot(context, cols(wo, part, 0, HD)) for part in range(HALF)], axis=1
    )
    h, s = norm_of(tok[here, :].astype(F32) + branch)
    hat[here, :] = h
    scale[here, :] = jnp.broadcast_to(s, (ROWS, 128))
    low = (h * vectors[0:1, :] + vectors[1:2, :]).astype(BF)
    normed[here, :] = low
    normed_t[:, here] = low.T


def hidden_step(part, c, normed, w1, hidden, active, slope):
    j = part * NCH + c
    bias = [hidden[pl.ds(j * (CH // 128) + q, 1), :] for q in range(CH // 128)]
    before = dot(normed[...], cols(w1, part, c * CH, CH)) + jnp.concatenate(bias, axis=1)
    half = 0.5 + 0.5 * lax.erf(before * math.sqrt(0.5))
    active[j] = (before * half).astype(BF)
    bell = jnp.exp(-0.5 * before * before) * (1.0 / math.sqrt(2 * math.pi))
    slope[j] = (half + before * bell).astype(BF)


def result_step(part, start, width, active, w2, acc):
    j, here = part * NCH + start // CH, pl.ds(start % CH, width)
    value = dot(active[j, :, here], cols(w2, part, start, width), NT)
    acc[...] = value if part == 0 and start == 0 else acc[...] + value


def second_norm(r, acc, normed, cot, vectors, low_out, grad, grad_t, small):
    here = pl.ds(r, ROWS)
    total = normed[here, :].astype(F32) + acc[here, :] + vectors[4:5, :]
    hat, scale = norm_of(total)
    low_out[here, :] = (hat * vectors[2:3, :] + vectors[3:4, :]).astype(BF)
    value, gain, shift = norm_back(cot[here, :].astype(F32), hat, scale, vectors[2:3, :])
    acc[here, :] = value
    low = value.astype(BF)
    grad[here, :] = low
    grad_t[:, here] = low.T
    sums = (gain, shift, jnp.sum(value, axis=0, keepdims=True))
    for k in range(3):
        put_vector(small, 2 + k, sums[k], r > 0)


def put_vector(small, k, value, more):
    one, two = pl.ds(R_VEC + k, 1), pl.ds(R_VEC + 5 + k, 1)
    left = value[:, :512]
    right = jnp.concatenate([value[:, 512:], jnp.zeros((1, 256), F32)], axis=1)
    small[one, :] = small[one, :] + left if more else left
    small[two, :] = small[two, :] + right if more else right


def hidden_back(part, start, width, grad, grad_t, w2, active, slope, small):
    j, here = part * NCH + start // CH, pl.ds(start % CH, width)
    before = dot(grad[...], cols(w2, part, start, width)) * slope[j, :, here].astype(F32)
    before = before.astype(BF)
    slope[j, :, here] = before
    put_cols(w2, part, start, dot(grad_t[...], active[j, :, here]).astype(BF))
    small[pl.ds(R_HID + j, 1), here] = jnp.sum(before.astype(F32), axis=0, keepdims=True)


def hidden_back_up(part, start, width, normed_t, w1, slope, acc):
    before = slope[part * NCH + start // CH, :, pl.ds(start % CH, width)]
    acc[...] += dot(before, cols(w1, part, start, width), NT)
    put_cols(w1, part, start, dot(normed_t[...], before).astype(BF))


def first_norm_back(r, acc, hat, scale, vectors, grad_low, small):
    here = pl.ds(r, ROWS)
    grad = acc[here, :].astype(BF).astype(F32)
    value, gain, shift = norm_back(grad, hat[here, :], scale[here, 0:1], vectors[0:1, :])
    hat[here, :] = value
    grad_low[here, :] = value.astype(BF)
    for k, total in enumerate((gain, shift)):
        put_vector(small, k, total, r > 0)


def context_back(r, grad_low, wo, grad_context_t):
    here = pl.ds(r, ROWS)
    low = grad_low[here, :]
    value = 0.0
    for part in range(HALF):
        value = value + dot(cols(wo, part, 0, HD), low[:, part * HD : (part + 1) * HD], NT)
    grad_context_t[:, here] = value.astype(BF)


def out_back(part, grad_low, context_t, go):
    low = grad_low[:, pl.ds(part * HD, HD)]
    put_cols(go, part, 0, dot(context_t[...], low).astype(BF))


def attend_back_head(part, g, e, mixed_t, mixed_n, attend, context_t, grad_context_t, scores, grad_mixed_t, small):
    values = mixed_n[part, :, pl.ds(g * 256 + 128, 128)]
    turn = lax.broadcasted_iota(jnp.int32, (TILE, TILE), 0) + lax.broadcasted_iota(
        jnp.int32, (TILE, TILE), 1
    )
    turn = jnp.where(turn == TILE - 1, 1.0, 0.0).astype(BF)
    row = g * PC + e * HEAD
    h = part * (H // HALF) + g * 2 + e
    place = pl.ds(pl.multiple_of(h * HEAD, HEAD), HEAD)
    grad_c = grad_context_t[place, :]
    inner = jnp.sum(
        grad_c.astype(F32) * context_t[place, :].astype(F32), axis=0, keepdims=True
    )
    scores[...] = dot(values, pad_head(grad_c, e))
    tiles = [0.0] * 7
    for i in range(WIN // TILE):
        here = pl.ds(i * TILE, TILE)
        ds = attend[h, :, here].astype(F32) * (scores[:, here] - inner[:, i * TILE : (i + 1) * TILE])
        for j in range(WIN // TILE):
            d = i - j + 3
            tiles[d] = tiles[d] + ds[j * TILE : (j + 1) * TILE, :]
        scores[:, here] = ds
    low = scores[...].astype(BF)
    key = mixed_t[part, pl.ds(row + 128, HEAD), :]
    query = mixed_t[part, pl.ds(row, HEAD), :]
    gq = dot(key, low) * (HEAD**-0.5)
    gk = dot(query, low, NT)
    gv = dot(grad_c, attend[h], NT)
    grad_mixed_t[part, pl.ds(row, HEAD), :] = gq.astype(BF)
    grad_mixed_t[part, pl.ds(row + 128, HEAD), :] = gk.astype(BF)
    grad_mixed_t[part, pl.ds(row + 256, HEAD), :] = gv.astype(BF)
    blocks = [0.0] * 8
    turned = dot(turn, jnp.concatenate([t.astype(BF) for t in tiles], axis=1))
    for d in range(7):
        wide = turned[:, d * TILE : (d + 1) * TILE]
        wide = jnp.concatenate([wide, jnp.zeros((TILE, TILE), F32)], axis=1)
        wide = pltpu.roll(wide, 0, 1, stride=1, stride_axis=0)
        line = jnp.sum(wide, axis=0, keepdims=True)
        blocks[d] = blocks[d] + line[:, :TILE]
        blocks[d + 1] = blocks[d + 1] + line[:, TILE:]
    small[pl.ds(h, 1), :] = jnp.concatenate(blocks[:4], axis=1)
    small[pl.ds(H + h, 1), :] = jnp.concatenate(blocks[4:], axis=1)


def project_back(part, g, tok_t, grad_mixed_t, gi):
    value = dot(tok_t[...], grad_mixed_t[part, pl.ds(g * PC, PC), :], NT)
    put_cols(gi, part, g * PC, value.astype(BF))


def input_back(r, grad_mixed_t, wi, hat):
    here = pl.ds(r, ROWS)
    value = 0.0
    for part in range(HALF):
        value = value + dot(cols(wi, part, 0, 3 * HD), grad_mixed_t[part, :, here])
    hat[here, :] = hat[here, :] + value.T


MESH = pl.DeviceIdType.MESH
WI, WO, W1, W2, GI_ALL = range(5)
WI_A, WO_A, W1_A, W2_A, WI_B, WI_D, WI_C, W2_B, W1_B, W2_C, W2_D = range(11)
GATHER = {
    WI_A: (WI, 0, 512, "x", 0),
    WO_A: (WO, 0, 384, "x", 0),
    W1_A: (W1, 0, 1024, "y", 0),
    W2_A: (W2, 0, 256, "x", 0),
    WI_B: (WI, 512, 384, "y", 0),
    WI_D: (WI, 896, 128, "y", 0),
    WI_C: (WI, 1024, 128, "x", 0),
    W2_B: (W2, 256, 768, "y", 0),
    W1_B: (W1, 1024, 512, "x", 1),
    W2_C: (W2, 1024, 384, "x", 1),
    W2_D: (W2, 1408, 128, "y", 1),
}
G2 = range(0, 6)
G1 = range(6, 12)
GO = 12
GI = range(13, 17)
SMALL = 17
SCATTER = {
    G2[0]: (W2, 0, 256, "x", 1),
    G1[0]: (W1, 0, 256, "x", 1),
    G2[1]: (W2, 256, 256, "y", 0),
    G1[1]: (W1, 256, 256, "x", 1),
    G2[2]: (W2, 512, 256, "y", 0),
    G1[2]: (W1, 512, 256, "y", 0),
    G2[3]: (W2, 768, 256, "y", 0),
    G1[3]: (W1, 768, 256, "x", 1),
    G2[4]: (W2, 1024, 256, "y", 0),
    G1[4]: (W1, 1024, 256, "y", 0),
    G2[5]: (W2, 1280, 256, "y", 0),
    G1[5]: (W1, 1280, 256, "x", 1),
    GO: (WO, 0, 384, "y", 1),
    GI[0]: (GI_ALL, 0, 384, "x", 0),
    GI[1]: (GI_ALL, 384, 384, "x", 0),
    GI[2]: (GI_ALL, 768, 256, "x", 0),
    GI[3]: (GI_ALL, 1024, 128, "x", 0),
}


N_SEND, N_RECV = len(GATHER) + len(SCATTER) + 9, 206


def scatter_buffers(depth, rows):
    out = {}
    for name, (_, _, width, first, late) in SCATTER.items():
        second = (depth, 2, rows, width) if first == "y" else (2, depth, rows, width)
        out[name] = (
            pltpu.VMEM((2, depth, 2, rows, width), BF),
            pltpu.VMEM(second, BF),
            pltpu.VMEM((rows, width) if late else (depth, rows, width), BF),
            pltpu.VMEM((depth, 2, rows, width) if late else (depth, rows, width), BF),
        )
    return out


class Exchange:
    def __init__(self, depth, send_sem, recv_sem):
        row = lax.axis_index("dp")
        y = lax.axis_index("mp")
        c, x, z = row % 2, (row // 2) % 2, row // 4
        self.depth = depth
        self.c, self.x, self.y, self.z = c, x, y, z
        self.c1_, self.x1, self.y1 = 1 - c, 1 - x, 1 - y
        self.up = [(z + k) % depth for k in range(depth)]
        self.down = [(z + depth - k) % depth for k in range(depth)]
        self.peers = {
            ("c", 1): ((z * 2 + x) * 2 + self.c1_, y),
            ("x", 1): ((z * 2 + self.x1) * 2 + c, y),
            ("y", 1): (row, self.y1),
        }
        for k in range(1, depth):
            self.peers["z", k] = ((self.up[k] * 2 + x) * 2 + c, y)
        self.around = dict(self.peers)
        half = self.half = depth // 2
        near = z // half * half
        self.starts = (half - near, near)
        self.goal, self.origin = {}, {}
        for g in range(2):
            for j in range(g, half):
                self.goal[g, j] = self.starts[g] + (z + j) % half
                self.origin[g, j] = self.starts[g] + (z + half - j) % half
                self.peers[g, j] = ((self.goal[g, j] * 2 + x) * 2 + c, y)
        self.send_sem, self.recv_sem = send_sem, recv_sem
        self.keys, self.sent = {}, {}

    def greet(self):
        barrier = pltpu.get_barrier_semaphore()
        for peer in self.around.values():
            pl.semaphore_signal(barrier, inc=1, device_id=peer, device_id_type=MESH)
        pl.semaphore_wait(barrier, len(self.around))

    def slot(self, keys, key, most):
        k = keys.setdefault(key, len(keys))
        assert k < most, k
        return k

    def copy(self, key, sent, src, dst, axis, step=1):
        return pltpu.make_async_remote_copy(
            src_ref=src,
            dst_ref=dst,
            send_sem=self.send_sem.at[self.slot(self.sent, sent, N_SEND)],
            recv_sem=self.recv_sem.at[self.slot(self.keys, key, N_RECV)],
            device_id=self.peers[axis, step],
            device_id_type=MESH,
        )

    def send(self, key, sent, src, dst, axis, step=1):
        self.copy(key, sent, src, dst, axis, step).start()

    def recv(self, key, dst, axis="c", step=1):
        k = self.recv_sem.at[self.slot(self.keys, key, N_RECV)]
        pltpu.make_async_remote_copy(
            src_ref=dst,
            dst_ref=dst,
            send_sem=k,
            recv_sem=k,
            device_id=self.peers[axis, step],
            device_id_type=MESH,
        ).wait_recv()

    def amount(self, width):
        high, wide = 16 * (8 * self.depth - 1), 8 * self.rows
        return self.room.at[pl.ds(0, width // 128), pl.ds(0, high), pl.ds(0, wide)]

    def gone(self, sent, ref):
        k = self.send_sem.at[self.slot(self.sent, sent, N_SEND)]
        pltpu.make_async_remote_copy(
            src_ref=ref,
            dst_ref=ref,
            send_sem=k,
            recv_sem=k,
            device_id=self.peers["c", 1],
            device_id_type=MESH,
        ).wait_send()


class Quiet:
    def __getattr__(self, name):
        return None


class Gather(Exchange):
    def use(self, refs):
        self.refs = refs

    def at(self, s, y, z, x, c):
        name, start, width, _, _ = GATHER[s]
        return self.refs[name].at[y, z, x, c, :, pl.ds(start, width)]

    def send(self, s, phase, k, src, axis, step=1):
        super().send((s, phase, k), (s, 0), src, src, axis, step)

    def begin(self, s):
        own = self.at(s, self.y, self.z, self.x, self.c)
        if GATHER[s][4]:
            self.across(s, 0)
        for k in range(1, self.depth):
            self.send(s, 0, k, own, "z", k)
        if not GATHER[s][4]:
            self.across(s, 0)

    def across(self, s, k):
        self.send(s, 1, k, self.at(s, self.y, self.down[k], self.x, self.c), GATHER[s][3])

    def zd(self, s, k):
        self.recv((s, 0, k), self.at(s, self.y, self.down[k], self.x, self.c))
        self.across(s, k)

    def beside(self, s, k):
        if GATHER[s][3] == "x":
            return self.at(s, self.y, self.down[k], self.x1, self.c)
        return self.at(s, self.y1, self.down[k], self.x, self.c)

    def pair(self, s, k):
        every = slice(None)
        if GATHER[s][3] == "x":
            return self.at(s, self.y, self.down[k], every, self.c)
        return self.at(s, every, self.down[k], self.x, self.c)

    def second(self, s, k):
        self.send(s, 2, 0, self.pair(s, k), "y" if GATHER[s][3] == "x" else "x")

    def pd(self, s, k):
        self.recv((s, 1, k), self.beside(s, k))
        self.second(s, k)

    def ad(self, s):
        self.recv((s, 1, 0), self.beside(s, 0))
        for k in range(1, self.depth):
            self.send(s, 0, k, self.beside(s, 0), "z", k)
        self.second(s, 0)

    def pz(self, s, k):
        self.recv((s, 0, k), self.pair(s, k))
        self.second(s, k)

    def parts(self, s, c):
        every = slice(None)
        if GATHER[s][3] == "x":
            return self.at(s, self.y, every, every, c), self.at(s, self.y1, every, every, c)
        return self.at(s, every, every, self.x, c), self.at(s, every, every, self.x1, c)

    def c1(self, s):
        self.send(s, 3, 0, self.parts(s, self.c)[0], "c")

    def qd(self, s):
        far = self.parts(s, self.c)[1]
        self.recv((s, 2, 0), far)
        self.send(s, 3, 1, far, "c")

    def f1(self, s):
        self.recv((s, 3, 0), self.parts(s, self.c1_)[0])

    def f2(self, s):
        self.recv((s, 3, 1), self.parts(s, self.c1_)[1])

    def land(self):
        for s in GATHER:
            self.gone((s, 0), self.amount(GATHER[s][2]))


class Scatter(Exchange):
    def use(self, refs, buffers, finish):
        self.refs, self.buffers, self.finish = refs, buffers, finish

    def at(self, s, y, z, x, c):
        name, start, width, _, _ = SCATTER[s]
        return self.refs[name].at[y, z, x, c, :, pl.ds(start, width)]

    def send(self, s, phase, k, src, dst, axis, step=1):
        super().send((~s, phase, k), (~s, phase // 4), src, dst, axis, step)

    def group(self, g):
        return pl.ds(self.starts[g], self.half)

    def s0(self, s):
        every = slice(None)
        away = self.at(s, every, every, every, self.c1_)
        self.send(s, 0, 0, away, self.buffers[s][0], "c")

    def landing(self, s, g):
        if SCATTER[s][3] == "y":
            return self.buffers[s][1].at[self.group(g)]
        return self.buffers[s][1].at[:, self.group(g)]

    def s1(self, s, g):
        every = slice(None)
        if g == 0:
            self.recv((~s, 0, 0), self.buffers[s][0])
        own = self.at(s, every, self.group(g), every, self.c)
        own[...] = own[...] + self.buffers[s][0][:, self.group(g)]
        if SCATTER[s][3] == "y":
            away = self.at(s, self.y1, self.group(g), every, self.c)
        else:
            away = self.at(s, every, self.group(g), self.x1, self.c)
        self.send(s, 1, g, away, self.landing(s, g), SCATTER[s][3])

    def both(self, s, z):
        every = slice(None)
        if SCATTER[s][3] == "y":
            return self.at(s, self.y, z, every, self.c)
        return self.at(s, every, z, self.x, self.c)

    def away(self, s, z):
        if SCATTER[s][3] == "y":
            return self.at(s, self.y, z, self.x1, self.c)
        return self.at(s, self.y1, z, self.x, self.c)

    def near(self, s, g):
        self.recv((~s, 1, g), self.landing(s, g))
        own = self.both(s, self.group(g))
        own[...] = own[...] + self.landing(s, g)[...]

    def s2(self, s, g):
        self.near(s, g)
        landing = self.buffers[s][2].at[self.group(g)]
        axis = "x" if SCATTER[s][3] == "y" else "y"
        self.send(s, 2, g, self.away(s, self.group(g)), landing, axis)

    def t2(self, s, g):
        self.near(s, g)
        for j in range(g, self.half):
            away = self.both(s, self.goal[g, j])
            self.send(s, 3, 0, away, self.buffers[s][3].at[self.z], g, j)

    def s3(self, s, g):
        got = self.buffers[s][2].at[self.group(g)]
        self.recv((~s, 2, g), got)
        own = self.at(s, self.y, self.group(g), self.x, self.c)
        own[...] = own[...] + got[...]
        for j in range(g, self.half):
            away = self.at(s, self.y, self.goal[g, j], self.x, self.c)
            self.send(s, 3, 0, away, self.buffers[s][3].at[self.z], g, j)

    def from_z(self, s, own):
        got = self.buffers[s][3]
        total = own[...].astype(F32)
        self.recv((~s, 3, 0), got.at[pl.ds(0, self.depth - 1)])
        for g in range(2):
            for j in range(g, self.half):
                total = total + got[self.origin[g, j]].astype(F32)
        return total

    def t3(self, s):
        own = self.both(s, self.z)
        own[...] = self.from_z(s, own).astype(BF)
        axis = "x" if SCATTER[s][3] == "y" else "y"
        self.send(s, 2, 0, self.away(s, self.z), self.buffers[s][2], axis)

    def s4(self, s):
        own = self.at(s, self.y, self.z, self.x, self.c)
        if SCATTER[s][4]:
            got = self.buffers[s][2]
            self.recv((~s, 2, 0), got)
            total = own[...].astype(F32) + got[...].astype(F32)
        else:
            total = self.from_z(s, own)
        self.finish(self, s, total)

    def land(self):
        for s in SCATTER:
            self.gone((~s, 0), self.amount(SCATTER[s][2]))
            if SCATTER[s][0] not in (W1, W2):
                self.gone((~s, 1), self.at(s, self.y, self.z, self.x, self.c))


def layer_kernel(comm, dims, names, *refs):
    r = dict(zip(names, refs))
    r.update(refs[len(names)])
    k = type("Refs", (), r)
    counts, gate, vectors, hidden, small = k.counts, k.gate, k.vectors, k.hidden, k.small
    tok, tok_t, wi, wo, w1, w2 = k.tok, k.tok_t, k.wi, k.wo, k.w1, k.w2
    mixed_t, mixed_n, attend, scores = k.mixed_t, k.mixed_n, k.attend, k.scores
    context_t, hat, scale, normed, acc = k.context_t, k.hat, k.scale, k.normed, k.acc

    def local_copy(j, src, dst):
        copy = pltpu.make_async_copy(src, dst, k.sems.at[j])
        copy.start()
        return copy

    depth, rows = dims
    matrices = {WI: wi, WO: wo, W1: w1, W2: w2}
    if comm:
        ag = Gather(depth, k.send_sem, k.recv_sem)
        ag.use(matrices)
        ag.room, ag.rows = attend, rows
        rs = Scatter(depth, k.send_sem, k.recv_sem)
        rs.keys, rs.sent = ag.keys, ag.sent
        rs.room, rs.rows = attend, rows
        own, other = ag.y, ag.y1
    else:
        ag = rs = Quiet()
        own, other = 0, 1

    def do(*steps):
        if comm:
            for step, *which in steps:
                step(*which)

    def attention(bias, mask, pattern, stage_i, stage_o, stage_f):

        def others():
            pairs = (k.counts_in, counts), (k.pattern_in, pattern), (k.gate_in, gate)
            pairs = pairs + ((k.tok_in, tok), (k.vectors_in, vectors), (k.hidden_in, hidden))
            return [local_copy(j, src, dst) for j, (src, dst) in enumerate(pairs)]

        if comm:
            y, z, x, c = ag.y, ag.z, ag.x, ag.c
            gets = [
                local_copy(
                    6 + kind,
                    k.wi_in.at[:, pl.ds(pl.multiple_of(kind * D + y * HD, 128), HD)],
                    stage_i.at[kind],
                )
                for kind in range(3)
            ]
            get_f = local_copy(9, k.wf_in, stage_f)
            get_o = local_copy(10, k.wo_in.at[:, pl.ds(pl.multiple_of(y * HD, 128), HD)], stage_o)
            more = others()
            ag.greet()
            for kind in range(3):
                gets[kind].wait()
            for g in range(PAIRS):
                for kind in range(3):
                    wi[y, z, x, c, :, pl.ds(g * PC + kind * 128, 128)] = stage_i[
                        kind, :, pl.ds(g * 128, 128)
                    ].astype(BF)
            for s in (WI_A, WI_B, WI_D, WI_C):
                ag.begin(s)
            get_o.wait()
            wo[y, z, x, c] = stage_o[...].astype(BF)
            get_f.wait()
            w1[y, z, x, c] = stage_f[0].astype(BF)
            w2[y, z, x, c] = stage_f[1].astype(BF)
            for s in GATHER:
                if s not in (WI_A, WI_B, WI_D, WI_C):
                    ag.begin(s)
        else:
            more = others()
            plain = [
                local_copy(6 + j, src, dst)
                for j, (src, dst) in enumerate(
                    ((k.wi_in, wi), (k.wo_in, wo), (k.w1_in, w1), (k.w2_in, w2))
                )
            ]
        for copy in more:
            copy.wait()
        if not comm:
            for copy in plain:
                copy.wait()

        def head(part, g, e):
            attend_head(part, g, e, mixed_t, mixed_n, bias, mask, scores, attend, context_t)

        tok_t[...] = tok[...].T
        build_mask(counts, pattern, mask)
        build_table(gate, k.table)
        build_bias(0, 3, k.table, bias)
        do((ag.pd, WI_A, 0), (ag.pd, WI_B, 0), (ag.pd, WI_D, 0))
        build_bias(3, 3, k.table, bias)
        do((ag.zd, WI_A, 1), (ag.pd, WO_A, 0), (ag.pd, WI_C, 0))
        build_bias(6, 3, k.table, bias)
        do((ag.zd, WI_A, 2))
        build_bias(9, 3, k.table, bias)
        do((ag.pd, W1_A, 0), (ag.zd, WI_A, 3), (ag.zd, WI_B, 1), (ag.pd, WI_A, 1), (ag.zd, WI_B, 2), (ag.pd, WI_A, 2), (ag.zd, WI_B, 3), (ag.zd, WI_D, 1), (ag.zd, WI_D, 2), (ag.pd, WI_B, 1), (ag.zd, WI_D, 3), (ag.zd, WI_C, 1), (ag.zd, WI_C, 2), (ag.zd, WI_C, 3), (ag.zd, WO_A, 1), (ag.pd, WI_B, 2), (ag.zd, WO_A, 2), (ag.pd, WI_A, 3), (ag.c1, WI_A), (ag.pd, W2_A, 0), (ag.zd, WO_A, 3), (ag.pd, WI_B, 3), (ag.c1, WI_B), (ag.pd, WI_D, 1), (ag.f1, WI_A))
        project_mixed(own, 0, tok, wi, mixed_t, mixed_n)
        do((ag.pd, WI_D, 2), (ag.pd, WI_D, 3), (ag.c1, WI_D), (ag.pd, WI_C, 1), (ag.pd, WI_C, 2), (ag.pd, WI_C, 3), (ag.c1, WI_C))
        head(own, 0, 0)
        do((ag.pd, WO_A, 1), (ag.zd, W1_A, 1), (ag.pd, W2_B, 0))
        head(own, 0, 1)
        do((ag.pd, WO_A, 2), (ag.qd, WI_A), (ag.zd, W1_A, 2), (ag.pd, WO_A, 3), (ag.c1, WO_A), (ag.qd, WI_B), (ag.qd, WI_C), (ag.zd, W1_A, 3), (ag.qd, WI_D), (ag.zd, W2_A, 1), (ag.f1, WI_B), (ag.f2, WI_B))
        project_mixed(own, 1, tok, wi, mixed_t, mixed_n)
        do((ag.zd, W2_A, 2))
        head(own, 1, 0)
        do((ag.zd, W2_A, 3))
        head(own, 1, 1)
        do((ag.pd, W1_A, 1), (ag.ad, W1_B), (ag.f2, WI_A))
        project_mixed(other, 0, tok, wi, mixed_t, mixed_n)
        do((ag.zd, W2_B, 1))
        head(other, 0, 0)
        head(other, 0, 1)
        do((ag.pd, W2_A, 1))
        project_mixed(other, 1, tok, wi, mixed_t, mixed_n)
        do((ag.pd, W1_A, 2), (ag.pd, W2_A, 2), (ag.pd, W2_A, 3), (ag.c1, W2_A))
        head(other, 1, 0)
        do((ag.zd, W2_B, 2))
        head(other, 1, 1)
        do((ag.qd, WO_A), (ag.zd, W2_B, 3), (ag.f1, WI_D), (ag.f2, WI_D), (ag.f1, WI_C))
        project_mixed(own, 2, tok, wi, mixed_t, mixed_n)
        head(own, 2, 0)
        do((ag.pd, W1_A, 3), (ag.c1, W1_A), (ag.ad, W2_C))
        head(own, 2, 1)
        do((ag.ad, W2_D), (ag.f2, WI_C))
        project_mixed(other, 2, tok, wi, mixed_t, mixed_n)
        head(other, 2, 0)
        head(other, 2, 1)

    pl.run_scoped(
        attention,
        pltpu.VMEM((H, 7, TILE, TILE), F32),
        pltpu.VMEM((WIN, WIN), F32),
        pltpu.VMEM((WIN, WIN), jnp.int32),
        pltpu.VMEM((3, rows, HD), F32),
        pltpu.VMEM((rows, HD), F32),
        pltpu.VMEM((2, rows, HF), F32),
    )

    def feed(active, slope, normed_t, grad, grad_t):
        get_cot = local_copy(0, k.cot_in, grad)

        if comm:
            rs.use(dict(matrices), k.buffers, None)

        def down(part, start, width):
            hidden_back(part, start, width, grad, grad_t, w2, active, slope, small)

        def up(part, start, width):
            hidden_back_up(part, start, width, normed_t, w1, slope, acc)

        do((ag.f1, WO_A), (ag.f2, WO_A))
        out_project(0, tok, context_t, wo, vectors, hat, scale, normed, normed_t)
        do((ag.pd, W2_B, 1))
        out_project(256, tok, context_t, wo, vectors, hat, scale, normed, normed_t)
        do((ag.qd, W2_A), (ag.pd, W2_B, 2), (ag.pz, W1_B, 1), (ag.qd, W1_A), (ag.pd, W2_B, 3), (ag.c1, W2_B), (ag.pz, W1_B, 2), (ag.pz, W1_B, 3), (ag.c1, W1_B), (ag.f1, W1_A), (ag.f2, W1_A))
        hidden_step(0, 0, normed, w1, hidden, active, slope)
        do((ag.pz, W2_C, 1))
        hidden_step(1, 0, normed, w1, hidden, active, slope)
        do((ag.pz, W2_C, 2))
        hidden_step(0, 1, normed, w1, hidden, active, slope)
        do((ag.pz, W2_C, 3), (ag.c1, W2_C), (ag.pz, W2_D, 1))
        hidden_step(1, 1, normed, w1, hidden, active, slope)
        do((ag.pz, W2_D, 2), (ag.pz, W2_D, 3), (ag.c1, W2_D), (ag.qd, W1_B), (ag.qd, W2_B), (ag.f1, W1_B), (ag.f2, W1_B))
        hidden_step(0, 2, normed, w1, hidden, active, slope)
        do((ag.qd, W2_D))
        hidden_step(1, 2, normed, w1, hidden, active, slope)
        do((ag.f1, W2_A), (ag.f2, W2_A), (ag.f1, W2_B), (ag.f2, W2_B))
        result_step(0, 0, 512, active, w2, acc)
        do((ag.qd, W2_C))
        result_step(1, 0, 512, active, w2, acc)
        result_step(0, 512, 512, active, w2, acc)
        result_step(1, 512, 512, active, w2, acc)
        do((ag.f1, W2_C), (ag.f2, W2_C), (ag.f1, W2_D), (ag.f2, W2_D))
        result_step(0, 1024, 512, active, w2, acc)
        result_step(1, 1024, 512, active, w2, acc)
        get_cot.wait()
        second_norm(0, acc, normed, grad, vectors, k.low, grad, grad_t, small)
        second_norm(256, acc, normed, grad, vectors, k.low, grad, grad_t, small)
        put_low = local_copy(7, k.low, k.low_out)
        if comm:
            ag.land()
        down(0, 0, 256)
        down(1, 0, 256)
        do((rs.s0, G2[0]))
        up(0, 0, 256)
        up(1, 0, 256)
        do((rs.s0, G1[0]))
        down(0, 256, 256)
        down(1, 256, 256)
        do((rs.s1, G2[0], 0), (rs.s1, G2[0], 1), (rs.s0, G2[1]))
        up(0, 256, 256)
        up(1, 256, 256)
        do((rs.s0, G1[1]), (rs.s1, G1[0], 0), (rs.s1, G1[0], 1))
        down(0, 512, 256)
        down(1, 512, 256)
        do((rs.s0, G2[2]), (rs.s1, G2[1], 0), (rs.s1, G2[1], 1))
        up(0, 512, 256)
        do((rs.s1, G1[1], 0), (rs.s1, G1[1], 1))
        up(1, 512, 256)
        do((rs.t2, G2[0], 0), (rs.s0, G1[2]))
        down(0, 768, 256)
        do((rs.s1, G2[2], 0), (rs.s1, G2[2], 1))
        down(1, 768, 256)
        do((rs.t2, G2[0], 1), (rs.s0, G2[3]))
        up(0, 768, 256)
        do((rs.s1, G1[2], 0), (rs.s1, G1[2], 1), (rs.s2, G2[1], 0))
        up(1, 768, 256)
        do((rs.s0, G1[3]))
        down(0, 1024, 256)
        do((rs.t2, G1[0], 0), (rs.s1, G2[3], 0))
        down(1, 1024, 256)
        do((rs.s2, G2[1], 1), (rs.s1, G2[3], 1), (rs.s0, G2[4]))
        up(0, 1024, 256)
        do((rs.s1, G1[3], 0), (rs.t2, G1[0], 1), (rs.s1, G1[3], 1))
        up(1, 1024, 256)
        do((rs.s0, G1[4]))
        down(0, 1280, 256)
        do((rs.s2, G2[2], 0), (rs.t3, G2[0]), (rs.s1, G2[4], 0))
        down(1, 1280, 256)
        do((rs.t2, G1[1], 0), (rs.s0, G2[5]))
        up(0, 1280, 256)
        do((rs.s2, G2[2], 1))
        up(1, 1280, 256)
        do((rs.s1, G1[4], 0), (rs.s0, G1[5]))
        put_low.wait()

    pl.run_scoped(
        feed,
        pltpu.VMEM((HALF * NCH, WIN, CH), BF),
        pltpu.VMEM((HALF * NCH, WIN, CH), BF),
        pltpu.VMEM((D, WIN), BF),
        pltpu.VMEM((WIN, D), BF),
        pltpu.VMEM((D, WIN), BF),
    )

    def finish(net, s, total):
        name, start, width, _, _ = SCATTER[s]
        here = pl.ds(start, width)
        if name in (W1, W2):
            k.box_f[0 if name == W1 else 1, :, here] = total
        else:
            box = k.box_i if name == GI_ALL else k.box_o
            box[net.y, :, here] = total.astype(BF)
            own = box.at[net.y, :, here]
            net.send(s, 4, 0, own, own, "y")

    def s5(s):
        name, start, width, _, _ = SCATTER[s]
        box = k.box_i if name == GI_ALL else k.box_o
        rs.recv((~s, 4, 0), box.at[rs.y1, :, pl.ds(start, width)])

    def spread(j, src, dst, axis, step=1):
        Exchange.send(rs, (SMALL, j), (SMALL, j), src, dst, axis, step)

    def m0():
        spread(0, small, k.line.at[0], "c")

    def m1():
        rs.recv((SMALL, 0), k.line.at[0])
        k.line[1] = small[...] + k.line[0]
        spread(1, k.line.at[1], k.line.at[2], "y")

    def m2():
        rs.recv((SMALL, 1), k.line.at[2])
        k.line[3] = k.line[1] + k.line[2]
        spread(2, k.line.at[3], k.line.at[4], "x")

    def m3():
        rs.recv((SMALL, 2), k.line.at[4])
        k.lines[rs.z] = k.line[3] + k.line[4]
        for j in range(1, depth):
            spread(3, k.lines.at[rs.z], k.lines.at[rs.z], "z", j)

    def m4():
        rs.recv((SMALL, 3), k.lines.at[pl.ds(0, depth - 1)])
        total = k.lines[0]
        for j in range(1, depth):
            total = total + k.lines[j]
        k.line[0] = total

    def last(grad_mixed_t, grad_context_t, gi):
        grad_low = normed
        if comm:
            rs.use({**matrices, GI_ALL: gi}, k.buffers, finish)

        def head(part, g, e):
            attend_back_head(
                part,
                g,
                e,
                mixed_t,
                mixed_n,
                attend,
                context_t,
                grad_context_t,
                scores,
                grad_mixed_t,
                small,
            )

        first_norm_back(0, acc, hat, scale, vectors, grad_low, small)
        do((rs.t2, G1[1], 1))
        first_norm_back(256, acc, hat, scale, vectors, grad_low, small)
        do((rs.s3, G2[1], 0), (rs.s2, G1[2], 0))
        context_back(0, grad_low, wo, grad_context_t)
        do((rs.s1, G1[4], 1), (rs.s3, G2[1], 1), (rs.s1, G1[5], 0), (rs.s1, G1[5], 1))
        context_back(256, grad_low, wo, grad_context_t)
        out_back(0, grad_low, context_t, wo)
        do((rs.s2, G1[2], 1))
        out_back(1, grad_low, context_t, wo)
        do((rs.s0, GO), (rs.t3, G1[0]), (rs.t2, G1[3], 0), (rs.s1, G2[5], 0))
        head(0, 0, 0)
        do((rs.s2, G2[3], 0))
        head(0, 0, 1)
        do((rs.t3, G1[1]), (rs.t2, G1[3], 1))
        project_back(0, 0, tok_t, grad_mixed_t, gi)
        do((rs.s1, GO, 0), (rs.s3, G2[2], 0), (rs.s2, G2[3], 1))
        head(1, 0, 0)
        do((rs.s3, G2[2], 1), (rs.s4, G2[0]), (rs.s4, G2[1]))
        head(1, 0, 1)
        do((rs.s3, G1[2], 0))
        project_back(1, 0, tok_t, grad_mixed_t, gi)
        do((rs.s1, GO, 1), (rs.s0, GI[0]), (rs.s2, G2[4], 0))
        head(0, 1, 0)
        do((rs.t2, G1[5], 0))
        head(0, 1, 1)
        do((rs.s2, G1[4], 0))
        project_back(0, 1, tok_t, grad_mixed_t, gi)
        do((rs.s1, GI[0], 0), (rs.s1, G2[5], 1), (rs.s1, GI[0], 1), (rs.t2, G1[5], 1))
        head(1, 1, 0)
        do((rs.s4, G2[2]), (rs.s4, G1[0]), (rs.s2, G1[4], 1), (rs.s3, G1[2], 1))
        head(1, 1, 1)
        do((rs.s3, G2[3], 0), (rs.t3, G1[3]), (rs.s1, G2[4], 1))
        project_back(1, 1, tok_t, grad_mixed_t, gi)
        do((rs.s2, G2[5], 0), (rs.s3, G2[3], 1), (rs.s0, GI[1]))
        head(0, 2, 0)
        do((rs.s4, G1[1]), (rs.s3, G2[4], 0))
        head(0, 2, 1)
        do((rs.s3, G1[4], 0))
        project_back(0, 2, tok_t, grad_mixed_t, gi)
        do((rs.s1, GI[1], 0))
        head(1, 2, 0)
        do((rs.t2, GO, 0), (rs.t3, G1[5]), (rs.s1, GI[1], 1), (rs.s4, G1[2]))
        head(1, 2, 1)
        do((m0,), (rs.s2, GI[0], 0))
        project_back(1, 2, tok_t, grad_mixed_t, gi)
        do((rs.s0, GI[2]), (rs.s0, GI[3]))
        input_back(0, grad_mixed_t, wi, hat)
        do((m1,), (rs.t2, GO, 1), (rs.s4, G2[3]))
        input_back(256, grad_mixed_t, wi, hat)
        put_grad = local_copy(0, hat, k.grad_out)
        do((rs.s3, G1[4], 1), (rs.s2, G2[5], 1), (rs.s4, G1[3]), (rs.s2, GI[0], 1), (rs.s1, GI[2], 0), (rs.s3, G2[5], 0), (rs.s1, GI[3], 0), (rs.s1, GI[2], 1), (rs.s4, G1[5]), (rs.s1, GI[3], 1), (rs.s3, GI[0], 0), (rs.s2, GI[1], 0), (rs.s2, G2[4], 1), (m2,), (rs.t3, GO), (rs.s2, GI[1], 1), (rs.s3, GI[0], 1), (rs.s4, G1[4]), (rs.s3, G2[5], 1), (rs.s3, GI[1], 0), (rs.s2, GI[2], 0), (rs.s3, GI[1], 1), (rs.s2, GI[3], 0), (rs.s4, GI[0]), (rs.s4, G2[5]), (rs.s2, GI[2], 1), (rs.s3, GI[2], 0), (rs.s3, GI[3], 0), (rs.s2, GI[3], 1), (s5, GI[0]), (rs.s3, G2[4], 1), (rs.s4, GI[1]), (rs.s3, GI[2], 1), (rs.s3, GI[3], 1), (m3,), (rs.s4, GO), (rs.s4, G2[4]), (s5, GI[1]), (rs.s4, GI[2]), (rs.s4, GI[3]), (s5, GO), (s5, GI[2]), (s5, GI[3]), (m4,))
        if comm:
            outs = ((k.line.at[0], k.small_out), (k.box_i, k.gi_out), (k.box_o, k.go_out))
            outs = outs + ((k.box_f, k.gf_out),)
        else:
            outs = ((small, k.small_out), (gi, k.gi_out), (wo, k.go_out))
            outs = outs + ((w1, k.g1_out), (w2, k.g2_out))
        outs = [local_copy(1 + j, src, dst) for j, (src, dst) in enumerate(outs)]
        if comm:
            rs.land()
            for j in range(3):
                rs.gone((SMALL, j), small)
            rs.gone((SMALL, 3), k.lines.at[pl.ds(0, depth - 1)])
        for copy in outs:
            copy.wait()
        put_grad.wait()

    pl.run_scoped(
        last,
        pltpu.VMEM((HALF, 3 * HD, WIN), BF),
        pltpu.VMEM((D, WIN), BF),
        pltpu.VMEM(wi.shape, BF),
    )


IN_NAMES = (
    "counts_in",
    "tok_in",
    "cot_in",
    "pattern_in",
    "gate_in",
    "vectors_in",
    "hidden_in",
    "wi_in",
    "wo_in",
    "w1_in",
    "w2_in",
)
OUT_NAMES_PLAIN = ("low_out", "grad_out", "small_out", "gi_out", "go_out", "g1_out", "g2_out")
OUT_NAMES = ("low_out", "grad_out", "small_out", "gi_out", "go_out", "gf_out")


def layer_call(comm, depth, rows, counts, tok, cot, pattern, gate, vectors, hidden, *weights):
    hbm = pl.BlockSpec(memory_space=pl.ANY)
    lead = (HALF, depth, 2, 2, rows) if comm else (HALF, 1, 1, 1, D)
    shapes = [lead + (n,) for n in (3 * HD, HD, HF, HF)]
    scratch = dict(
        wi=pltpu.VMEM(shapes[0], BF),
        wo=pltpu.VMEM(shapes[1], BF),
        w1=pltpu.VMEM(shapes[2], BF),
        w2=pltpu.VMEM(shapes[3], BF),
        tok=pltpu.VMEM((WIN, D), BF),
        low=pltpu.VMEM((WIN, D), BF),
        tok_t=pltpu.VMEM((D, WIN), BF),
        mixed_t=pltpu.VMEM((HALF, 3 * HD, WIN), BF),
        mixed_n=pltpu.VMEM((HALF, WIN, 2 * HD), BF),
        attend=pltpu.VMEM((H, WIN, WIN), BF),
        scores=pltpu.VMEM((WIN, WIN), F32),
        context_t=pltpu.VMEM((D, WIN), BF),
        hat=pltpu.VMEM((WIN, D), F32),
        scale=pltpu.VMEM((WIN, 128), F32),
        normed=pltpu.VMEM((WIN, D), BF),
        acc=pltpu.VMEM((WIN, D), F32),
        table=pltpu.VMEM((H, 2 * WIN), F32),
        small=pltpu.VMEM((R_ALL, 512), F32),
        counts=pltpu.SMEM((1, 4), jnp.int32),
        gate=pltpu.VMEM(gate.shape, F32),
        vectors=pltpu.VMEM(vectors.shape, F32),
        hidden=pltpu.VMEM(hidden.shape, F32),
        sems=pltpu.SemaphoreType.DMA((12,)),
    )
    outs = [
        jax.ShapeDtypeStruct((WIN, D), BF),
        jax.ShapeDtypeStruct((WIN, D), F32),
        jax.ShapeDtypeStruct((R_ALL, 512), F32),
    ]
    names = IN_NAMES
    if comm:
        outs += [
            jax.ShapeDtypeStruct((HALF, rows, 3 * HD), BF),
            jax.ShapeDtypeStruct((HALF, rows, HD), BF),
            jax.ShapeDtypeStruct((2, rows, HF), F32),
        ]
        out_specs = [hbm] * 6
        scratch.update(
            box_i=pltpu.VMEM((HALF, rows, 3 * HD), BF),
            box_o=pltpu.VMEM((HALF, rows, HD), BF),
            box_f=pltpu.VMEM((2, rows, HF), F32),
            line=pltpu.VMEM((5, R_ALL, 512), F32),
            lines=pltpu.VMEM((depth, R_ALL, 512), F32),
            buffers=scatter_buffers(depth, rows),
            send_sem=pltpu.SemaphoreType.DMA((N_SEND,)),
            recv_sem=pltpu.SemaphoreType.DMA((N_RECV,)),
        )
        names = names[:9] + ("wf_in",)
        params = dict(collective_id=0, has_side_effects=True)
    else:
        weights = [w.reshape(s) for w, s in zip(weights, shapes)]
        outs += [jax.ShapeDtypeStruct(s, BF) for s in shapes]
        out_specs = [hbm] * 7
        params = {}
    names = names + (OUT_NAMES if comm else OUT_NAMES_PLAIN)
    return pl.pallas_call(
        functools.partial(layer_kernel, comm, (depth, rows), names),
        out_shape=outs,
        in_specs=[hbm] * (7 + len(weights)),
        out_specs=out_specs,
        scratch_shapes=[scratch],
        compiler_params=pltpu.CompilerParams(vmem_limit_bytes=62 * 2**20, **params),
        cost_estimate=pl.CostEstimate(
            flops=25 * 10**9, bytes_accessed=40 * 2**20, transcendentals=10**7
        ),
        name="layer",
    )(counts, tok, cot, pattern, gate, vectors, hidden, *weights)


def update_kernel(*refs):
    ins, outs, (low, grad, small, gi, go, gf, *held), sems = refs[:24], refs[24:44], refs[44:-1], refs[-1]

    def copy(j, src, dst):
        one = pltpu.make_async_copy(src, dst, sems.at[j])
        one.start()
        return one

    sums = [copy(2 + j, src, dst) for j, (src, dst) in enumerate(zip(ins[2:6], (small, gi, go, gf)))]
    gets = {}
    for j in (6, 7, 8, 0, 1, 2, 3, 4, 5) + tuple(range(9, 18)):
        gets[j] = copy(6 + j, ins[6 + j], held[j])
    passing = [copy(0, ins[0], low), copy(1, ins[1], grad)]
    puts = []
    for one in sums:
        one.wait()

    def step(n, here, value):
        p, m, v = (held[3 * n + j] for j in range(3))
        p[here], m[here], v[here] = adam_step(p[here], m[here], v[here], value, RATES[n])

    def ready(n):
        for j in range(3 * n, 3 * n + 3):
            gets[j].wait()

    def done(n):
        for j in range(3 * n, 3 * n + 3):
            puts.append(copy(6 + j, held[j], outs[2 + j]))

    every = slice(None)
    ready(2)
    for part in range(2):
        for c in range(HF // HD):
            here = (part, every, pl.ds(c * HD, HD))
            step(2, here, gf[here])
    done(2)
    for j in range(2):
        passing[j].wait()
        puts.append(copy(j, (low, grad)[j], outs[j]))
    ready(0)
    for kind in range(3):
        for part in range(HALF):
            value = [gi[part, :, pl.ds(g * PC + kind * 128, 128)] for g in range(PAIRS)]
            value = jnp.concatenate(value, axis=1).astype(F32)
            step(0, (every, pl.ds(kind * D + part * HD, HD)), value)
    done(0)
    ready(1)
    for part in range(HALF):
        step(1, (every, pl.ds(part * HD, HD)), go[part].astype(F32))
    done(1)
    for n in (3, 4, 5):
        ready(n)
    value = jnp.concatenate([small[pl.ds(0, H), :], small[pl.ds(H, H), :]], axis=1)
    value = value[:, : held[9].shape[1]] / (1.0 + jnp.exp(held[9][...]))
    step(3, (every, every), value)
    value = [small[pl.ds(R_VEC, 5), :], small[pl.ds(R_VEC + 5, 5), pl.ds(0, 256)]]
    step(4, (every, every), jnp.concatenate(value, axis=1))
    value = [
        small[pl.ds(R_HID + j, 1), pl.ds(q * 128, 128)]
        for j in range(HALF * NCH)
        for q in range(CH // 128)
    ]
    step(5, (every, every), jnp.concatenate(value, axis=0))
    for n in (3, 4, 5):
        done(n)
    for one in puts:
        one.wait()


def update_call(layer, weights):
    hbm = pl.BlockSpec(memory_space=pl.ANY)
    ins = list(layer) + list(weights)
    shapes = [jax.ShapeDtypeStruct(x.shape, x.dtype) for x in list(layer[:2]) + list(weights)]
    return pl.pallas_call(
        update_kernel,
        out_shape=shapes,
        in_specs=[hbm] * len(ins),
        out_specs=[hbm] * len(shapes),
        scratch_shapes=[pltpu.VMEM(x.shape, x.dtype) for x in ins]
        + [pltpu.SemaphoreType.DMA((len(ins),))],
        compiler_params=pltpu.CompilerParams(vmem_limit_bytes=62 * 2**20),
        cost_estimate=pl.CostEstimate(flops=10**7, bytes_accessed=12 * 10**6, transcendentals=10**6),
        name="update",
    )(*ins)


def collect(w, width):
    return w.reshape(D, HALF, width).transpose(1, 0, 2)


def local(
    tokens,
    cotangent,
    seq_counts,
    pattern,
    project_in,
    project_in_first,
    project_in_second,
    project_out,
    project_out_first,
    project_out_second,
    feed_forward,
    feed_forward_first,
    feed_forward_second,
    gate_logits,
    gate_logits_first,
    gate_logits_second,
    norm_vectors,
    norm_vectors_first,
    norm_vectors_second,
    hidden_bias,
    hidden_bias_first,
    hidden_bias_second,
):
    rows = project_in.shape[0]
    groups, halves = lax.axis_size("dp"), lax.axis_size("mp")
    comm = halves == HALF and groups == 16 and rows % 16 == 0
    shared = (
        seq_counts,
        tokens,
        cotangent,
        pattern,
        gate_logits,
        norm_vectors,
        hidden_bias.reshape(FF // 128, 128),
    )
    if comm:
        layer = layer_call(True, groups // 4, rows, *shared, project_in, project_out, feed_forward)
        weights = (
            project_in,
            project_in_first,
            project_in_second,
            project_out,
            project_out_first,
            project_out_second,
            feed_forward,
            feed_forward_first,
            feed_forward_second,
            gate_logits,
            gate_logits_first,
            gate_logits_second,
            norm_vectors,
            norm_vectors_first,
            norm_vectors_second,
        )
        flat = [w.reshape(-1, 128) for w in (hidden_bias, hidden_bias_first, hidden_bias_second)]
        outs = update_call(layer, weights + tuple(flat))
        return tuple(outs[:-3]) + tuple(w.reshape(FF) for w in outs[-3:])

    whole_in = lax.all_gather(project_in.astype(BF), "dp", axis=0, tiled=True)
    whole_out = lax.all_gather(project_out.astype(BF), "dp", axis=0, tiled=True)
    pair = lax.all_gather(feed_forward.astype(BF), "dp", axis=1, tiled=True)
    pair = lax.all_gather(pair, "mp", axis=2, tiled=True)
    wi = whole_in.reshape(D, 3, HALF, PAIRS, 128).transpose(2, 0, 3, 1, 4)
    wi = wi.reshape(HALF, D, 3 * HD)
    layer_out, input_grad, small, gi, go, g1, g2 = layer_call(
        False,
        1,
        D,
        *shared,
        wi,
        collect(whole_out, HD),
        collect(pair[0], HF),
        collect(pair[1], HF),
    )
    gi = gi.reshape(HALF, D, PAIRS, 3, 128).transpose(1, 3, 0, 2, 4).reshape(D, 3 * D)
    go = go.reshape(HALF, D, HD).transpose(1, 0, 2).reshape(D, D)
    gf = jnp.stack([g.reshape(HALF, D, HF).transpose(1, 0, 2).reshape(D, FF) for g in (g1, g2)])
    sum_in = lax.psum_scatter(gi, "dp", scatter_dimension=0, tiled=True)
    sum_in = lax.psum(sum_in.astype(F32), "mp")
    sum_out = lax.psum_scatter(go, "dp", scatter_dimension=0, tiled=True)
    sum_out = lax.psum(sum_out.astype(F32), "mp")
    sum_pair = lax.psum_scatter(gf, "dp", scatter_dimension=1, tiled=True)
    sum_pair = lax.psum_scatter(sum_pair, "mp", scatter_dimension=2, tiled=True).astype(F32)
    small = lax.psum(small, ("dp", "mp"))
    sum_gate = jnp.concatenate([small[:H], small[H : 2 * H]], axis=1)[:, : 2 * WIN - 1]
    sum_gate = sum_gate * jax.nn.sigmoid(-gate_logits)
    sum_vectors = jnp.concatenate(
        [small[R_VEC : R_VEC + 5], small[R_VEC + 5 : R_VEC + 10, :256]], axis=1
    )
    sum_bias = small[R_HID:].reshape(FF)
    outs = [layer_out, input_grad]
    for weight, first, second, grad, rate in (
        (project_in, project_in_first, project_in_second, sum_in, RATES[0]),
        (project_out, project_out_first, project_out_second, sum_out, RATES[1]),
        (feed_forward, feed_forward_first, feed_forward_second, sum_pair, RATES[2]),
        (gate_logits, gate_logits_first, gate_logits_second, sum_gate, RATES[3]),
        (norm_vectors, norm_vectors_first, norm_vectors_second, sum_vectors, RATES[4]),
        (hidden_bias, hidden_bias_first, hidden_bias_second, sum_bias, RATES[5]),
    ):
        outs.extend(adam_step(weight, first, second, grad, rate))
    return tuple(outs)


def solution(mesh):
    rows, whole = P(("dp", "mp"), None), P()
    split, pair = P("dp", None), P(None, "dp", "mp")
    return jax.shard_map(
        local,
        mesh=mesh,
        in_specs=(rows, rows, rows, whole) + (split,) * 6 + (pair,) * 3 + (whole,) * 9,
        out_specs=(rows, rows) + (split,) * 6 + (pair,) * 3 + (whole,) * 9,
        check_vma=False,
    )
```
